512 devices in a mesh: gx: 64 (over z, x_hi, core), gy: 8 (over x_lo, y).
Axes of the slice: x: 4 (x_hi: 2, x_lo: 2; x = x_hi * 2 + x_lo), y: 4, z: 16, core: 2. Of those that a mesh axis runs over, the one named last changes fastest.
Arguments:
- voxels: bfloat16 [64, 8, 8, 64, 128], P('gx', 'gy'), may hold values from -6 to 6
- first_weight: bfloat16 [27, 128, 128], replicated, may hold values from -0.21875 to 0.21875
- second_weight: bfloat16 [27, 128, 128], replicated, may hold values from -0.21875 to 0.21875
- in_slots: int32 [64, 8, 27, 2], P('gx', 'gy'), may hold values from 0 to 23
- out_slots: int32 [64, 8, 27, 2], P('gx', 'gy'), may hold values from 0 to 7
- live_slots: int32 [64, 8, 27, 2], P('gx', 'gy'), may hold values 0 or 1
- out_grad: bfloat16 [64, 8, 8, 64, 128], P('gx', 'gy'), may hold values from -6 to 6
Outputs:
- result: bfloat16 [64, 8, 8, 64, 128], P('gx', 'gy')
- input_grad: bfloat16 [64, 8, 8, 64, 128], P('gx', 'gy')
- first_grad: bfloat16 [27, 128, 128], replicated
- second_grad: bfloat16 [27, 128, 128], replicated
The draws below stay inside these ranges and needn't reach their ends.
Inputs may be any that keep to these rules, and one draw needn't show every extreme that they name: `in_slots`: A value below 8 names the tile's own block; 8 + g * 2 + r names block r of the g-th neighbouring tile (3 x 3 neighbourhood in row-major order, centre skipped). A tile's blocks 0 to 1 are its boundary blocks. `out_slots`: output blocks always belong to the pair's own tile. `live_slots`: A slot with 0 holds no pair and contributes nothing.
All inputs are finite; a program needn't handle non-finite values. No bound on the sum of `live_slots` on one device may be relied on, other than what follows from the above.
Results may differ from the reference program's by a relative error of at most 0.0058.
Values may be sent and summed in bfloat16 or wider, within the bound.
A program may use at most 64 MiB of HBM per device.

```python
import math
import jax
import jax.numpy as jnp
from jax import lax

C = 128
V = 64
KV = 27
BLK = 8
RIM = 2
CAP = 2
N_GX = 64
N_GY = 8


def plant(drawn, key, smallest, top_value):
    dims = drawn.shape
    spot = [jax.random.randint(jax.random.fold_in(key, axis), (), 0, dims[axis]) for axis in range(len(dims))]
    drawn = drawn.at[tuple(spot)].set(smallest)
    longest = dims.index(max(dims))
    spot[longest] = (spot[longest] + 1) % dims[longest]
    return drawn.at[tuple(spot)].set(top_value)


def level_of(stream_key, dims, shards, smallest, largest):
    loudness, own = 1.0, jax.random.fold_in(stream_key, 6)
    for position, blocks in shards:
        heights = jnp.exp(jax.random.uniform(jax.random.fold_in(own, position), (blocks,), jnp.float32, smallest / len(shards), largest / len(shards)))
        loudness = loudness * jnp.repeat(heights, dims[position] // blocks).reshape([-1 if axis == position else 1 for axis in range(len(dims))])
    return loudness


def centred(own_key, shape, spread, bound, split=(), held_as=jnp.bfloat16):
    drawn = spread * jax.random.normal(own_key, shape, jnp.float32)
    if split:
        drawn = drawn * level_of(own_key, shape, split, -0.22, 0.18)
    return jnp.clip(drawn, -bound, bound).astype(held_as)


def setup_inputs(seed: int = 0) -> dict:
    keys = jax.random.split(jax.random.key(seed), 8)
    return {
        "voxels": centred(keys[0], (N_GX, N_GY, BLK, V, C), 1.0, 6.0, ((0, 64), (1, 8))),
        "first_weight": centred(keys[1], (KV, C, C), (KV * CAP * C // BLK) ** -0.5, 0.21875),
        "second_weight": centred(keys[2], (KV, C, C), (KV * CAP * C // BLK) ** -0.5, 0.21875),
        "in_slots": plant(jax.random.randint(keys[3], (N_GX, N_GY, KV, CAP), 0, BLK + 8 * RIM), jax.random.fold_in(keys[3], 1), 0, (BLK + 8 * RIM) - 1).astype(jnp.int32),
        "out_slots": plant(jax.random.randint(keys[4], (N_GX, N_GY, KV, CAP), 0, BLK), jax.random.fold_in(keys[4], 1), 0, BLK - 1).astype(jnp.int32),
        "live_slots": plant((jax.random.randint(keys[5], (N_GX, N_GY, KV, CAP), 0, 3) < 2).astype(jnp.int32), jax.random.fold_in(keys[5], 1), 0, 1),
        "out_grad": centred(keys[6], (N_GX, N_GY, BLK, V, C), 1.0, 6.0, ((0, 64), (1, 8))),
    }


def smooth_slope(values):
    sigmoid = jax.nn.sigmoid(values)
    return sigmoid * (1.0 + values * (1.0 - sigmoid))

def build_table(field):
    edge = field[:, :, :RIM]
    padded = jnp.pad(edge, ((1, 1), (1, 1), (0, 0), (0, 0), (0, 0)))
    pieces = [field]
    for place in range(9):
        if place != 4:
            row_pos = place // 3
            col_pos = place % 3
            pieces.append(padded[row_pos:row_pos + N_GX, col_pos:col_pos + N_GY])
    return jnp.concatenate(pieces, axis=2)

def route_back(table_grad):
    local = table_grad[:, :, :BLK]
    remote = table_grad[:, :, BLK:].reshape(N_GX, N_GY, 8, RIM, V, C)
    padded = jnp.pad(remote, ((1, 1), (1, 1), (0, 0), (0, 0), (0, 0), (0, 0)))
    arrived = jnp.zeros((N_GX, N_GY, RIM, V, C), table_grad.dtype)
    for group in range(8):
        place = group + (1 if group >= 4 else 0)
        row_pos = place // 3
        col_pos = place % 3
        arrived = arrived + padded[2 - row_pos:2 - row_pos + N_GX, 2 - col_pos:2 - col_pos + N_GY, group]
    return local.at[:, :, :RIM].add(arrived)

def forward_conv(table, in_slots, out_slots, live_slots, weight):
    tiles = N_GX * N_GY
    weight_full = weight.astype(jnp.float32)
    targets = jnp.arange(BLK, dtype=jnp.int32)

    def one_tile(item):
        tile_table, in_rows, out_rows, live_rows = item
        picked = tile_table[in_rows.reshape(-1)].astype(jnp.float32).reshape(KV, CAP * V, C)
        product = jnp.einsum('kmc,kcd->kmd', picked, weight_full, precision=lax.Precision.HIGHEST)
        product = product.reshape(KV * CAP, V * C)
        placing = ((out_rows.reshape(1, -1) == targets[:, None]) & (live_rows.reshape(1, -1) > 0)).astype(jnp.float32)
        return jnp.dot(placing, product, precision=lax.Precision.HIGHEST).reshape(BLK, V, C)
    summed = lax.map(one_tile, (table.reshape((tiles,) + table.shape[2:]), in_slots.reshape(tiles, KV, CAP), out_slots.reshape(tiles, KV, CAP), live_slots.reshape(tiles, KV, CAP)))
    return summed.reshape(N_GX, N_GY, BLK, V, C)

def backward_conv(delta, table, in_slots, out_slots, live_slots, weight):
    tiles = N_GX * N_GY
    weight_full = weight.astype(jnp.float32)
    sources = jnp.arange(BLK + 8 * RIM, dtype=jnp.int32)

    def one_tile(total, item):
        tile_delta, tile_table, in_rows, out_rows, live_rows = item
        keep = live_rows.reshape(-1, 1, 1).astype(jnp.float32)
        gathered = (tile_delta[out_rows.reshape(-1)].astype(jnp.float32) * keep).reshape(KV, CAP * V, C)
        picked = tile_table[in_rows.reshape(-1)].astype(jnp.float32).reshape(KV, CAP * V, C)
        backward = jnp.einsum('kmd,kcd->kmc', gathered, weight_full, precision=lax.Precision.HIGHEST)
        backward = backward.reshape(KV * CAP, V * C)
        placing = (in_rows.reshape(1, -1) == sources[:, None]).astype(jnp.float32)
        tile_grad = jnp.dot(placing, backward, precision=lax.Precision.HIGHEST).reshape(BLK + 8 * RIM, V, C)
        total = total + jnp.einsum('kmc,kmd->kcd', picked, gathered, precision=lax.Precision.HIGHEST)
        return (total, tile_grad)
    total, grads = lax.scan(one_tile, jnp.zeros((KV, C, C), jnp.float32), (delta.reshape(tiles, BLK, V, C), table.reshape((tiles,) + table.shape[2:]), in_slots.reshape(tiles, KV, CAP), out_slots.reshape(tiles, KV, CAP), live_slots.reshape(tiles, KV, CAP)))
    return (grads.reshape(N_GX, N_GY, BLK + 8 * RIM, V, C), total)

def reference(voxels, first_weight, second_weight, in_slots, out_slots, live_slots, out_grad):
    table_x = build_table(voxels)
    first_sum = forward_conv(table_x, in_slots, out_slots, live_slots, first_weight)
    hidden = jax.nn.silu(first_sum).astype(jnp.bfloat16)
    table_h = build_table(hidden)
    second_sum = forward_conv(table_h, in_slots, out_slots, live_slots, second_weight)
    joined = second_sum + voxels.astype(jnp.float32)
    result = jax.nn.silu(joined).astype(jnp.bfloat16)
    second_delta = (out_grad.astype(jnp.float32) * smooth_slope(joined)).astype(jnp.bfloat16)
    grads_h, second_grad = backward_conv(second_delta, table_h, in_slots, out_slots, live_slots, second_weight)
    hidden_grad = route_back(grads_h)
    first_delta = (hidden_grad * smooth_slope(first_sum)).astype(jnp.bfloat16)
    grads_x, first_grad = backward_conv(first_delta, table_x, in_slots, out_slots, live_slots, first_weight)
    input_grad = (route_back(grads_x) + second_delta.astype(jnp.float32)).astype(jnp.bfloat16)
    scale = 1.0 / math.sqrt(N_GX * N_GY * KV * CAP * V)
    return (result, input_grad, (first_grad * scale).astype(jnp.bfloat16), (second_grad * scale).astype(jnp.bfloat16))
```

```python
import functools
import math

import jax
import jax.numpy as jnp
from jax import lax
from jax.experimental import pallas as pl
from jax.experimental.pallas import tpu as pltpu
from jax.sharding import PartitionSpec as P

RIM = 2
MESH = pl.DeviceIdType.MESH

ROWS = 27 * 128
HALF = 1792
FULL = 2 * HALF
A_ROWS = 1024
B_ROWS = 768
A1, A2 = A_ROWS // 4, A_ROWS // 16
B1, B2 = B_ROWS // 4, B_ROWS // 16
TILES = (A2 + B2) // 16
OWNER_BASE = (0, 8)


def rows(start, size):
    return pl.ds(pl.multiple_of(start, 16), size)


def place():
    gx, gy = lax.axis_index("gx"), lax.axis_index("gy")
    core = lax.rem(gx, 2)
    x = lax.rem(gx // 2, 2) * 2 + gy // 4
    return gx // 4, x, lax.rem(gy, 4), core


def device(z, x, y, core):
    return ((z * 2 + x // 2) * 2 + core, lax.rem(x, 2) * 4 + y)


def group_peers():
    z, x, y, core = place()
    peers = [device(z, x, y, 1 - core)]
    peers += [device(z, x, lax.rem(y + d, 4), core) for d in (1, 2, 3)]
    peers += [device(z, lax.rem(x + d, 4), y, core) for d in (1, 2, 3)]
    return peers


class Reduce:
    scratch = [
        pltpu.VMEM((HALF, 128), jnp.bfloat16),
        pltpu.VMEM((HALF, 128), jnp.bfloat16),
        pltpu.VMEM((3, A1, 128), jnp.bfloat16),
        pltpu.VMEM((3, B1, 128), jnp.bfloat16),
        pltpu.VMEM((A1 + B1, 128), jnp.bfloat16),
        pltpu.VMEM((3, A2, 128), jnp.bfloat16),
        pltpu.VMEM((3, B2, 128), jnp.bfloat16),
        pltpu.VMEM((A2 + B2, 128), jnp.bfloat16),
        pltpu.VMEM((16, 16, 128), jnp.bfloat16),
        pltpu.SemaphoreType.DMA((2, 28)),
        pltpu.SemaphoreType.DMA((2, 16)),
        pltpu.SemaphoreType.DMA((2, 16)),
    ]

    def __init__(self, index, part, out, scale, *scratch):
        self.base, self.part, self.out, self.scale = OWNER_BASE[index], part, out, scale
        (
            self.got_core,
            self.sum_core,
            self.got_a1,
            self.got_b1,
            self.sum_1,
            self.got_a2,
            self.got_b2,
            self.sum_2,
            self.got_z,
            self.sems,
            self.to_owner,
            self.from_owner,
        ) = scratch
        self.z, self.x, self.y, self.core = place()
        self.sent = []

    def send(self, src, dst, sem, device_id):
        copy = pltpu.make_async_remote_copy(
            src_ref=src,
            dst_ref=dst,
            send_sem=self.sems.at[0, sem],
            recv_sem=self.sems.at[1, sem],
            device_id=device_id,
            device_id_type=MESH,
        )
        copy.start()
        self.sent.append(copy)
        return copy

    def along(self, axis, d):
        if axis == "y":
            return device(self.z, self.x, lax.rem(self.y + d, 4), self.core)
        return device(self.z, lax.rem(self.x + d, 4), self.y, self.core)

    def at(self, axis, d):
        return lax.rem((self.y if axis == "y" else self.x) + d, 4)

    def start_core(self):
        other = 1 - self.core
        self.wait_core = self.send(
            self.part.at[rows(other * HALF, HALF)],
            self.got_core,
            0,
            device(self.z, self.x, self.y, other),
        )

    def scatter(self, src, offset, size, got, axis, sem):
        return [
            self.send(
                src.at[rows(offset + self.at(axis, d) * size, size)],
                got.at[d - 1],
                sem + d,
                self.along(axis, d),
            )
            for d in (1, 2, 3)
        ]

    def start_first(self):
        self.wait_core.wait_recv()
        own = self.part[rows(self.core * HALF, HALF)]
        self.sum_core[...] = (
            own.astype(jnp.float32) + self.got_core[...].astype(jnp.float32)
        ).astype(jnp.bfloat16)
        self.wait_a = self.scatter(self.sum_core, 0, A1, self.got_a1, "y", 0)
        self.wait_b = self.scatter(self.sum_core, A_ROWS, B1, self.got_b1, "x", 3)

    def gathered(self, own, got):
        total = own.astype(jnp.float32)
        for d in range(3):
            total = total + got[d].astype(jnp.float32)
        return total.astype(jnp.bfloat16)

    def start_second(self):
        for copy in self.wait_a:
            copy.wait_recv()
        self.sum_1[:A1] = self.gathered(self.sum_core[rows(self.y * A1, A1)], self.got_a1)
        wait_a = self.scatter(self.sum_1, 0, A2, self.got_a2, "x", 6)
        for copy in self.wait_b:
            copy.wait_recv()
        self.sum_1[A1:] = self.gathered(
            self.sum_core[rows(A_ROWS + self.x * B1, B1)], self.got_b1
        )
        self.wait_b = self.scatter(self.sum_1, A1, B2, self.got_b2, "y", 9)
        self.wait_a = wait_a

    def owner_copy(self, tile):
        owner = self.base + tile
        d = lax.rem(owner - self.z + 16, 16)
        return pltpu.make_async_remote_copy(
            src_ref=self.sum_2.at[rows(tile * 16, 16)],
            dst_ref=self.got_z.at[d],
            send_sem=self.to_owner.at[0, d],
            recv_sem=self.to_owner.at[1, d],
            device_id=device(owner, self.x, self.y, self.core),
            device_id_type=MESH,
        )

    def start_owner(self):
        for copy in self.wait_a:
            copy.wait_recv()
        self.sum_2[:A2] = self.gathered(self.sum_1[rows(self.x * A2, A2)], self.got_a2)
        for copy in self.wait_b:
            copy.wait_recv()
        self.sum_2[A2:] = self.gathered(self.sum_1[rows(A1 + self.y * B2, B2)], self.got_b2)

        @pl.loop(0, TILES)
        def _(tile):
            @pl.when(self.base + tile != self.z)
            def _():
                self.owner_copy(tile).start()

    def spot(self, tile):
        a = self.core * HALF + self.y * A1 + self.x * A2 + tile * 16
        b = self.core * HALF + A_ROWS + self.x * B1 + self.y * B2 + (tile - A2 // 16) * 16
        first = tile < A2 // 16
        return jnp.where(first, a, b)

    def result_copy(self, tile, d):
        piece = self.out.at[rows(self.spot(tile), 16)]
        return pltpu.make_async_remote_copy(
            src_ref=piece,
            dst_ref=piece,
            send_sem=self.from_owner.at[0, d],
            recv_sem=self.from_owner.at[1, tile],
            device_id=device(lax.rem(self.z + d, 16), self.x, self.y, self.core),
            device_id_type=MESH,
        )

    def owned(self):
        return (self.z >= self.base) & (self.z < self.base + TILES)

    def start_result(self):
        @pl.when(self.owned())
        def _():
            tile = self.z - self.base

            @pl.loop(1, 16)
            def _(d):
                pltpu.make_async_copy(
                    self.got_z.at[d], self.got_z.at[d], self.to_owner.at[1, d]
                ).wait()

            total = self.sum_2[rows(tile * 16, 16)].astype(jnp.float32)
            for d in range(1, 16):
                total = total + self.got_z[d].astype(jnp.float32)
            self.out[rows(self.spot(tile), 16)] = (total * self.scale).astype(jnp.bfloat16)

            @pl.loop(1, 16)
            def _(d):
                self.result_copy(tile, d).start()

    def gather(self, offset, size, axis, sem):
        piece = self.out.at[rows(offset + self.at(axis, 0) * size, size)]
        for d in (1, 2, 3):
            self.send(piece, piece, sem + d, self.along(axis, d))

    def wait_gather(self, offset, size, axis, sem):
        for d in (1, 2, 3):
            piece = self.out.at[rows(offset + self.at(axis, 4 - d) * size, size)]
            pltpu.make_async_copy(piece, piece, self.sems.at[1, sem + d]).wait()

    def start_gather_second(self):
        @pl.loop(0, TILES)
        def _(tile):
            @pl.when(self.base + tile != self.z)
            def _():
                piece = self.out.at[rows(self.spot(tile), 16)]
                pltpu.make_async_copy(piece, piece, self.from_owner.at[1, tile]).wait()

        half = self.core * HALF
        self.gather(half + self.y * A1, A2, "x", 12)
        self.gather(half + A_ROWS + self.x * B1, B2, "y", 15)

    def start_gather_first(self):
        half = self.core * HALF
        self.wait_gather(half + self.y * A1, A2, "x", 12)
        self.gather(half, A1, "y", 18)
        self.wait_gather(half + A_ROWS + self.x * B1, B2, "y", 15)
        self.gather(half + A_ROWS, B1, "x", 21)

    def start_gather_core(self):
        half = self.core * HALF
        self.wait_gather(half, A1, "y", 18)
        self.wait_gather(half + A_ROWS, B1, "x", 21)
        other = device(self.z, self.x, self.y, 1 - self.core)
        piece = self.out.at[rows(half, HALF)]
        self.send(piece, piece, 25, other)

    def finish(self):
        piece = self.out.at[rows((1 - self.core) * HALF, HALF)]
        pltpu.make_async_copy(piece, piece, self.sems.at[1, 25]).wait()
        for copy in self.sent:
            copy.wait_send()

        @pl.loop(0, TILES)
        def _(tile):
            @pl.when(self.base + tile != self.z)
            def _():
                self.owner_copy(tile).wait_send()

        @pl.when(self.owned())
        def _():
            @pl.loop(1, 16)
            def _(d):
                self.result_copy(self.z - self.base, d).wait_send()


def enter(peers):
    barrier = pltpu.get_barrier_semaphore()
    for peer in peers:
        pl.semaphore_signal(barrier, inc=1, device_id=peer, device_id_type=MESH)
    z, x, y, core = place()

    @pl.loop(1, 16)
    def _(d):
        pl.semaphore_signal(
            barrier,
            inc=1,
            device_id=device(lax.rem(z + d, 16), x, y, core),
            device_id_type=MESH,
        )

    pl.semaphore_wait(barrier, len(peers) + 15)


def reduce_kernel(scale, first_part, second_part, first_out, second_out, *scratch):
    enter(group_peers())
    count = len(Reduce.scratch)
    both = [
        Reduce(0, first_part, first_out, scale, *scratch[:count]),
        Reduce(1, second_part, second_out, scale, *scratch[count:]),
    ]
    for step in (
        "start_core",
        "start_first",
        "start_second",
        "start_owner",
        "start_result",
        "start_gather_second",
        "start_gather_first",
        "start_gather_core",
        "finish",
    ):
        for one in both:
            getattr(one, step)()


def reduce_all(first_grad, second_grad, scale):
    def prepared(grad):
        flat = grad.reshape(ROWS, 128).astype(jnp.bfloat16)
        return jnp.pad(flat, ((0, FULL - ROWS), (0, 0)))

    shape = jax.ShapeDtypeStruct((FULL, 128), jnp.bfloat16)
    first, second = pl.pallas_call(
        functools.partial(reduce_kernel, scale),
        out_shape=(shape, shape),
        in_specs=[pl.BlockSpec(memory_space=pltpu.VMEM)] * 2,
        out_specs=[pl.BlockSpec(memory_space=pltpu.VMEM)] * 2,
        scratch_shapes=Reduce.scratch * 2,
        compiler_params=pltpu.CompilerParams(
            collective_id=0, has_side_effects=True, vmem_limit_bytes=32 * 1024 * 1024
        ),
        cost_estimate=pl.CostEstimate(
            flops=FULL * 128 * 4, bytes_accessed=8 * FULL * 128, transcendentals=0
        ),
    )(prepared(first_grad), prepared(second_grad))
    return first[:ROWS].reshape(27, 128, 128), second[:ROWS].reshape(27, 128, 128)


def padded(block, sides, width):
    for axis, dim in sides:
        count = lax.axis_size(axis)
        forward = [(i, i + 1) for i in range(count - 1)]
        backward = [(target, source) for source, target in forward]
        low = lax.ppermute(
            lax.slice_in_dim(block, block.shape[dim] - width, None, axis=dim), axis, forward
        )
        high = lax.ppermute(lax.slice_in_dim(block, 0, width, axis=dim), axis, backward)
        block = jnp.concatenate([low, block, high], axis=dim)
    return block


def smooth_slope(values):
    sigmoid = jax.nn.sigmoid(values)
    return sigmoid * (1.0 + values * (1.0 - sigmoid))


def share_rim(local):
    depth = RIM
    edge = local[:depth][None, None]
    beside_all = padded(edge, (("gx", 0), ("gy", 1)), 1)
    beside_all = beside_all.reshape((9, depth) + local.shape[1:])
    lower = beside_all[:4].reshape((-1,) + local.shape[1:])
    upper = beside_all[5:].reshape((-1,) + local.shape[1:])
    return jnp.concatenate([local, lower, upper], axis=0)


def return_rim(table_grad, blocks):
    depth = RIM
    shape_tail = table_grad.shape[1:]
    remote = table_grad[blocks:].reshape((8, depth) + shape_tail)
    middle = jnp.zeros((1, depth) + shape_tail, jnp.float32)
    layout = jnp.concatenate([remote[:4], middle, remote[4:]], axis=0).reshape(
        (3, 3, depth) + shape_tail
    )
    along = padded(layout, (("gx", 0),), 1)
    column = along[0] + along[2] + along[4]
    across = padded(column, (("gy", 0),), 1)
    arrived = across[0] + across[2] + across[4]
    return table_grad[:blocks].at[:depth].add(arrived)


def convolve(table, in_rows, out_rows, live_rows, weight, blocks):
    offsets, slot_count = in_rows.shape
    voxel_count, width = (table.shape[1], table.shape[2])
    picked = jnp.take(table, in_rows.reshape(-1), axis=0).reshape(
        offsets, slot_count * voxel_count, width
    )
    product = jnp.einsum("kmc,kcd->kmd", picked, weight, preferred_element_type=jnp.float32)
    product = product.reshape(offsets * slot_count, voxel_count * width)
    targets = lax.broadcasted_iota(jnp.int32, (blocks, offsets * slot_count), 0)
    placing = ((out_rows.reshape(1, -1) == targets) & (live_rows.reshape(1, -1) > 0)).astype(
        jnp.float32
    )
    summed = jnp.dot(
        placing, product, precision=lax.Precision.HIGHEST, preferred_element_type=jnp.float32
    )
    return (summed.reshape(blocks, voxel_count, width), picked)


def transpose_conv(delta, picked, in_rows, out_rows, live_rows, weight, table_rows):
    offsets, slot_count = in_rows.shape
    voxel_count, width = (delta.shape[1], delta.shape[2])
    keep = live_rows.reshape(-1, 1, 1).astype(delta.dtype)
    gathered = (jnp.take(delta, out_rows.reshape(-1), axis=0) * keep).reshape(
        offsets, slot_count * voxel_count, width
    )
    backward = jnp.einsum("kmd,kcd->kmc", gathered, weight, preferred_element_type=jnp.float32)
    backward = backward.reshape(offsets * slot_count, voxel_count * width)
    sources = lax.broadcasted_iota(jnp.int32, (table_rows, offsets * slot_count), 0)
    placing = (in_rows.reshape(1, -1) == sources).astype(jnp.float32)
    table_grad = jnp.dot(
        placing, backward, precision=lax.Precision.HIGHEST, preferred_element_type=jnp.float32
    )
    weight_grad = jnp.einsum("kmc,kmd->kcd", picked, gathered, preferred_element_type=jnp.float32)
    return (table_grad.reshape(table_rows, voxel_count, width), weight_grad)


def shards(voxels, first_weight, second_weight, in_slots, out_slots, live_slots, out_grad):
    blocks = voxels.shape[2]
    shape_tail = voxels.shape[3:]
    inputs = voxels.reshape((blocks,) + shape_tail)
    cotangent = out_grad.reshape((blocks,) + shape_tail)
    in_rows = in_slots.reshape(in_slots.shape[2:])
    out_rows = out_slots.reshape(out_slots.shape[2:])
    live_rows = live_slots.reshape(live_slots.shape[2:])
    table_x = share_rim(inputs)
    table_rows = table_x.shape[0]
    first_sum, picked_x = convolve(table_x, in_rows, out_rows, live_rows, first_weight, blocks)
    hidden = jax.nn.silu(first_sum).astype(jnp.bfloat16)
    table_h = share_rim(hidden)
    second_sum, picked_h = convolve(table_h, in_rows, out_rows, live_rows, second_weight, blocks)
    joined = second_sum + inputs.astype(jnp.float32)
    result = jax.nn.silu(joined).astype(jnp.bfloat16)
    second_delta = (cotangent.astype(jnp.float32) * smooth_slope(joined)).astype(jnp.bfloat16)
    grads_h, second_grad = transpose_conv(
        second_delta, picked_h, in_rows, out_rows, live_rows, second_weight, table_rows
    )
    hidden_grad = return_rim(grads_h, blocks)
    first_delta = (hidden_grad * smooth_slope(first_sum)).astype(jnp.bfloat16)
    grads_x, first_grad = transpose_conv(
        first_delta, picked_x, in_rows, out_rows, live_rows, first_weight, table_rows
    )
    input_grad = return_rim(grads_x, blocks) + second_delta.astype(jnp.float32)
    scale = 1.0 / math.sqrt(
        lax.axis_size("gx")
        * lax.axis_size("gy")
        * in_rows.shape[0]
        * in_rows.shape[1]
        * shape_tail[0]
    )
    first_grad, second_grad = reduce_all(first_grad, second_grad, scale)
    return (
        result.reshape(voxels.shape),
        input_grad.astype(jnp.bfloat16).reshape(voxels.shape),
        first_grad,
        second_grad,
    )


def solution(mesh):
    return jax.shard_map(
        shards,
        mesh=mesh,
        in_specs=(
            P("gx", "gy", None, None, None),
            P(),
            P(),
            P("gx", "gy", None, None),
            P("gx", "gy", None, None),
            P("gx", "gy", None, None),
            P("gx", "gy", None, None, None),
        ),
        out_specs=(P("gx", "gy", None, None, None), P("gx", "gy", None, None, None), P(), P()),
        check_vma=False,
    )
```

```python
import functools
import math

import jax
import jax.numpy as jnp
from jax import lax
from jax.experimental import pallas as pl
from jax.experimental.pallas import tpu as pltpu
from jax.sharding import PartitionSpec as P

RIM = 2
MESH = pl.DeviceIdType.MESH

ROWS = 27 * 128
HALF = 1792
FULL = 2 * HALF
A_ROWS = 1024
B_ROWS = 768
A1, A2 = A_ROWS // 4, A_ROWS // 16
B1, B2 = B_ROWS // 4, B_ROWS // 16
TILES = (A2 + B2) // 16
OWNER_BASE = (0, 8)


def rows(start, size):
    return pl.ds(pl.multiple_of(start, 16), size)


def place():
    gx, gy = lax.axis_index("gx"), lax.axis_index("gy")
    core = lax.rem(gx, 2)
    x = lax.rem(gx // 2, 2) * 2 + gy // 4
    return gx // 4, x, lax.rem(gy, 4), core


def device(z, x, y, core):
    return ((z * 2 + x // 2) * 2 + core, lax.rem(x, 2) * 4 + y)


def group_peers():
    z, x, y, core = place()
    peers = [device(z, x, y, 1 - core)]
    peers += [device(z, x, lax.rem(y + d, 4), core) for d in (1, 2, 3)]
    peers += [device(z, lax.rem(x + d, 4), y, core) for d in (1, 2, 3)]
    return peers


class Reduce:
    scratch = [
        pltpu.VMEM((HALF, 128), jnp.bfloat16),
        pltpu.VMEM((HALF, 128), jnp.bfloat16),
        pltpu.VMEM((3, A1, 128), jnp.bfloat16),
        pltpu.VMEM((3, B1, 128), jnp.bfloat16),
        pltpu.VMEM((A1 + B1, 128), jnp.bfloat16),
        pltpu.VMEM((3, A2, 128), jnp.bfloat16),
        pltpu.VMEM((3, B2, 128), jnp.bfloat16),
        pltpu.VMEM((A2 + B2, 128), jnp.bfloat16),
        pltpu.VMEM((16, 16, 128), jnp.bfloat16),
        pltpu.SemaphoreType.DMA((2, 28)),
        pltpu.SemaphoreType.DMA((2, 16)),
        pltpu.SemaphoreType.DMA((2, 16)),
    ]

    def __init__(self, index, part, out, scale, *scratch):
        self.base, self.part, self.out, self.scale = OWNER_BASE[index], part, out, scale
        (
            self.got_core,
            self.sum_core,
            self.got_a1,
            self.got_b1,
            self.sum_1,
            self.got_a2,
            self.got_b2,
            self.sum_2,
            self.got_z,
            self.sems,
            self.to_owner,
            self.from_owner,
        ) = scratch
        self.z, self.x, self.y, self.core = place()
        self.sent = []

    def send(self, src, dst, sem, device_id):
        copy = pltpu.make_async_remote_copy(
            src_ref=src,
            dst_ref=dst,
            send_sem=self.sems.at[0, sem],
            recv_sem=self.sems.at[1, sem],
            device_id=device_id,
            device_id_type=MESH,
        )
        copy.start()
        self.sent.append(copy)
        return copy

    def along(self, axis, d):
        if axis == "y":
            return device(self.z, self.x, lax.rem(self.y + d, 4), self.core)
        return device(self.z, lax.rem(self.x + d, 4), self.y, self.core)

    def at(self, axis, d):
        return lax.rem((self.y if axis == "y" else self.x) + d, 4)

    def start_core(self):
        other = 1 - self.core
        self.wait_core = self.send(
            self.part.at[rows(other * HALF, HALF)],
            self.got_core,
            0,
            device(self.z, self.x, self.y, other),
        )

    def scatter(self, src, offset, size, got, axis, sem):
        return [
            self.send(
                src.at[rows(offset + self.at(axis, d) * size, size)],
                got.at[d - 1],
                sem + d,
                self.along(axis, d),
            )
            for d in (1, 2, 3)
        ]

    def start_first(self):
        self.wait_core.wait_recv()
        own = self.part[rows(self.core * HALF, HALF)]
        self.sum_core[...] = (
            own.astype(jnp.float32) + self.got_core[...].astype(jnp.float32)
        ).astype(jnp.bfloat16)
        self.wait_a = self.scatter(self.sum_core, 0, A1, self.got_a1, "y", 0)
        self.wait_b = self.scatter(self.sum_core, A_ROWS, B1, self.got_b1, "x", 3)

    def gathered(self, own, got):
        total = own.astype(jnp.float32)
        for d in range(3):
            total = total + got[d].astype(jnp.float32)
        return total.astype(jnp.bfloat16)

    def start_second(self):
        for copy in self.wait_a:
            copy.wait_recv()
        self.sum_1[:A1] = self.gathered(self.sum_core[rows(self.y * A1, A1)], self.got_a1)
        wait_a = self.scatter(self.sum_1, 0, A2, self.got_a2, "x", 6)
        for copy in self.wait_b:
            copy.wait_recv()
        self.sum_1[A1:] = self.gathered(
            self.sum_core[rows(A_ROWS + self.x * B1, B1)], self.got_b1
        )
        self.wait_b = self.scatter(self.sum_1, A1, B2, self.got_b2, "y", 9)
        self.wait_a = wait_a

    def owner_copy(self, tile):
        owner = self.base + tile
        d = lax.rem(owner - self.z + 16, 16)
        return pltpu.make_async_remote_copy(
            src_ref=self.sum_2.at[rows(tile * 16, 16)],
            dst_ref=self.got_z.at[d],
            send_sem=self.to_owner.at[0, d],
            recv_sem=self.to_owner.at[1, d],
            device_id=device(owner, self.x, self.y, self.core),
            device_id_type=MESH,
        )

    def start_owner(self):
        for copy in self.wait_a:
            copy.wait_recv()
        self.sum_2[:A2] = self.gathered(self.sum_1[rows(self.x * A2, A2)], self.got_a2)
        for copy in self.wait_b:
            copy.wait_recv()
        self.sum_2[A2:] = self.gathered(self.sum_1[rows(A1 + self.y * B2, B2)], self.got_b2)

        @pl.loop(0, TILES)
        def _(tile):
            @pl.when(self.base + tile != self.z)
            def _():
                self.owner_copy(tile).start()

    def spot(self, tile):
        a = self.core * HALF + self.y * A1 + self.x * A2 + tile * 16
        b = self.core * HALF + A_ROWS + self.x * B1 + self.y * B2 + (tile - A2 // 16) * 16
        first = tile < A2 // 16
        return jnp.where(first, a, b)

    def result_copy(self, tile, d):
        piece = self.out.at[rows(self.spot(tile), 16)]
        return pltpu.make_async_remote_copy(
            src_ref=piece,
            dst_ref=piece,
            send_sem=self.from_owner.at[0, d],
            recv_sem=self.from_owner.at[1, tile],
            device_id=device(lax.rem(self.z + d, 16), self.x, self.y, self.core),
            device_id_type=MESH,
        )

    def owned(self):
        return (self.z >= self.base) & (self.z < self.base + TILES)

    def start_result(self):
        @pl.when(self.owned())
        def _():
            tile = self.z - self.base

            @pl.loop(1, 16)
            def _(d):
                pltpu.make_async_copy(
                    self.got_z.at[d], self.got_z.at[d], self.to_owner.at[1, d]
                ).wait()

            total = self.sum_2[rows(tile * 16, 16)].astype(jnp.float32)
            for d in range(1, 16):
                total = total + self.got_z[d].astype(jnp.float32)
            self.out[rows(self.spot(tile), 16)] = (total * self.scale).astype(jnp.bfloat16)

            @pl.loop(1, 16)
            def _(d):
                self.result_copy(tile, d).start()

    def gather(self, offset, size, axis, sem):
        piece = self.out.at[rows(offset + self.at(axis, 0) * size, size)]
        for d in (1, 2, 3):
            self.send(piece, piece, sem + d, self.along(axis, d))

    def wait_gather(self, offset, size, axis, sem):
        for d in (1, 2, 3):
            piece = self.out.at[rows(offset + self.at(axis, 4 - d) * size, size)]
            pltpu.make_async_copy(piece, piece, self.sems.at[1, sem + d]).wait()

    def start_gather_second(self):
        @pl.loop(0, TILES)
        def _(tile):
            @pl.when(self.base + tile != self.z)
            def _():
                piece = self.out.at[rows(self.spot(tile), 16)]
                pltpu.make_async_copy(piece, piece, self.from_owner.at[1, tile]).wait()

        half = self.core * HALF
        self.gather(half + self.y * A1, A2, "x", 12)
        self.gather(half + A_ROWS + self.x * B1, B2, "y", 15)

    def start_gather_first(self):
        half = self.core * HALF
        self.wait_gather(half + self.y * A1, A2, "x", 12)
        self.gather(half, A1, "y", 18)
        self.wait_gather(half + A_ROWS + self.x * B1, B2, "y", 15)
        self.gather(half + A_ROWS, B1, "x", 21)

    def start_gather_core(self):
        half = self.core * HALF
        self.wait_gather(half, A1, "y", 18)
        self.wait_gather(half + A_ROWS, B1, "x", 21)
        other = device(self.z, self.x, self.y, 1 - self.core)
        piece = self.out.at[rows(half, HALF)]
        self.send(piece, piece, 25, other)

    def finish(self):
        piece = self.out.at[rows((1 - self.core) * HALF, HALF)]
        pltpu.make_async_copy(piece, piece, self.sems.at[1, 25]).wait()
        for copy in self.sent:
            copy.wait_send()

        @pl.loop(0, TILES)
        def _(tile):
            @pl.when(self.base + tile != self.z)
            def _():
                self.owner_copy(tile).wait_send()

        @pl.when(self.owned())
        def _():
            @pl.loop(1, 16)
            def _(d):
                self.result_copy(self.z - self.base, d).wait_send()


def enter(peers):
    barrier = pltpu.get_barrier_semaphore()
    for peer in peers:
        pl.semaphore_signal(barrier, inc=1, device_id=peer, device_id_type=MESH)
    z, x, y, core = place()

    @pl.loop(1, 16)
    def _(d):
        pl.semaphore_signal(
            barrier,
            inc=1,
            device_id=device(lax.rem(z + d, 16), x, y, core),
            device_id_type=MESH,
        )

    pl.semaphore_wait(barrier, len(peers) + 15)


BLOCKS, VOXELS, OFFSETS, SLOTS, TABLE = 8, 64, 27, 54, 24
DIRECTIONS = [(a, b) for a in (-1, 0, 1) for b in (-1, 0, 1) if (a, b) != (0, 0)]


def neighbour(direction):
    a, b = direction
    gx, gy = lax.axis_index("gx"), lax.axis_index("gy")
    return lax.rem(gx + a + 64, 64), lax.rem(gy + b + 8, 8)


def present(direction):
    a, b = direction
    gx, gy = lax.axis_index("gx") + a, lax.axis_index("gy") + b
    return (gx >= 0) & (gx < 64) & (gy >= 0) & (gy < 8)


def sigmoid(values):
    return 1.0 / (1.0 + jnp.exp(-values))


def slope(values):
    s = sigmoid(values)
    return s * (1.0 + values * (1.0 - s))


def write_plan(in_ref, out_ref, live_ref, plan):
    shape = (OFFSETS, 128)
    lane = lax.broadcasted_iota(jnp.int32, shape, 1)
    even = 2 * lax.broadcasted_iota(jnp.int32, shape, 0)

    def columns(values):
        return [jnp.broadcast_to(values[:, s : s + 1], shape) for s in (0, 1)]

    def along(pair):
        picked = jnp.where(lane == even, pair[0], 0) + jnp.where(lane == even + 1, pair[1], 0)
        return jnp.sum(picked, axis=0, keepdims=True)

    def chain(pair):
        target = jnp.broadcast_to(along(pair), shape)
        found = jnp.zeros(shape, jnp.int32)
        last = jnp.zeros(shape, jnp.int32)
        for s in (0, 1):
            same = (pair[s] == target) & (even + s < lane) & (pair[s] >= 0)
            found = jnp.maximum(found, jnp.where(same, even + s + 1, 0))
            last = jnp.maximum(last, jnp.where(pair[s] == lane, even + s + 1, 0))
        return jnp.max(found, axis=0, keepdims=True), jnp.max(last, axis=0, keepdims=True)

    source, target, live = in_ref[...], out_ref[...], live_ref[...]
    plan[0:1] = along(columns(source))
    plan[1:2] = along(columns(jnp.where(live > 0, target, BLOCKS)))
    plan[2:3], plan[3:4] = chain(columns(jnp.where(live > 0, target, -1)))
    plan[4:5], plan[5:6] = chain(columns(jnp.where(live > 0, source, -1)))
    plan[6:8] = jnp.zeros((2, 128), jnp.int32)


def step_loop(body):
    @pl.loop(0, OFFSETS // 3)
    def _(step):
        for u in range(3):
            body(step * 3 + u)


def pair_of(table, plan, row, k):
    return jnp.concatenate([table[plan[row, 2 * k]], table[plan[row, 2 * k + 1]]], axis=0)


def convolve(table, plan, row, chain, weight, sums, flipped):
    def body(k):
        product = lax.dot_general(
            pair_of(table, plan, row, k),
            weight[k],
            (((1,), (1 if flipped else 0,)), ((), ())),
            preferred_element_type=jnp.float32,
        )
        sums[2 * k + 1] = sums[plan[chain, 2 * k]] + product[:VOXELS]
        sums[2 * k + 2] = sums[plan[chain, 2 * k + 1]] + product[VOXELS:]

    step_loop(body)


def weight_terms(table, delta, plan, part):
    def body(k):
        product = lax.dot_general(
            pair_of(table, plan, 0, k),
            pair_of(delta, plan, 1, k),
            (((0,), (0,)), ((), ())),
            preferred_element_type=jnp.float32,
        )
        part[rows(k * 128, 128)] = product.astype(jnp.bfloat16)

    step_loop(body)


class Swap:
    def __init__(self, index, send_sems, recv_sems, sources, targets):
        self.copies = []
        for g, direction in enumerate(DIRECTIONS):
            copy = pltpu.make_async_remote_copy(
                src_ref=sources[g],
                dst_ref=targets[7 - g],
                send_sem=send_sems.at[index, g],
                recv_sem=recv_sems.at[index, 7 - g],
                device_id=neighbour(direction),
                device_id_type=MESH,
            )
            copy.start()
            self.copies.append(copy)

    def arrive(self):
        for copy in self.copies:
            copy.wait_recv()

    def finish(self):
        for copy in self.copies:
            copy.wait_send()


def rim_slots(table):
    return [table.at[pl.ds(BLOCKS + RIM * g, RIM)] for g in range(8)]


def clear_outside(table):
    for g, direction in enumerate(DIRECTIONS):

        @pl.when(jnp.logical_not(present(direction)))
        def _():
            table[BLOCKS + RIM * g : BLOCKS + RIM * (g + 1)] = jnp.zeros(
                (RIM, VOXELS, 128), jnp.bfloat16
            )


def routed(own, arrived, r):
    total = own
    for g, direction in enumerate(DIRECTIONS):
        total = total + jnp.where(present(direction), arrived[g, r].astype(jnp.float32), 0.0)
    return total


BLOCK_SET = (VOXELS, 128)
SCRATCH = [
    pltpu.VMEM((8, 128), jnp.int32),
    pltpu.SMEM((8, 128), jnp.int32),
    pltpu.VMEM((TABLE,) + BLOCK_SET, jnp.bfloat16),
    pltpu.VMEM((TABLE,) + BLOCK_SET, jnp.bfloat16),
    pltpu.VMEM((SLOTS + 2,) + BLOCK_SET, jnp.float32),
    pltpu.VMEM((BLOCKS,) + BLOCK_SET, jnp.float32),
    pltpu.VMEM((BLOCKS + 1,) + BLOCK_SET, jnp.bfloat16),
    pltpu.VMEM((BLOCKS + 1,) + BLOCK_SET, jnp.bfloat16),
    pltpu.VMEM((8, RIM) + BLOCK_SET, jnp.bfloat16),
    pltpu.VMEM((8, RIM) + BLOCK_SET, jnp.bfloat16),
    pltpu.VMEM((8, RIM) + BLOCK_SET, jnp.bfloat16),
    pltpu.VMEM((8, RIM) + BLOCK_SET, jnp.bfloat16),
    pltpu.VMEM((FULL, 128), jnp.bfloat16),
    pltpu.VMEM((FULL, 128), jnp.bfloat16),
    pltpu.SemaphoreType.DMA,
    pltpu.SemaphoreType.DMA((4, 8)),
    pltpu.SemaphoreType.DMA((4, 8)),
]


def block_kernel(
    scale,
    voxels,
    first_weight,
    second_weight,
    in_slots,
    out_slots,
    live_slots,
    out_grad,
    result,
    input_grad,
    first_grad,
    second_grad,
    *scratch,
):
    (
        plan_rows,
        plan,
        table_x,
        table_h,
        sums,
        first_sum,
        first_delta,
        second_delta,
        give_h,
        got_h,
        give_x,
        got_x,
        first_part,
        second_part,
        plan_sem,
        send_sems,
        recv_sems,
    ) = scratch[: len(SCRATCH)]
    count = len(Reduce.scratch)
    reduces = scratch[len(SCRATCH) :]
    first = Reduce(0, first_part, first_grad, scale, *reduces[:count])
    second = Reduce(1, second_part, second_grad, scale, *reduces[count:])

    enter([neighbour(direction) for direction in DIRECTIONS] + group_peers())
    rim_x = voxels.at[pl.ds(0, RIM)]
    swap_x = Swap(0, send_sems, recv_sems, [rim_x] * 8, rim_slots(table_x))

    write_plan(in_slots, out_slots, live_slots, plan_rows)
    copy = pltpu.make_async_copy(plan_rows, plan, plan_sem)
    copy.start()
    table_x[:BLOCKS] = voxels[...]
    zeros = jnp.zeros(BLOCK_SET, jnp.bfloat16)
    first_delta[BLOCKS] = zeros
    second_delta[BLOCKS] = zeros
    sums[0] = jnp.zeros(BLOCK_SET, jnp.float32)
    for part in (first_part, second_part):
        part[ROWS:] = jnp.zeros((FULL - ROWS, 128), jnp.bfloat16)
    copy.wait()

    swap_x.arrive()
    clear_outside(table_x)
    convolve(table_x, plan, 0, 2, first_weight, sums, False)

    def hide(block):
        total = sums[plan[3, block]]
        first_sum[block] = total
        table_h[block] = (total * sigmoid(total)).astype(jnp.bfloat16)

    for block in range(RIM):
        hide(block)
    rim_h = table_h.at[pl.ds(0, RIM)]
    swap_h = Swap(1, send_sems, recv_sems, [rim_h] * 8, rim_slots(table_h))
    pl.loop(RIM, BLOCKS)(hide)

    swap_h.arrive()
    clear_outside(table_h)
    convolve(table_h, plan, 0, 2, second_weight, sums, False)

    @pl.loop(0, BLOCKS)
    def _(block):
        joined = sums[plan[3, block]] + voxels[block].astype(jnp.float32)
        result[block] = (joined * sigmoid(joined)).astype(jnp.bfloat16)
        second_delta[block] = (out_grad[block].astype(jnp.float32) * slope(joined)).astype(
            jnp.bfloat16
        )

    def give(buffer):
        @pl.loop(0, 8)
        def _(g):
            for r in range(RIM):
                buffer[g, r] = sums[plan[5, BLOCKS + RIM * g + r]].astype(jnp.bfloat16)

    def eight(buffer):
        return [buffer.at[g] for g in range(8)]

    convolve(second_delta, plan, 1, 4, second_weight, sums, True)
    give(give_h)
    back_h = Swap(2, send_sems, recv_sems, eight(give_h), eight(got_h))

    def descend(block, total):
        first_delta[block] = (total * slope(first_sum[block])).astype(jnp.bfloat16)

    @pl.loop(RIM, BLOCKS)
    def _(block):
        descend(block, sums[plan[5, block]])

    weight_terms(table_h, second_delta, plan, second_part)
    second.start_core()

    back_h.arrive()
    for r in range(RIM):
        descend(r, routed(sums[plan[5, r]], got_h, r))

    weight_terms(table_x, first_delta, plan, first_part)
    first.start_core()
    second.start_first()

    convolve(first_delta, plan, 1, 4, first_weight, sums, True)
    give(give_x)
    back_x = Swap(3, send_sems, recv_sems, eight(give_x), eight(got_x))
    first.start_first()
    second.start_second()

    def land(block, total):
        input_grad[block] = (total + second_delta[block].astype(jnp.float32)).astype(jnp.bfloat16)

    @pl.loop(RIM, BLOCKS)
    def _(block):
        land(block, sums[plan[5, block]])

    first.start_second()
    second.start_owner()
    back_x.arrive()
    for r in range(RIM):
        land(r, routed(sums[plan[5, r]], got_x, r))

    first.start_owner()
    second.start_result()
    first.start_result()
    second.start_gather_second()
    first.start_gather_second()
    second.start_gather_first()
    first.start_gather_first()
    second.start_gather_core()
    first.start_gather_core()
    for swap in (swap_x, swap_h, back_h, back_x):
        swap.finish()
    second.finish()
    first.finish()


def shards(voxels, first_weight, second_weight, in_slots, out_slots, live_slots, out_grad):
    tile = (BLOCKS,) + BLOCK_SET
    scale = 1.0 / math.sqrt(
        lax.axis_size("gx") * lax.axis_size("gy") * OFFSETS * in_slots.shape[3] * VOXELS
    )
    field = jax.ShapeDtypeStruct(tile, jnp.bfloat16)
    grad = jax.ShapeDtypeStruct((FULL, 128), jnp.bfloat16)
    result, input_grad, first_grad, second_grad = pl.pallas_call(
        functools.partial(block_kernel, scale),
        out_shape=(field, field, grad, grad),
        in_specs=[pl.BlockSpec(memory_space=pltpu.VMEM)] * 7,
        out_specs=[pl.BlockSpec(memory_space=pltpu.VMEM)] * 4,
        scratch_shapes=SCRATCH + Reduce.scratch * 2,
        compiler_params=pltpu.CompilerParams(
            collective_id=0, has_side_effects=True, vmem_limit_bytes=40 * 1024 * 1024
        ),
        cost_estimate=pl.CostEstimate(
            flops=6 * SLOTS * VOXELS * 128 * 128 * 2,
            bytes_accessed=4 * FULL * 256,
            transcendentals=4 * BLOCKS * VOXELS * 128,
        ),
    )(
        voxels.reshape(tile),
        first_weight,
        second_weight,
        in_slots.reshape(in_slots.shape[2:]),
        out_slots.reshape(in_slots.shape[2:]),
        live_slots.reshape(in_slots.shape[2:]),
        out_grad.reshape(tile),
    )

    def unpadded(whole):
        return whole[:ROWS].reshape(first_weight.shape)

    return (
        result.reshape(voxels.shape),
        input_grad.reshape(voxels.shape),
        unpadded(first_grad),
        unpadded(second_grad),
    )


def solution(mesh):
    return jax.shard_map(
        shards,
        mesh=mesh,
        in_specs=(
            P("gx", "gy", None, None, None),
            P(),
            P(),
            P("gx", "gy", None, None),
            P("gx", "gy", None, None),
            P("gx", "gy", None, None),
            P("gx", "gy", None, None, None),
        ),
        out_specs=(P("gx", "gy", None, None, None), P("gx", "gy", None, None, None), P(), P()),
        check_vma=False,
    )
```

```python
import functools
import math

import jax
import jax.numpy as jnp
from jax import lax
from jax.experimental import pallas as pl
from jax.experimental.pallas import tpu as pltpu
from jax.sharding import PartitionSpec as P

RIM = 2
MESH = pl.DeviceIdType.MESH

ROWS = 27 * 128
HALF = 1792
FULL = 2 * HALF
HALF_OFFSETS = HALF // 128
PIECE = HALF // 16
QUARTER = 32


def rows(start, size):
    return pl.ds(pl.multiple_of(start, 16), size)


def place():
    gx, gy = lax.axis_index("gx"), lax.axis_index("gy")
    core = lax.rem(gx, 2)
    x = lax.rem(gx // 2, 2) * 2 + gy // 4
    return gx // 4, x, lax.rem(gy, 4), core


def device(z, x, y, core):
    return ((z * 2 + x // 2) * 2 + core, lax.rem(x, 2) * 4 + y)


def partner():
    z, x, y, core = place()
    return device(z, x, y, 1 - core)


def hops(d):
    return min(d // 4, 4 - d // 4) + min(d % 4, 4 - d % 4)


PLANE = sorted(range(1, 16), key=lambda d: -hops(d))


def in_plane(d):
    z, x, y, core = place()
    return device(z, lax.rem(x + d // 4, 4), lax.rem(y + d % 4, 4), core)


def plane_index(d):
    _, x, y, _ = place()
    return lax.rem(x + d // 4, 4) * 4 + lax.rem(y + d % 4, 4)


def opposite(d):
    return (4 - d // 4) % 4 * 4 + (4 - d % 4) % 4


def near(d):
    z, x, y, core = place()
    index = lax.rem(z + d, 4)
    return index, device(z // 4 * 4 + index, x, y, core)


def far(d):
    z, x, y, core = place()
    return device(lax.rem(z + 4 * d, 16), x, y, core)


class Reduce:
    scratch = [
        pltpu.VMEM((HALF, 128), jnp.bfloat16),
        pltpu.VMEM((15, PIECE, 128), jnp.bfloat16),
        pltpu.VMEM((4 * QUARTER, 128), jnp.bfloat16),
        pltpu.VMEM((3, QUARTER, 128), jnp.bfloat16),
        pltpu.VMEM((4, QUARTER, 128), jnp.bfloat16),
        pltpu.VMEM((4 * QUARTER, 128), jnp.bfloat16),
        pltpu.SemaphoreType.DMA((2, 16)),
        pltpu.SemaphoreType.DMA((2, 4)),
        pltpu.SemaphoreType.DMA((2, 4)),
        pltpu.SemaphoreType.DMA((2, 4)),
        pltpu.SemaphoreType.DMA((2, 16)),
        pltpu.SemaphoreType.DMA((2, 16)),
    ]

    def __init__(self, out, scale, *scratch):
        self.out, self.scale = out, scale
        (
            self.part,
            self.got_plane,
            self.plane_sum,
            self.got_near,
            self.fars,
            self.whole,
            self.plane_sems,
            self.near_sems,
            self.far_sems,
            self.back_sems,
            self.gather_sems,
            self.core_sems,
        ) = scratch
        self.sent = []

    def clear(self):
        self.plane_sum[PIECE:] = jnp.zeros((4 * QUARTER - PIECE, 128), jnp.bfloat16)

    def send(self, src, dst, sems, index, device_id):
        copy = pltpu.make_async_remote_copy(
            src_ref=src,
            dst_ref=dst,
            send_sem=sems.at[0, index],
            recv_sem=sems.at[1, index],
            device_id=device_id,
            device_id_type=MESH,
        )
        copy.start()
        self.sent.append(copy)

    def arrive(self, dst, sems, index):
        pltpu.make_async_copy(dst, dst, sems.at[1, index]).wait()

    def start_plane(self):
        for d in PLANE:
            self.send(
                self.part.at[rows(plane_index(d) * PIECE, PIECE)],
                self.got_plane.at[d - 1],
                self.plane_sems,
                d,
                in_plane(d),
            )

    def start_near(self):
        total = self.part[rows(plane_index(0) * PIECE, PIECE)].astype(jnp.float32)
        for d in reversed(PLANE):
            self.arrive(self.got_plane.at[d - 1], self.plane_sems, d)
            total = total + self.got_plane[d - 1].astype(jnp.float32)
        self.plane_sum[:PIECE] = total.astype(jnp.bfloat16)
        for d in (2, 1, 3):
            index, target = near(d)
            self.send(
                self.plane_sum.at[rows(index * QUARTER, QUARTER)],
                self.got_near.at[d - 1],
                self.near_sems,
                d,
                target,
            )

    def start_far(self):
        index, _ = near(0)
        total = self.plane_sum[rows(index * QUARTER, QUARTER)].astype(jnp.float32)
        for d in (1, 2, 3):
            self.arrive(self.got_near.at[d - 1], self.near_sems, d)
            total = total + self.got_near[d - 1].astype(jnp.float32)
        group = place()[0] // 4
        self.fars[group] = total.astype(jnp.bfloat16)
        for d in (2, 1, 3):
            self.send(self.fars.at[group], self.fars.at[group], self.far_sems, d, far(d))

    def start_back(self):
        group = place()[0] // 4
        for d in (1, 3, 2):
            self.arrive(self.fars.at[lax.rem(group + 4 - d, 4)], self.far_sems, d)
        total = self.fars[0].astype(jnp.float32)
        for other in (1, 2, 3):
            total = total + self.fars[other].astype(jnp.float32)
        index, _ = near(0)
        piece = rows(index * QUARTER, QUARTER)
        self.whole[piece] = (total * self.scale).astype(jnp.bfloat16)
        for d in (2, 1, 3):
            self.send(self.whole.at[piece], self.whole.at[piece], self.back_sems, d, near(d)[1])

    def spot(self, d, core):
        return self.out.at[rows(core * HALF + plane_index(d) * PIECE, PIECE)]

    def start_gather(self):
        for d in (1, 3, 2):
            piece = self.whole.at[rows(near(4 - d)[0] * QUARTER, QUARTER)]
            self.arrive(piece, self.back_sems, d)
        core = place()[3]
        own = self.spot(0, core)
        own[...] = self.whole[:PIECE]
        for d in PLANE:
            self.send(own, own, self.gather_sems, d, in_plane(d))
        self.send(own, own, self.core_sems, 0, partner())

    def start_core(self):
        core = place()[3]
        for d in reversed(PLANE):
            piece = self.spot(opposite(d), core)
            self.arrive(piece, self.gather_sems, d)
            self.send(piece, piece, self.core_sems, d, partner())

    def finish(self):
        core = place()[3]
        for d in range(16):
            self.arrive(self.spot(opposite(d), 1 - core), self.core_sems, d)
        for copy in self.sent:
            copy.wait_send()


def enter(peers):
    barrier = pltpu.get_barrier_semaphore()
    for peer in peers:
        pl.semaphore_signal(barrier, inc=1, device_id=peer, device_id_type=MESH)
    pl.semaphore_wait(barrier, len(peers))


BLOCKS, VOXELS, OFFSETS, SLOTS, TABLE = 8, 64, 27, 54, 24
DIRECTIONS = [(a, b) for a in (-1, 0, 1) for b in (-1, 0, 1) if (a, b) != (0, 0)]


def neighbour(direction):
    a, b = direction
    gx, gy = lax.axis_index("gx"), lax.axis_index("gy")
    return lax.rem(gx + a + 64, 64), lax.rem(gy + b + 8, 8)


def present(direction):
    a, b = direction
    gx, gy = lax.axis_index("gx") + a, lax.axis_index("gy") + b
    return (gx >= 0) & (gx < 64) & (gy >= 0) & (gy < 8)


def sigmoid(values):
    return 1.0 / (1.0 + jnp.exp(-values))


def slope(values):
    s = sigmoid(values)
    return s * (1.0 + values * (1.0 - s))


IN, DELTA, OUT_CHAIN, OUT_LAST, IN_CHAIN, IN_LAST = 0, 2, 4, 6, 8, 10


def write_plan(in_ref, out_ref, live_ref, plan):
    shape = (OFFSETS, OFFSETS)
    lane = lax.broadcasted_iota(jnp.int32, shape, 1)
    offset = lax.broadcasted_iota(jnp.int32, shape, 0)

    def across(values, s):
        return jnp.broadcast_to(values[s : s + 1], shape)

    def down(values, s):
        picked = jnp.where(lane == offset, across(values, s), -1)
        return jnp.broadcast_to(jnp.max(picked, axis=1, keepdims=True), shape)

    def chain(values, row, last_row):
        columns = [down(values, s) for s in (0, 1)]
        last = jnp.zeros(shape, jnp.int32)
        for s in (0, 1):
            target = across(values, s)
            found = jnp.zeros(shape, jnp.int32)
            for t in (0, 1):
                earlier = 2 * offset + t < 2 * lane + s
                same = (columns[t] == target) & earlier & (target >= 0)
                found = jnp.maximum(found, jnp.where(same, 2 * offset + t + 1, 0))
            last = jnp.maximum(last, jnp.where(columns[s] == lane, 2 * offset + s + 1, 0))
            plan[row + s : row + s + 1, :OFFSETS] = jnp.max(found, axis=0, keepdims=True)
        plan[last_row : last_row + 1, :OFFSETS] = jnp.max(last, axis=0, keepdims=True)

    plan[...] = jnp.zeros_like(plan)
    source, target, live = in_ref[...], out_ref[...], live_ref[...]
    plan[IN : IN + 2, :OFFSETS] = source
    plan[DELTA : DELTA + 2, :OFFSETS] = jnp.where(live > 0, target, BLOCKS)
    chain(jnp.where(live > 0, target, -1), OUT_CHAIN, OUT_LAST)
    chain(jnp.where(live > 0, source, -1), IN_CHAIN, IN_LAST)


UNROLL = 9


def step_loop(count, body, unroll=None):
    unroll = unroll or UNROLL
    unroll = max(u for u in range(1, unroll + 1) if count % u == 0)

    @pl.loop(0, count // unroll)
    def _(step):
        for u in range(unroll):
            body(step * unroll + u)


def pair_of(table, plan, row, k):
    return [table[plan[row, k]], table[plan[row + 1, k]]]


def convolve(table, plan, row, chain, weight, sums, flipped):
    def body(k):
        product = lax.dot_general(
            jnp.concatenate(pair_of(table, plan, row, k), axis=0),
            weight[k],
            (((1,), (1 if flipped else 0,)), ((), ())),
            preferred_element_type=jnp.float32,
        )
        sums[2 * k + 1] = sums[plan[chain, k]] + product[:VOXELS]
        sums[2 * k + 2] = sums[plan[chain + 1, k]] + product[VOXELS:]

    step_loop(OFFSETS, body)


def weight_terms(tables, deltas, plans, part):
    core = place()[3]

    def body(j):
        k = jnp.minimum(core * HALF_OFFSETS + j, OFFSETS - 1)
        left, right = [], []
        for table, delta, plan in zip(tables, deltas, plans):
            left += pair_of(table, plan, IN, k)
            right += pair_of(delta, plan, DELTA, k)
        product = lax.dot_general(
            jnp.concatenate(left, axis=0),
            jnp.concatenate(right, axis=0),
            (((0,), (0,)), ((), ())),
            preferred_element_type=jnp.float32,
        )
        part[rows(j * 128, 128)] = product.astype(jnp.bfloat16)

    step_loop(HALF_OFFSETS, body, 7)


class Swap:
    def __init__(self, index, send_sems, recv_sems, sources, targets):
        self.copies = []
        for g, direction in enumerate(DIRECTIONS):
            copy = pltpu.make_async_remote_copy(
                src_ref=sources[g],
                dst_ref=targets[7 - g],
                send_sem=send_sems.at[index, g],
                recv_sem=recv_sems.at[index, 7 - g],
                device_id=neighbour(direction),
                device_id_type=MESH,
            )
            copy.start()
            self.copies.append(copy)

    def arrive(self):
        for copy in self.copies:
            copy.wait_recv()

    def finish(self):
        for copy in self.copies:
            copy.wait_send()


def rim_slots(table):
    return [table.at[pl.ds(BLOCKS + RIM * g, RIM)] for g in range(8)]


def clear_outside(table):
    for g, direction in enumerate(DIRECTIONS):

        @pl.when(jnp.logical_not(present(direction)))
        def _():
            table[BLOCKS + RIM * g : BLOCKS + RIM * (g + 1)] = jnp.zeros(
                (RIM, VOXELS, 128), jnp.bfloat16
            )


def routed(own, arrived, r):
    total = own
    for g, direction in enumerate(DIRECTIONS):
        total = total + jnp.where(present(direction), arrived[g, r].astype(jnp.float32), 0.0)
    return total


BLOCK_SET = (VOXELS, 128)
SCRATCH = [
    pltpu.VMEM((2, OFFSETS), jnp.int32),
    pltpu.VMEM((2, OFFSETS), jnp.int32),
    pltpu.VMEM((2, OFFSETS), jnp.int32),
    pltpu.VMEM((OFFSETS, 128, 128), jnp.bfloat16),
    pltpu.VMEM((OFFSETS, 128, 128), jnp.bfloat16),
    pltpu.VMEM((BLOCKS,) + BLOCK_SET, jnp.bfloat16),
    pltpu.VMEM((16, 128), jnp.int32),
    pltpu.VMEM((16, 128), jnp.int32),
    pltpu.SMEM((16, 128), jnp.int32),
    pltpu.SMEM((16, 128), jnp.int32),
    pltpu.VMEM((TABLE,) + BLOCK_SET, jnp.bfloat16),
    pltpu.VMEM((TABLE,) + BLOCK_SET, jnp.bfloat16),
    pltpu.VMEM((TABLE,) + BLOCK_SET, jnp.bfloat16),
    pltpu.VMEM((TABLE,) + BLOCK_SET, jnp.bfloat16),
    pltpu.VMEM((2 * OFFSETS + 2,) + BLOCK_SET, jnp.float32),
    pltpu.VMEM((BLOCKS,) + BLOCK_SET, jnp.float32),
    pltpu.VMEM((BLOCKS + 1,) + BLOCK_SET, jnp.bfloat16),
    pltpu.VMEM((BLOCKS + 1,) + BLOCK_SET, jnp.bfloat16),
    pltpu.VMEM((BLOCKS + 1,) + BLOCK_SET, jnp.bfloat16),
    pltpu.VMEM((BLOCKS + 1,) + BLOCK_SET, jnp.bfloat16),
    pltpu.VMEM((8, RIM) + BLOCK_SET, jnp.bfloat16),
    pltpu.VMEM((8, RIM) + BLOCK_SET, jnp.bfloat16),
    pltpu.VMEM((8, RIM) + BLOCK_SET, jnp.bfloat16),
    pltpu.VMEM((8, RIM) + BLOCK_SET, jnp.bfloat16),
    pltpu.SemaphoreType.DMA((9,)),
    pltpu.SemaphoreType.DMA((2, 8)),
    pltpu.SemaphoreType.DMA((4, 8)),
    pltpu.SemaphoreType.DMA((4, 8)),
]


def block_kernel(
    scale,
    voxels_in,
    first_weight_in,
    second_weight_in,
    in_slots,
    out_slots,
    live_slots,
    out_grad_in,
    result,
    input_grad,
    first_grad,
    second_grad,
    *scratch,
):
    (
        in_rows,
        out_rows,
        live_rows,
        first_weight,
        second_weight,
        out_grad,
        plan_rows,
        other_rows,
        plan,
        other_plan,
        table_x,
        table_h,
        other_x,
        other_h,
        sums,
        first_sum,
        first_delta,
        second_delta,
        other_first,
        other_second,
        give_h,
        got_h,
        give_x,
        got_x,
        load_sems,
        core_sems,
        send_sems,
        recv_sems,
    ) = scratch[: len(SCRATCH)]
    count = len(Reduce.scratch)
    reduces = scratch[len(SCRATCH) :]
    first = Reduce(first_grad, scale, *reduces[:count])
    second = Reduce(second_grad, scale, *reduces[count:])
    to_core = []

    def load(index, src, dst):
        copy = pltpu.make_async_copy(src, dst, load_sems.at[index])
        copy.start()
        return copy

    def share(index, src, dst):
        copy = pltpu.make_async_remote_copy(
            src_ref=src,
            dst_ref=dst,
            send_sem=core_sems.at[0, index],
            recv_sem=core_sems.at[1, index],
            device_id=partner(),
            device_id_type=MESH,
        )
        copy.start()
        to_core.append(copy)
        return copy

    own = table_x.at[pl.ds(0, BLOCKS)]
    load_x = load(0, voxels_in, own)
    load_slots = [
        load(1, in_slots, in_rows),
        load(2, out_slots, out_rows),
        load(3, live_slots, live_rows),
    ]
    load_first = load(4, first_weight_in, first_weight)
    load_second = load(5, second_weight_in, second_weight)
    load_grad = load(6, out_grad_in, out_grad)

    others = [far(d) for d in (2, 1, 3)] + [near(d)[1] for d in (1, 2, 3)]
    others += [neighbour(direction) for direction in DIRECTIONS]
    others += [in_plane(d) for d in PLANE] + [partner()]
    enter(others)
    load_x.wait()
    rim_x = table_x.at[pl.ds(0, RIM)]
    swap_x = Swap(0, send_sems, recv_sems, [rim_x] * 8, rim_slots(table_x))

    for copy in load_slots:
        copy.wait()
    write_plan(in_rows, out_rows, live_rows, plan_rows)
    load_plan = load(7, plan_rows, plan)
    share_plan = share(0, plan_rows, other_rows)
    zeros = jnp.zeros(BLOCK_SET, jnp.bfloat16)
    for delta in (first_delta, second_delta, other_first, other_second):
        delta[BLOCKS] = zeros
    sums[0] = jnp.zeros(BLOCK_SET, jnp.float32)
    first.clear()
    second.clear()
    load_plan.wait()
    share_plan.wait_recv()
    load_other = load(8, other_rows, other_plan)
    load_first.wait()

    swap_x.arrive()
    clear_outside(table_x)
    share_x = share(1, table_x, other_x)
    convolve(table_x, plan, IN, OUT_CHAIN, first_weight, sums, False)

    def hide(block):
        total = sums[plan[OUT_LAST, block]]
        first_sum[block] = total
        table_h[block] = (total * sigmoid(total)).astype(jnp.bfloat16)

    for block in range(RIM):
        hide(block)
    rim_h = table_h.at[pl.ds(0, RIM)]
    swap_h = Swap(1, send_sems, recv_sems, [rim_h] * 8, rim_slots(table_h))
    pl.loop(RIM, BLOCKS)(hide)

    load_other.wait()
    load_second.wait()
    load_grad.wait()
    swap_h.arrive()
    clear_outside(table_h)
    share_h = share(2, table_h, other_h)
    convolve(table_h, plan, IN, OUT_CHAIN, second_weight, sums, False)

    @pl.loop(0, BLOCKS)
    def _(block):
        joined = sums[plan[OUT_LAST, block]] + table_x[block].astype(jnp.float32)
        gate = sigmoid(joined)
        result[block] = (joined * gate).astype(jnp.bfloat16)
        second_delta[block] = (
            out_grad[block].astype(jnp.float32) * (gate * (1.0 + joined * (1.0 - gate)))
        ).astype(jnp.bfloat16)

    def all_of(delta, first_block, last_block):
        return delta.at[pl.ds(first_block, last_block - first_block)]

    share_second = share(
        3, all_of(second_delta, 0, BLOCKS), all_of(other_second, 0, BLOCKS)
    )

    def give(buffer):
        @pl.loop(0, 8)
        def _(g):
            for r in range(RIM):
                buffer[g, r] = sums[plan[IN_LAST, BLOCKS + RIM * g + r]].astype(jnp.bfloat16)

    def eight(buffer):
        return [buffer.at[g] for g in range(8)]

    convolve(second_delta, plan, DELTA, IN_CHAIN, second_weight, sums, True)
    give(give_h)
    back_h = Swap(2, send_sems, recv_sems, eight(give_h), eight(got_h))

    def descend(block, total):
        first_delta[block] = (total * slope(first_sum[block])).astype(jnp.bfloat16)

    @pl.loop(RIM, BLOCKS)
    def _(block):
        descend(block, sums[plan[IN_LAST, block]])

    share_inner = share(
        4, all_of(first_delta, RIM, BLOCKS), all_of(other_first, RIM, BLOCKS)
    )
    share_h.wait_recv()
    share_second.wait_recv()
    weight_terms(
        (table_h, other_h), (second_delta, other_second), (plan, other_plan), second.part
    )
    second.start_plane()

    back_h.arrive()
    for r in range(RIM):
        descend(r, routed(sums[plan[IN_LAST, r]], got_h, r))
    share_rim = share(5, all_of(first_delta, 0, RIM), all_of(other_first, 0, RIM))
    share_x.wait_recv()
    share_inner.wait_recv()
    share_rim.wait_recv()
    weight_terms((table_x, other_x), (first_delta, other_first), (plan, other_plan), first.part)
    first.start_plane()

    convolve(first_delta, plan, DELTA, IN_CHAIN, first_weight, sums, True)
    give(give_x)
    back_x = Swap(3, send_sems, recv_sems, eight(give_x), eight(got_x))
    second.start_near()

    def land(block, total):
        input_grad[block] = (total + second_delta[block].astype(jnp.float32)).astype(jnp.bfloat16)

    @pl.loop(RIM, BLOCKS)
    def _(block):
        land(block, sums[plan[IN_LAST, block]])

    second.start_far()
    first.start_near()
    back_x.arrive()
    for r in range(RIM):
        land(r, routed(sums[plan[IN_LAST, r]], got_x, r))
    first.start_far()
    second.start_back()
    first.start_back()
    second.start_gather()
    first.start_gather()
    second.start_core()
    first.start_core()
    for copy in to_core:
        copy.wait_send()
    for swap in (swap_x, swap_h, back_h, back_x):
        swap.finish()
    second.finish()
    first.finish()


def place_kernel(*refs):
    sems = refs[-1]
    copies = []
    for index in range(4):
        copy = pltpu.make_async_copy(refs[index], refs[4 + index], sems.at[index])
        copy.start()
        copies.append(copy)
    for copy in copies:
        copy.wait()


def shards(voxels, first_weight, second_weight, in_slots, out_slots, live_slots, out_grad):
    tile = (BLOCKS,) + BLOCK_SET
    scale = 1.0 / math.sqrt(
        lax.axis_size("gx") * lax.axis_size("gy") * OFFSETS * in_slots.shape[3] * VOXELS
    )
    field = jax.ShapeDtypeStruct(tile, jnp.bfloat16)
    grad = jax.ShapeDtypeStruct((FULL, 128), jnp.bfloat16)
    vmem, hbm = (pl.BlockSpec(memory_space=space) for space in (pltpu.VMEM, pltpu.HBM))

    def slots(values):
        return values.reshape(values.shape[2:]).T

    def in_hbm(*values):
        return [pltpu.with_memory_space_constraint(value, pltpu.HBM) for value in values]

    outputs = pl.pallas_call(
        functools.partial(block_kernel, scale),
        out_shape=(field, field, grad, grad),
        in_specs=[hbm] * 7,
        out_specs=[vmem] * 4,
        scratch_shapes=SCRATCH + Reduce.scratch * 2,
        compiler_params=pltpu.CompilerParams(
            collective_id=0, has_side_effects=True, vmem_limit_bytes=48 * 1024 * 1024
        ),
        cost_estimate=pl.CostEstimate(
            flops=6 * 54 * VOXELS * 128 * 128 * 2,
            bytes_accessed=4 * FULL * 256,
            transcendentals=4 * BLOCKS * VOXELS * 128,
        ),
        name="block",
    )(
        *in_hbm(
            voxels.reshape(tile),
            first_weight,
            second_weight,
            slots(in_slots),
            slots(out_slots),
            slots(live_slots),
            out_grad.reshape(tile),
        )
    )
    whole = jax.ShapeDtypeStruct((ROWS, 128), jnp.bfloat16)
    result, input_grad, first_grad, second_grad = pl.pallas_call(
        lambda *refs: place_kernel(
            refs[0], refs[1], refs[2].at[pl.ds(0, ROWS)], refs[3].at[pl.ds(0, ROWS)], *refs[4:]
        ),
        out_shape=(field, field, whole, whole),
        in_specs=[vmem] * 4,
        out_specs=[hbm] * 4,
        scratch_shapes=[pltpu.SemaphoreType.DMA((4,))],
        compiler_params=pltpu.CompilerParams(vmem_limit_bytes=1024 * 1024),
        name="place",
    )(*outputs)
    return (
        result.reshape(voxels.shape),
        input_grad.reshape(voxels.shape),
        first_grad.reshape(first_weight.shape),
        second_grad.reshape(first_weight.shape),
    )


def solution(mesh):
    return jax.shard_map(
        shards,
        mesh=mesh,
        in_specs=(
            P("gx", "gy", None, None, None),
            P(),
            P(),
            P("gx", "gy", None, None),
            P("gx", "gy", None, None),
            P("gx", "gy", None, None),
            P("gx", "gy", None, None, None),
        ),
        out_specs=(P("gx", "gy", None, None, None), P("gx", "gy", None, None, None), P(), P()),
        check_vma=False,
    )
```

```python
import functools
import math

import jax
import jax.numpy as jnp
from jax import lax
from jax.experimental import pallas as pl
from jax.experimental.pallas import tpu as pltpu
from jax.sharding import PartitionSpec as P

RIM = 2
MESH = pl.DeviceIdType.MESH

ROWS = 27 * 128
HALF = 1792
FULL = 2 * HALF
HALF_OFFSETS = HALF // 128
PIECE = HALF // 16
QUARTER = 32


def rows(start, size):
    return pl.ds(pl.multiple_of(start, 16), size)


def place():
    gx, gy = lax.axis_index("gx"), lax.axis_index("gy")
    core = lax.rem(gx, 2)
    x = lax.rem(gx // 2, 2) * 2 + gy // 4
    return gx // 4, x, lax.rem(gy, 4), core


def device(z, x, y, core):
    return ((z * 2 + x // 2) * 2 + core, lax.rem(x, 2) * 4 + y)


def partner():
    z, x, y, core = place()
    return device(z, x, y, 1 - core)


def hops(d):
    return min(d // 4, 4 - d // 4) + min(d % 4, 4 - d % 4)


PLANE = sorted(range(1, 16), key=lambda d: -hops(d))


def in_plane(d):
    z, x, y, core = place()
    return device(z, lax.rem(x + d // 4, 4), lax.rem(y + d % 4, 4), core)


def plane_index(d):
    _, x, y, _ = place()
    return lax.rem(x + d // 4, 4) * 4 + lax.rem(y + d % 4, 4)


def opposite(d):
    return (4 - d // 4) % 4 * 4 + (4 - d % 4) % 4


def near(d):
    z, x, y, core = place()
    index = lax.rem(z + d, 4)
    return index, device(z // 4 * 4 + index, x, y, core)


def ring(d):
    z, x, y, core = place()
    return device(lax.rem(z + d + 16, 16), x, y, core)


def far(d):
    z, x, y, core = place()
    return device(lax.rem(z + 4 * d, 16), x, y, core)


class Reduce:
    scratch = [
        pltpu.VMEM((HALF, 128), jnp.bfloat16),
        pltpu.VMEM((15, PIECE, 128), jnp.bfloat16),
        pltpu.VMEM((4 * QUARTER, 128), jnp.bfloat16),
        pltpu.VMEM((3, QUARTER, 128), jnp.bfloat16),
        pltpu.VMEM((4, QUARTER, 128), jnp.bfloat16),
        pltpu.VMEM((4 * QUARTER, 128), jnp.bfloat16),
        pltpu.SemaphoreType.DMA((2, 16)),
        pltpu.SemaphoreType.DMA((2, 4)),
        pltpu.SemaphoreType.DMA((2, 4)),
        pltpu.SemaphoreType.DMA((2, 4)),
        pltpu.SemaphoreType.DMA((2, 16)),
        pltpu.SemaphoreType.DMA((2, 16)),
    ]

    def __init__(self, out, scale, *scratch):
        self.out, self.scale = out, scale
        (
            self.part,
            self.got_plane,
            self.plane_sum,
            self.got_near,
            self.fars,
            self.whole,
            self.plane_sems,
            self.near_sems,
            self.far_sems,
            self.back_sems,
            self.gather_sems,
            self.core_sems,
        ) = scratch
        self.sent = []

    def clear(self):
        self.plane_sum[PIECE:] = jnp.zeros((4 * QUARTER - PIECE, 128), jnp.bfloat16)

    def send(self, src, dst, sems, index, device_id):
        copy = pltpu.make_async_remote_copy(
            src_ref=src,
            dst_ref=dst,
            send_sem=sems.at[0, index],
            recv_sem=sems.at[1, index],
            device_id=device_id,
            device_id_type=MESH,
        )
        copy.start()
        self.sent.append(copy)

    def drain(self):
        for copy in self.sent:
            copy.wait_send()
        self.sent = []

    def arrive(self, dst, sems, index):
        pltpu.make_async_copy(dst, dst, sems.at[1, index]).wait()

    def start_plane(self):
        for d in PLANE:
            self.send(
                self.part.at[rows(plane_index(d) * PIECE, PIECE)],
                self.got_plane.at[d - 1],
                self.plane_sems,
                d,
                in_plane(d),
            )

    def start_near(self):
        total = self.part[rows(plane_index(0) * PIECE, PIECE)].astype(jnp.float32)
        for d in reversed(PLANE):
            self.arrive(self.got_plane.at[d - 1], self.plane_sems, d)
            total = total + self.got_plane[d - 1].astype(jnp.float32)
        self.plane_sum[:PIECE] = total.astype(jnp.bfloat16)
        before, self.sent = self.sent, []
        for d in (2, 1, 3):
            index, target = near(d)
            self.send(
                self.plane_sum.at[rows(index * QUARTER, QUARTER)],
                self.got_near.at[d - 1],
                self.near_sems,
                d,
                target,
            )
        for copy in before:
            copy.wait_send()

    def start_far(self):
        index, _ = near(0)
        total = self.plane_sum[rows(index * QUARTER, QUARTER)].astype(jnp.float32)
        for d in (1, 2, 3):
            self.arrive(self.got_near.at[d - 1], self.near_sems, d)
            total = total + self.got_near[d - 1].astype(jnp.float32)
        group = place()[0] // 4
        self.fars[group] = total.astype(jnp.bfloat16)
        for d in (2, 1, 3):
            self.send(self.fars.at[group], self.fars.at[group], self.far_sems, d, far(d))

    def start_back(self):
        group = place()[0] // 4
        for d in (1, 3, 2):
            self.arrive(self.fars.at[lax.rem(group + 4 - d, 4)], self.far_sems, d)
        total = self.fars[0].astype(jnp.float32)
        for other in (1, 2, 3):
            total = total + self.fars[other].astype(jnp.float32)
        index, _ = near(0)
        piece = rows(index * QUARTER, QUARTER)
        self.whole[piece] = (total * self.scale).astype(jnp.bfloat16)
        for d in (2, 1, 3):
            self.send(self.whole.at[piece], self.whole.at[piece], self.back_sems, d, near(d)[1])

    def spot(self, d, core):
        return self.out.at[rows(core * HALF + plane_index(d) * PIECE, PIECE)]

    def start_gather(self):
        for d in (1, 3, 2):
            piece = self.whole.at[rows(near(4 - d)[0] * QUARTER, QUARTER)]
            self.arrive(piece, self.back_sems, d)
        core = place()[3]
        own = self.spot(0, core)
        own[...] = self.whole[:PIECE]
        before, self.sent = self.sent, []
        for d in PLANE:
            self.send(own, own, self.gather_sems, d, in_plane(d))
        self.send(own, own, self.core_sems, 0, partner())
        for copy in before:
            copy.wait_send()

    def start_core(self):
        core = place()[3]
        for d in reversed(PLANE):
            piece = self.spot(opposite(d), core)
            self.arrive(piece, self.gather_sems, d)
            self.send(piece, piece, self.core_sems, d, partner())

    def finish(self):
        core = place()[3]
        for d in range(16):
            self.arrive(self.spot(opposite(d), 1 - core), self.core_sems, d)
        self.drain()


def enter(peers):
    barrier = pltpu.get_barrier_semaphore()
    for peer in peers:
        pl.semaphore_signal(barrier, inc=1, device_id=peer, device_id_type=MESH)
    pl.semaphore_wait(barrier, len(peers))


BLOCKS, VOXELS, OFFSETS, SLOTS, TABLE = 8, 64, 27, 54, 24
DIRECTIONS = [(a, b) for a in (-1, 0, 1) for b in (-1, 0, 1) if (a, b) != (0, 0)]


def neighbour(direction):
    a, b = direction
    gx, gy = lax.axis_index("gx"), lax.axis_index("gy")
    return lax.rem(gx + a + 64, 64), lax.rem(gy + b + 8, 8)


def present(direction):
    a, b = direction
    gx, gy = lax.axis_index("gx") + a, lax.axis_index("gy") + b
    return (gx >= 0) & (gx < 64) & (gy >= 0) & (gy < 8)


def sigmoid(values):
    return 1.0 / (1.0 + jnp.exp(-values))


def slope(values):
    s = sigmoid(values)
    return s * (1.0 + values * (1.0 - s))


IN, DELTA, OUT_CHAIN, OUT_LAST, IN_CHAIN, IN_LAST = 0, 2, 4, 6, 8, 10


def write_plan(in_ref, out_ref, live_ref, plan):
    shape = (OFFSETS, OFFSETS)
    lane = lax.broadcasted_iota(jnp.int32, shape, 1)
    offset = lax.broadcasted_iota(jnp.int32, shape, 0)

    def across(values, s):
        return jnp.broadcast_to(values[s : s + 1], shape)

    def down(values, s):
        picked = jnp.where(lane == offset, across(values, s), -1)
        return jnp.broadcast_to(jnp.max(picked, axis=1, keepdims=True), shape)

    def chain(values, row, last_row):
        columns = [down(values, s) for s in (0, 1)]
        last = jnp.zeros(shape, jnp.int32)
        for s in (0, 1):
            target = across(values, s)
            found = jnp.zeros(shape, jnp.int32)
            for t in (0, 1):
                earlier = 2 * offset + t < 2 * lane + s
                same = (columns[t] == target) & earlier & (target >= 0)
                found = jnp.maximum(found, jnp.where(same, 2 * offset + t + 1, 0))
            last = jnp.maximum(last, jnp.where(columns[s] == lane, 2 * offset + s + 1, 0))
            plan[row + s : row + s + 1, :OFFSETS] = jnp.max(found, axis=0, keepdims=True)
        plan[last_row : last_row + 1, :OFFSETS] = jnp.max(last, axis=0, keepdims=True)

    plan[...] = jnp.zeros_like(plan)
    source, target, live = in_ref[...], out_ref[...], live_ref[...]
    plan[IN : IN + 2, :OFFSETS] = source
    plan[DELTA : DELTA + 2, :OFFSETS] = jnp.where(live > 0, target, BLOCKS)
    chain(jnp.where(live > 0, target, -1), OUT_CHAIN, OUT_LAST)
    chain(jnp.where(live > 0, source, -1), IN_CHAIN, IN_LAST)


UNROLL = 9


def step_loop(count, body, unroll=None):
    unroll = unroll or UNROLL
    unroll = max(u for u in range(1, unroll + 1) if count % u == 0)

    @pl.loop(0, count // unroll)
    def _(step):
        for u in range(unroll):
            body(step * unroll + u)


def pair_of(table, plan, row, k):
    return [table[plan[row, k]], table[plan[row + 1, k]]]


def convolve(table, plan, row, chain, weight, sums, flipped):
    def body(k):
        product = lax.dot_general(
            jnp.concatenate(pair_of(table, plan, row, k), axis=0),
            weight[k],
            (((1,), (1 if flipped else 0,)), ((), ())),
            preferred_element_type=jnp.float32,
        )
        sums[2 * k + 1] = sums[plan[chain, k]] + product[:VOXELS]
        sums[2 * k + 2] = sums[plan[chain + 1, k]] + product[VOXELS:]

    step_loop(OFFSETS, body)


def weight_terms(tables, deltas, plans, part):
    core = place()[3]

    def body(j):
        k = jnp.minimum(core * HALF_OFFSETS + j, OFFSETS - 1)
        left, right = [], []
        for table, delta, plan in zip(tables, deltas, plans):
            left += pair_of(table, plan, IN, k)
            right += pair_of(delta, plan, DELTA, k)
        product = lax.dot_general(
            jnp.concatenate(left, axis=0),
            jnp.concatenate(right, axis=0),
            (((0,), (0,)), ((), ())),
            preferred_element_type=jnp.float32,
        )
        part[rows(j * 128, 128)] = product.astype(jnp.bfloat16)

    step_loop(HALF_OFFSETS, body, 7)


class Swap:
    def __init__(self, index, send_sems, recv_sems, sources, targets):
        self.copies = []
        for g, direction in enumerate(DIRECTIONS):
            copy = pltpu.make_async_remote_copy(
                src_ref=sources[g],
                dst_ref=targets[7 - g],
                send_sem=send_sems.at[index, g],
                recv_sem=recv_sems.at[index, 7 - g],
                device_id=neighbour(direction),
                device_id_type=MESH,
            )
            copy.start()
            self.copies.append(copy)

    def arrive(self):
        for copy in self.copies:
            copy.wait_recv()

    def finish(self):
        for copy in self.copies:
            copy.wait_send()


def rim_slots(table):
    return [table.at[pl.ds(BLOCKS + RIM * g, RIM)] for g in range(8)]


def clear_outside(table):
    for g, direction in enumerate(DIRECTIONS):

        @pl.when(jnp.logical_not(present(direction)))
        def _():
            table[BLOCKS + RIM * g : BLOCKS + RIM * (g + 1)] = jnp.zeros(
                (RIM, VOXELS, 128), jnp.bfloat16
            )


def routed(own, arrived, r):
    total = own
    for g, direction in enumerate(DIRECTIONS):
        total = total + jnp.where(present(direction), arrived[g, r].astype(jnp.float32), 0.0)
    return total


BLOCK_SET = (VOXELS, 128)
SCRATCH = [
    pltpu.VMEM((2, OFFSETS), jnp.int32),
    pltpu.VMEM((2, OFFSETS), jnp.int32),
    pltpu.VMEM((2, OFFSETS), jnp.int32),
    pltpu.VMEM((OFFSETS, 128, 128), jnp.bfloat16),
    pltpu.VMEM((OFFSETS, 128, 128), jnp.bfloat16),
    pltpu.VMEM((BLOCKS,) + BLOCK_SET, jnp.bfloat16),
    pltpu.VMEM((16, 128), jnp.int32),
    pltpu.VMEM((16, 128), jnp.int32),
    pltpu.SMEM((16, 128), jnp.int32),
    pltpu.SMEM((16, 128), jnp.int32),
    pltpu.VMEM((TABLE,) + BLOCK_SET, jnp.bfloat16),
    pltpu.VMEM((TABLE,) + BLOCK_SET, jnp.bfloat16),
    pltpu.VMEM((TABLE,) + BLOCK_SET, jnp.bfloat16),
    pltpu.VMEM((TABLE,) + BLOCK_SET, jnp.bfloat16),
    pltpu.VMEM((2 * OFFSETS + 2,) + BLOCK_SET, jnp.float32),
    pltpu.VMEM((BLOCKS,) + BLOCK_SET, jnp.float32),
    pltpu.VMEM((BLOCKS + 1,) + BLOCK_SET, jnp.bfloat16),
    pltpu.VMEM((BLOCKS + 1,) + BLOCK_SET, jnp.bfloat16),
    pltpu.VMEM((BLOCKS + 1,) + BLOCK_SET, jnp.bfloat16),
    pltpu.VMEM((BLOCKS + 1,) + BLOCK_SET, jnp.bfloat16),
    pltpu.VMEM((8, RIM) + BLOCK_SET, jnp.bfloat16),
    pltpu.VMEM((8, RIM) + BLOCK_SET, jnp.bfloat16),
    pltpu.VMEM((8, RIM) + BLOCK_SET, jnp.bfloat16),
    pltpu.VMEM((8, RIM) + BLOCK_SET, jnp.bfloat16),
    pltpu.SemaphoreType.DMA((9,)),
    pltpu.SemaphoreType.DMA((2, 8)),
    pltpu.SemaphoreType.DMA((4, 8)),
    pltpu.SemaphoreType.DMA((4, 8)),
    pltpu.SemaphoreType.REGULAR((3,)),
]


def block_kernel(
    scale,
    voxels_in,
    first_weight_in,
    second_weight_in,
    in_slots,
    out_slots,
    live_slots,
    out_grad_in,
    result,
    input_grad,
    first_grad,
    second_grad,
    *scratch,
):
    (
        in_rows,
        out_rows,
        live_rows,
        first_weight,
        second_weight,
        out_grad,
        plan_rows,
        other_rows,
        plan,
        other_plan,
        table_x,
        table_h,
        other_x,
        other_h,
        sums,
        first_sum,
        first_delta,
        second_delta,
        other_first,
        other_second,
        give_h,
        got_h,
        give_x,
        got_x,
        load_sems,
        core_sems,
        send_sems,
        recv_sems,
        reach,
    ) = scratch[: len(SCRATCH)]
    count = len(Reduce.scratch)
    reduces = scratch[len(SCRATCH) :]
    first = Reduce(first_grad, scale, *reduces[:count])
    second = Reduce(second_grad, scale, *reduces[count:])
    to_core = []

    def load(index, src, dst):
        copy = pltpu.make_async_copy(src, dst, load_sems.at[index])
        copy.start()
        return copy

    def share(index, src, dst):
        copy = pltpu.make_async_remote_copy(
            src_ref=src,
            dst_ref=dst,
            send_sem=core_sems.at[0, index],
            recv_sem=core_sems.at[1, index],
            device_id=partner(),
            device_id_type=MESH,
        )
        copy.start()
        to_core.append(copy)
        return copy

    own = table_x.at[pl.ds(0, BLOCKS)]
    load_x = load(0, voxels_in, own)
    load_slots = [
        load(1, in_slots, in_rows),
        load(2, out_slots, out_rows),
        load(3, live_slots, live_rows),
    ]
    load_first = load(4, first_weight_in, first_weight)
    load_second = load(5, second_weight_in, second_weight)
    load_grad = load(6, out_grad_in, out_grad)

    def signal_reach(step):
        for d in (1 << step, -(1 << step)):
            pl.semaphore_signal(reach.at[step], inc=1, device_id=ring(d), device_id_type=MESH)

    enter(
        [neighbour(direction) for direction in DIRECTIONS]
        + [in_plane(d) for d in PLANE]
        + [ring(1), ring(-1), partner()]
    )
    load_x.wait()
    rim_x = table_x.at[pl.ds(0, RIM)]
    swap_x = Swap(0, send_sems, recv_sems, [rim_x] * 8, rim_slots(table_x))
    signal_reach(0)

    for copy in load_slots:
        copy.wait()
    write_plan(in_rows, out_rows, live_rows, plan_rows)
    load_plan = load(7, plan_rows, plan)
    share_plan = share(0, plan_rows, other_rows)
    zeros = jnp.zeros(BLOCK_SET, jnp.bfloat16)
    for delta in (first_delta, second_delta, other_first, other_second):
        delta[BLOCKS] = zeros
    sums[0] = jnp.zeros(BLOCK_SET, jnp.float32)
    first.clear()
    second.clear()
    load_plan.wait()
    share_plan.wait_recv()
    load_other = load(8, other_rows, other_plan)
    load_first.wait()

    swap_x.arrive()
    pl.semaphore_wait(reach.at[0], 2)
    signal_reach(1)
    clear_outside(table_x)
    share_x = share(1, table_x, other_x)
    convolve(table_x, plan, IN, OUT_CHAIN, first_weight, sums, False)

    def hide(block):
        total = sums[plan[OUT_LAST, block]]
        first_sum[block] = total
        table_h[block] = (total * sigmoid(total)).astype(jnp.bfloat16)

    for block in range(RIM):
        hide(block)
    rim_h = table_h.at[pl.ds(0, RIM)]
    swap_h = Swap(1, send_sems, recv_sems, [rim_h] * 8, rim_slots(table_h))
    for block in range(RIM, BLOCKS):
        hide(block)
    swap_x.finish()

    load_other.wait()
    load_second.wait()
    load_grad.wait()
    swap_h.arrive()
    pl.semaphore_wait(reach.at[1], 2)
    signal_reach(2)
    clear_outside(table_h)
    share_h = share(2, table_h, other_h)
    convolve(table_h, plan, IN, OUT_CHAIN, second_weight, sums, False)

    for block in range(BLOCKS):
        joined = sums[plan[OUT_LAST, block]] + table_x[block].astype(jnp.float32)
        gate = sigmoid(joined)
        result[block] = (joined * gate).astype(jnp.bfloat16)
        second_delta[block] = (
            out_grad[block].astype(jnp.float32) * (gate * (1.0 + joined * (1.0 - gate)))
        ).astype(jnp.bfloat16)

    def all_of(delta, first_block, last_block):
        return delta.at[pl.ds(first_block, last_block - first_block)]

    share_second = share(
        3, all_of(second_delta, 0, BLOCKS), all_of(other_second, 0, BLOCKS)
    )

    def give(buffer):
        for g in range(8):
            for r in range(RIM):
                buffer[g, r] = sums[plan[IN_LAST, BLOCKS + RIM * g + r]].astype(jnp.bfloat16)

    def eight(buffer):
        return [buffer.at[g] for g in range(8)]

    convolve(second_delta, plan, DELTA, IN_CHAIN, second_weight, sums, True)
    give(give_h)
    back_h = Swap(2, send_sems, recv_sems, eight(give_h), eight(got_h))

    def descend(block, total):
        first_delta[block] = (total * slope(first_sum[block])).astype(jnp.bfloat16)

    swap_h.finish()
    for block in range(RIM, BLOCKS):
        descend(block, sums[plan[IN_LAST, block]])

    share_inner = share(
        4, all_of(first_delta, RIM, BLOCKS), all_of(other_first, RIM, BLOCKS)
    )
    share_h.wait_recv()
    share_second.wait_recv()
    weight_terms(
        (table_h, other_h), (second_delta, other_second), (plan, other_plan), second.part
    )
    second.start_plane()

    back_h.arrive()
    for r in range(RIM):
        descend(r, routed(sums[plan[IN_LAST, r]], got_h, r))
    share_rim = share(5, all_of(first_delta, 0, RIM), all_of(other_first, 0, RIM))
    share_x.wait_recv()
    share_inner.wait_recv()
    share_rim.wait_recv()
    weight_terms((table_x, other_x), (first_delta, other_first), (plan, other_plan), first.part)
    first.start_plane()

    convolve(first_delta, plan, DELTA, IN_CHAIN, first_weight, sums, True)
    give(give_x)
    back_x = Swap(3, send_sems, recv_sems, eight(give_x), eight(got_x))
    pl.semaphore_wait(reach.at[2], 2)
    second.start_near()
    back_h.finish()

    def land(block, total):
        input_grad[block] = (total + second_delta[block].astype(jnp.float32)).astype(jnp.bfloat16)

    for block in range(RIM, BLOCKS):
        land(block, sums[plan[IN_LAST, block]])
    second.start_far()
    first.start_near()
    second.start_back()
    back_x.arrive()
    for r in range(RIM):
        land(r, routed(sums[plan[IN_LAST, r]], got_x, r))
    for copy in to_core:
        copy.wait_send()
    back_x.finish()
    first.start_far()
    second.start_gather()
    first.start_back()
    second.start_core()
    first.start_gather()
    second.finish()
    first.start_core()
    first.finish()


def place_kernel(*refs):
    sems = refs[-1]
    copies = []
    for index in range(4):
        copy = pltpu.make_async_copy(refs[index], refs[4 + index], sems.at[index])
        copy.start()
        copies.append(copy)
    for copy in copies:
        copy.wait()


def shards(voxels, first_weight, second_weight, in_slots, out_slots, live_slots, out_grad):
    tile = (BLOCKS,) + BLOCK_SET
    scale = 1.0 / math.sqrt(
        lax.axis_size("gx") * lax.axis_size("gy") * OFFSETS * in_slots.shape[3] * VOXELS
    )
    field = jax.ShapeDtypeStruct(tile, jnp.bfloat16)
    grad = jax.ShapeDtypeStruct((FULL, 128), jnp.bfloat16)
    vmem, hbm = (pl.BlockSpec(memory_space=space) for space in (pltpu.VMEM, pltpu.HBM))

    def slots(values):
        return values.reshape(values.shape[2:]).T

    def in_hbm(*values):
        return [pltpu.with_memory_space_constraint(value, pltpu.HBM) for value in values]

    outputs = pl.pallas_call(
        functools.partial(block_kernel, scale),
        out_shape=(field, field, grad, grad),
        in_specs=[hbm] * 7,
        out_specs=[vmem] * 4,
        scratch_shapes=SCRATCH + Reduce.scratch * 2,
        compiler_params=pltpu.CompilerParams(
            collective_id=0, has_side_effects=True, vmem_limit_bytes=48 * 1024 * 1024
        ),
        cost_estimate=pl.CostEstimate(
            flops=6 * 54 * VOXELS * 128 * 128 * 2,
            bytes_accessed=4 * FULL * 256,
            transcendentals=4 * BLOCKS * VOXELS * 128,
        ),
        name="block",
    )(
        *in_hbm(
            voxels.reshape(tile),
            first_weight,
            second_weight,
            slots(in_slots),
            slots(out_slots),
            slots(live_slots),
            out_grad.reshape(tile),
        )
    )
    whole = jax.ShapeDtypeStruct((ROWS, 128), jnp.bfloat16)
    result, input_grad, first_grad, second_grad = pl.pallas_call(
        lambda *refs: place_kernel(
            refs[0], refs[1], refs[2].at[pl.ds(0, ROWS)], refs[3].at[pl.ds(0, ROWS)], *refs[4:]
        ),
        out_shape=(field, field, whole, whole),
        in_specs=[vmem] * 4,
        out_specs=[hbm] * 4,
        scratch_shapes=[pltpu.SemaphoreType.DMA((4,))],
        compiler_params=pltpu.CompilerParams(vmem_limit_bytes=1024 * 1024),
        name="place",
    )(*outputs)
    return (
        result.reshape(voxels.shape),
        input_grad.reshape(voxels.shape),
        first_grad.reshape(first_weight.shape),
        second_grad.reshape(first_weight.shape),
    )


def solution(mesh):
    return jax.shard_map(
        shards,
        mesh=mesh,
        in_specs=(
            P("gx", "gy", None, None, None),
            P(),
            P(),
            P("gx", "gy", None, None),
            P("gx", "gy", None, None),
            P("gx", "gy", None, None),
            P("gx", "gy", None, None, None),
        ),
        out_specs=(P("gx", "gy", None, None, None), P("gx", "gy", None, None, None), P(), P()),
        check_vma=False,
    )
```

```python
import functools
import math

import jax
import jax.numpy as jnp
from jax import lax
from jax.experimental import pallas as pl
from jax.experimental.pallas import tpu as pltpu
from jax.sharding import PartitionSpec as P

RIM = 2
MESH = pl.DeviceIdType.MESH

ROWS = 27 * 128
HALF = 1792
FULL = 2 * HALF
HALF_OFFSETS = HALF // 128
PIECE = HALF // 16
QUARTER = 32


def rows(start, size):
    return pl.ds(pl.multiple_of(start, 16), size)


def place():
    gx, gy = lax.axis_index("gx"), lax.axis_index("gy")
    core = lax.rem(gx, 2)
    x = lax.rem(gx // 2, 2) * 2 + gy // 4
    return gx // 4, x, lax.rem(gy, 4), core


def device(z, x, y, core):
    return ((z * 2 + x // 2) * 2 + core, lax.rem(x, 2) * 4 + y)


def partner():
    z, x, y, core = place()
    return device(z, x, y, 1 - core)


def hops(d):
    return min(d // 4, 4 - d // 4) + min(d % 4, 4 - d % 4)


PLANE = sorted(range(1, 16), key=lambda d: -hops(d))


def ring_of(d):
    return min(hops(d), 3) - 1


def in_plane(d):
    z, x, y, core = place()
    return device(z, lax.rem(x + d // 4, 4), lax.rem(y + d % 4, 4), core)


def plane_index(d):
    _, x, y, _ = place()
    return lax.rem(x + d // 4, 4) * 4 + lax.rem(y + d % 4, 4)


def opposite(d):
    return (4 - d // 4) % 4 * 4 + (4 - d % 4) % 4


def near(d):
    z, x, y, core = place()
    index = lax.rem(z + d, 4)
    return index, device(z // 4 * 4 + index, x, y, core)


def ring(d):
    z, x, y, core = place()
    return device(lax.rem(z + d + 16, 16), x, y, core)


def far(d):
    z, x, y, core = place()
    return device(lax.rem(z + 4 * d, 16), x, y, core)


def wait_bytes(ref, sem):
    pltpu.make_async_copy(ref, ref, sem).wait()


class Reduce:
    scratch = [
        pltpu.VMEM((HALF, 128), jnp.bfloat16),
        pltpu.VMEM((15, PIECE, 128), jnp.bfloat16),
        pltpu.VMEM((4 * QUARTER, 128), jnp.bfloat16),
        pltpu.VMEM((3, QUARTER, 128), jnp.bfloat16),
        pltpu.VMEM((4, QUARTER, 128), jnp.bfloat16),
        pltpu.VMEM((4 * QUARTER, 128), jnp.bfloat16),
        pltpu.SemaphoreType.DMA((6,)),
        pltpu.SemaphoreType.DMA((8,)),
    ]

    def __init__(self, out, scale, *scratch):
        self.out, self.scale = out, scale
        (
            self.part,
            self.got_plane,
            self.plane_sum,
            self.got_near,
            self.fars,
            self.whole,
            self.send_sems,
            self.recv_sems,
        ) = scratch

    def clear(self):
        self.plane_sum[PIECE:] = jnp.zeros((4 * QUARTER - PIECE, 128), jnp.bfloat16)

    def send(self, src, dst, send_index, recv_index, device_id):
        pltpu.make_async_remote_copy(
            src_ref=src,
            dst_ref=dst,
            send_sem=self.send_sems.at[send_index],
            recv_sem=self.recv_sems.at[recv_index],
            device_id=device_id,
            device_id_type=MESH,
        ).start()

    def sent(self, index, count, size):
        wait_bytes(self.part.at[pl.ds(0, count * size)], self.send_sems.at[index])

    def start_plane(self):
        for d in PLANE:
            self.send(
                self.part.at[rows(plane_index(d) * PIECE, PIECE)],
                self.got_plane.at[d - 1],
                0,
                0,
                in_plane(d),
            )

    def start_near(self):
        wait_bytes(self.got_plane, self.recv_sems.at[0])
        total = self.part[rows(plane_index(0) * PIECE, PIECE)].astype(jnp.float32)
        for d in range(15):
            total = total + self.got_plane[d].astype(jnp.float32)
        self.plane_sum[:PIECE] = total.astype(jnp.bfloat16)
        for d in (2, 1, 3):
            index, target = near(d)
            self.send(
                self.plane_sum.at[rows(index * QUARTER, QUARTER)],
                self.got_near.at[d - 1],
                1,
                1,
                target,
            )
        self.sent(0, 15, PIECE)

    def start_far(self):
        index, _ = near(0)
        wait_bytes(self.got_near, self.recv_sems.at[1])
        total = self.plane_sum[rows(index * QUARTER, QUARTER)].astype(jnp.float32)
        for d in range(3):
            total = total + self.got_near[d].astype(jnp.float32)
        group = place()[0] // 4
        self.fars[group] = total.astype(jnp.bfloat16)
        for d in (2, 1, 3):
            self.send(self.fars.at[group], self.fars.at[group], 2, 2, far(d))
        self.sent(1, 3, QUARTER)

    def start_back(self):
        wait_bytes(self.fars.at[pl.ds(0, 3)], self.recv_sems.at[2])
        total = self.fars[0].astype(jnp.float32)
        for other in (1, 2, 3):
            total = total + self.fars[other].astype(jnp.float32)
        piece = rows(near(0)[0] * QUARTER, QUARTER)
        self.whole[piece] = (total * self.scale).astype(jnp.bfloat16)
        for d in (2, 1, 3):
            self.send(self.whole.at[piece], self.whole.at[piece], 3, 3, near(d)[1])
        self.sent(2, 3, QUARTER)

    def spot(self, d, core):
        return self.out.at[rows(core * HALF + plane_index(d) * PIECE, PIECE)]

    def start_gather(self):
        wait_bytes(self.whole.at[pl.ds(0, 3 * QUARTER)], self.recv_sems.at[3])
        own = self.spot(0, place()[3])
        own[...] = self.whole[:PIECE]
        for d in PLANE:
            self.send(own, own, 4, 4 + ring_of(d), in_plane(d))
        self.send(own, own, 5, 7, partner())
        self.sent(3, 3, QUARTER)

    def start_core(self):
        core = place()[3]
        for index in range(3):
            group = [d for d in PLANE if ring_of(d) == index]
            wait_bytes(self.part.at[pl.ds(0, len(group) * PIECE)], self.recv_sems.at[4 + index])
            for d in group:
                piece = self.spot(opposite(d), core)
                self.send(piece, piece, 5, 7, partner())
        self.sent(4, 15, PIECE)

    def finish(self):
        wait_bytes(self.part, self.recv_sems.at[7])
        self.sent(5, 16, PIECE)


def enter(peers):
    barrier = pltpu.get_barrier_semaphore()
    for peer in peers:
        pl.semaphore_signal(barrier, inc=1, device_id=peer, device_id_type=MESH)
    pl.semaphore_wait(barrier, len(peers))


BLOCKS, VOXELS, OFFSETS, SLOTS, TABLE = 8, 64, 27, 54, 24
DIRECTIONS = [(a, b) for a in (-1, 0, 1) for b in (-1, 0, 1) if (a, b) != (0, 0)]


def neighbour(direction):
    a, b = direction
    gx, gy = lax.axis_index("gx"), lax.axis_index("gy")
    return lax.rem(gx + a + 64, 64), lax.rem(gy + b + 8, 8)


def present(direction):
    a, b = direction
    gx, gy = lax.axis_index("gx") + a, lax.axis_index("gy") + b
    return (gx >= 0) & (gx < 64) & (gy >= 0) & (gy < 8)


def sigmoid(values):
    return 1.0 / (1.0 + jnp.exp(-values))


def slope(values):
    s = sigmoid(values)
    return s * (1.0 + values * (1.0 - s))


IN, DELTA, OUT_CHAIN, OUT_LAST, IN_CHAIN, IN_LAST = 0, 2, 4, 6, 8, 10


def write_plan(in_ref, out_ref, live_ref, plan):
    shape = (OFFSETS, OFFSETS)
    lane = lax.broadcasted_iota(jnp.int32, shape, 1)
    offset = lax.broadcasted_iota(jnp.int32, shape, 0)

    def across(values, s):
        return jnp.broadcast_to(values[s : s + 1], shape)

    def down(values, s):
        picked = jnp.where(lane == offset, across(values, s), -1)
        return jnp.broadcast_to(jnp.max(picked, axis=1, keepdims=True), shape)

    def chain(values, row, last_row):
        columns = [down(values, s) for s in (0, 1)]
        last = jnp.zeros(shape, jnp.int32)
        for s in (0, 1):
            target = across(values, s)
            found = jnp.zeros(shape, jnp.int32)
            for t in (0, 1):
                earlier = 2 * offset + t < 2 * lane + s
                same = (columns[t] == target) & earlier & (target >= 0)
                found = jnp.maximum(found, jnp.where(same, 2 * offset + t + 1, 0))
            last = jnp.maximum(last, jnp.where(columns[s] == lane, 2 * offset + s + 1, 0))
            plan[row + s : row + s + 1, :OFFSETS] = jnp.max(found, axis=0, keepdims=True)
        plan[last_row : last_row + 1, :OFFSETS] = jnp.max(last, axis=0, keepdims=True)

    plan[...] = jnp.zeros_like(plan)
    source, target, live = in_ref[...], out_ref[...], live_ref[...]
    plan[IN : IN + 2, :OFFSETS] = source
    plan[DELTA : DELTA + 2, :OFFSETS] = jnp.where(live > 0, target, BLOCKS)
    chain(jnp.where(live > 0, target, -1), OUT_CHAIN, OUT_LAST)
    chain(jnp.where(live > 0, source, -1), IN_CHAIN, IN_LAST)


UNROLL = 27


def step_loop(count, body, unroll=None):
    unroll = unroll or UNROLL
    unroll = max(u for u in range(1, unroll + 1) if count % u == 0)

    @pl.loop(0, count // unroll)
    def _(step):
        for u in range(unroll):
            body(step * unroll + u)


def pair_of(table, plan, row, k):
    return [table[plan[row, k]], table[plan[row + 1, k]]]


def convolve(table, plan, row, chain, weight, sums, flipped):
    def body(k):
        product = lax.dot_general(
            jnp.concatenate(pair_of(table, plan, row, k), axis=0),
            weight[k],
            (((1,), (1 if flipped else 0,)), ((), ())),
            preferred_element_type=jnp.float32,
        )
        sums[2 * k + 1] = sums[plan[chain, k]] + product[:VOXELS]
        sums[2 * k + 2] = sums[plan[chain + 1, k]] + product[VOXELS:]

    step_loop(OFFSETS, body)


def weight_terms(tables, deltas, plans, part):
    core = place()[3]

    def body(j):
        k = jnp.minimum(core * HALF_OFFSETS + j, OFFSETS - 1)
        left, right = [], []
        for table, delta, plan in zip(tables, deltas, plans):
            left += pair_of(table, plan, IN, k)
            right += pair_of(delta, plan, DELTA, k)
        product = lax.dot_general(
            jnp.concatenate(left, axis=0),
            jnp.concatenate(right, axis=0),
            (((0,), (0,)), ((), ())),
            preferred_element_type=jnp.float32,
        )
        part[rows(j * 128, 128)] = product.astype(jnp.bfloat16)

    step_loop(HALF_OFFSETS, body, 14)


class Swap:
    def __init__(self, index, sems, sources, targets, blocks):
        self.sems, self.blocks = [sems.at[side, index] for side in (0, 1)], blocks
        for g, direction in enumerate(DIRECTIONS):
            pltpu.make_async_remote_copy(
                src_ref=sources[g],
                dst_ref=targets[7 - g],
                send_sem=self.sems[0],
                recv_sem=self.sems[1],
                device_id=neighbour(direction),
                device_id_type=MESH,
            ).start()

    def arrive(self):
        wait_bytes(self.blocks, self.sems[1])

    def finish(self):
        wait_bytes(self.blocks, self.sems[0])


def beyond(table):
    return table.at[pl.ds(BLOCKS, 8 * RIM)]


def rim_slots(table):
    return [table.at[pl.ds(BLOCKS + RIM * g, RIM)] for g in range(8)]


def clear_outside(table):
    for g, direction in enumerate(DIRECTIONS):

        @pl.when(jnp.logical_not(present(direction)))
        def _():
            table[BLOCKS + RIM * g : BLOCKS + RIM * (g + 1)] = jnp.zeros(
                (RIM, VOXELS, 128), jnp.bfloat16
            )


def routed(own, arrived, r):
    total = own
    for g, direction in enumerate(DIRECTIONS):
        total = total + jnp.where(present(direction), arrived[g, r].astype(jnp.float32), 0.0)
    return total


BLOCK_SET = (VOXELS, 128)
SCRATCH = [
    pltpu.VMEM((3, 2, OFFSETS), jnp.int32),
    pltpu.VMEM((OFFSETS, 128, 128), jnp.bfloat16),
    pltpu.VMEM((OFFSETS, 128, 128), jnp.bfloat16),
    pltpu.VMEM((BLOCKS,) + BLOCK_SET, jnp.bfloat16),
    pltpu.VMEM((16, 128), jnp.int32),
    pltpu.VMEM((16, 128), jnp.int32),
    pltpu.SMEM((16, 128), jnp.int32),
    pltpu.SMEM((16, 128), jnp.int32),
    pltpu.VMEM((TABLE,) + BLOCK_SET, jnp.bfloat16),
    pltpu.VMEM((TABLE,) + BLOCK_SET, jnp.bfloat16),
    pltpu.VMEM((TABLE,) + BLOCK_SET, jnp.bfloat16),
    pltpu.VMEM((TABLE,) + BLOCK_SET, jnp.bfloat16),
    pltpu.VMEM((2 * OFFSETS + 2,) + BLOCK_SET, jnp.float32),
    pltpu.VMEM((BLOCKS,) + BLOCK_SET, jnp.float32),
    pltpu.VMEM((BLOCKS + 1,) + BLOCK_SET, jnp.bfloat16),
    pltpu.VMEM((BLOCKS + 1,) + BLOCK_SET, jnp.bfloat16),
    pltpu.VMEM((BLOCKS + 1,) + BLOCK_SET, jnp.bfloat16),
    pltpu.VMEM((BLOCKS + 1,) + BLOCK_SET, jnp.bfloat16),
    pltpu.VMEM((8, RIM) + BLOCK_SET, jnp.bfloat16),
    pltpu.VMEM((8, RIM) + BLOCK_SET, jnp.bfloat16),
    pltpu.VMEM((8, RIM) + BLOCK_SET, jnp.bfloat16),
    pltpu.VMEM((8, RIM) + BLOCK_SET, jnp.bfloat16),
    pltpu.SemaphoreType.DMA((5,)),
    pltpu.SemaphoreType.DMA((7,)),
    pltpu.SemaphoreType.DMA((2, 4)),
    pltpu.SemaphoreType.REGULAR((3,)),
]


def block_kernel(
    scale,
    voxels_in,
    first_weight_in,
    second_weight_in,
    in_slots,
    out_slots,
    live_slots,
    out_grad_in,
    result,
    input_grad,
    first_grad,
    second_grad,
    *scratch,
):
    (
        slot_rows,
        first_weight,
        second_weight,
        out_grad,
        plan_rows,
        other_rows,
        plan,
        other_plan,
        table_x,
        table_h,
        other_x,
        other_h,
        sums,
        first_sum,
        first_delta,
        second_delta,
        other_first,
        other_second,
        give_h,
        got_h,
        give_x,
        got_x,
        load_sems,
        core_sems,
        swap_sems,
        reach,
    ) = scratch[: len(SCRATCH)]
    count = len(Reduce.scratch)
    reduces = scratch[len(SCRATCH) :]
    first = Reduce(first_grad, scale, *reduces[:count])
    second = Reduce(second_grad, scale, *reduces[count:])

    def load(index, src, dst):
        copy = pltpu.make_async_copy(src, dst, load_sems.at[index])
        copy.start()
        return copy

    def share(index, src, dst):
        copy = pltpu.make_async_remote_copy(
            src_ref=src,
            dst_ref=dst,
            send_sem=core_sems.at[6],
            recv_sem=core_sems.at[index],
            device_id=partner(),
            device_id_type=MESH,
        )
        copy.start()
        return copy

    own = table_x.at[pl.ds(0, BLOCKS)]
    load_x = load(0, voxels_in, own)
    for index, slots in enumerate((in_slots, out_slots, live_slots)):
        load(1, slots, slot_rows.at[index])
    load_first = load(2, first_weight_in, first_weight)
    load_second = load(3, second_weight_in, second_weight)
    load_grad = load(4, out_grad_in, out_grad)

    def signal_reach(step):
        for d in (1 << step, -(1 << step)):
            pl.semaphore_signal(reach.at[step], inc=1, device_id=ring(d), device_id_type=MESH)

    enter(
        [neighbour(direction) for direction in DIRECTIONS]
        + [in_plane(d) for d in PLANE]
        + [ring(1), ring(-1), partner()]
    )
    load_x.wait()
    rim_x = table_x.at[pl.ds(0, RIM)]
    swap_x = Swap(0, swap_sems, [rim_x] * 8, rim_slots(table_x), beyond(table_x))
    signal_reach(0)

    wait_bytes(slot_rows, load_sems.at[1])
    write_plan(slot_rows.at[0], slot_rows.at[1], slot_rows.at[2], plan_rows)
    load_plan = load(0, plan_rows, plan)
    share_plan = share(0, plan_rows, other_rows)
    zeros = jnp.zeros(BLOCK_SET, jnp.bfloat16)
    for delta in (first_delta, second_delta, other_first, other_second):
        delta[BLOCKS] = zeros
    sums[0] = jnp.zeros(BLOCK_SET, jnp.float32)
    first.clear()
    second.clear()
    load_plan.wait()
    share_plan.wait_recv()
    load_other = load(1, other_rows, other_plan)
    load_first.wait()

    swap_x.arrive()
    pl.semaphore_wait(reach.at[0], 2)
    signal_reach(1)
    clear_outside(table_x)
    share_plan.wait_send()
    share_x = share(1, table_x, other_x)
    convolve(table_x, plan, IN, OUT_CHAIN, first_weight, sums, False)

    def hide(block):
        total = sums[plan[OUT_LAST, block]]
        first_sum[block] = total
        table_h[block] = (total * sigmoid(total)).astype(jnp.bfloat16)

    for block in range(RIM):
        hide(block)
    rim_h = table_h.at[pl.ds(0, RIM)]
    swap_h = Swap(1, swap_sems, [rim_h] * 8, rim_slots(table_h), beyond(table_h))
    for block in range(RIM, BLOCKS):
        hide(block)
    swap_x.finish()

    load_other.wait()
    load_second.wait()
    load_grad.wait()
    swap_h.arrive()
    pl.semaphore_wait(reach.at[1], 2)
    signal_reach(2)
    clear_outside(table_h)
    share_x.wait_send()
    share_h = share(2, table_h, other_h)
    convolve(table_h, plan, IN, OUT_CHAIN, second_weight, sums, False)

    for block in range(BLOCKS):
        joined = sums[plan[OUT_LAST, block]] + table_x[block].astype(jnp.float32)
        gate = sigmoid(joined)
        result[block] = (joined * gate).astype(jnp.bfloat16)
        second_delta[block] = (
            out_grad[block].astype(jnp.float32) * (gate * (1.0 + joined * (1.0 - gate)))
        ).astype(jnp.bfloat16)

    def all_of(delta, first_block, last_block):
        return delta.at[pl.ds(first_block, last_block - first_block)]

    share_h.wait_send()
    share_second = share(
        3, all_of(second_delta, 0, BLOCKS), all_of(other_second, 0, BLOCKS)
    )

    def give(buffer):
        for g in range(8):
            for r in range(RIM):
                buffer[g, r] = sums[plan[IN_LAST, BLOCKS + RIM * g + r]].astype(jnp.bfloat16)

    def eight(buffer):
        return [buffer.at[g] for g in range(8)]

    convolve(second_delta, plan, DELTA, IN_CHAIN, second_weight, sums, True)
    give(give_h)
    back_h = Swap(2, swap_sems, eight(give_h), eight(got_h), got_h)

    def descend(block, total):
        first_delta[block] = (total * slope(first_sum[block])).astype(jnp.bfloat16)

    swap_h.finish()
    for block in range(RIM, BLOCKS):
        descend(block, sums[plan[IN_LAST, block]])

    share_second.wait_send()
    share_inner = share(
        4, all_of(first_delta, RIM, BLOCKS), all_of(other_first, RIM, BLOCKS)
    )
    share_h.wait_recv()
    share_second.wait_recv()
    weight_terms(
        (table_h, other_h), (second_delta, other_second), (plan, other_plan), second.part
    )
    second.start_plane()

    back_h.arrive()
    for r in range(RIM):
        descend(r, routed(sums[plan[IN_LAST, r]], got_h, r))
    share_inner.wait_send()
    share_rim = share(5, all_of(first_delta, 0, RIM), all_of(other_first, 0, RIM))
    share_x.wait_recv()
    share_inner.wait_recv()
    share_rim.wait_recv()
    weight_terms((table_x, other_x), (first_delta, other_first), (plan, other_plan), first.part)
    first.start_plane()

    convolve(first_delta, plan, DELTA, IN_CHAIN, first_weight, sums, True)
    give(give_x)
    back_x = Swap(3, swap_sems, eight(give_x), eight(got_x), got_x)
    pl.semaphore_wait(reach.at[2], 2)
    second.start_near()
    back_h.finish()

    def land(block, total):
        input_grad[block] = (total + second_delta[block].astype(jnp.float32)).astype(jnp.bfloat16)

    for block in range(RIM, BLOCKS):
        land(block, sums[plan[IN_LAST, block]])
    second.start_far()
    first.start_near()
    second.start_back()
    back_x.arrive()
    for r in range(RIM):
        land(r, routed(sums[plan[IN_LAST, r]], got_x, r))
    share_rim.wait_send()
    back_x.finish()
    first.start_far()
    second.start_gather()
    first.start_back()
    second.start_core()
    first.start_gather()
    second.finish()
    first.start_core()
    first.finish()


def place_kernel(*refs):
    sems = refs[-1]
    copies = []
    for index in range(4):
        copy = pltpu.make_async_copy(refs[index], refs[4 + index], sems.at[index])
        copy.start()
        copies.append(copy)
    for copy in copies:
        copy.wait()


def shards(voxels, first_weight, second_weight, in_slots, out_slots, live_slots, out_grad):
    tile = (BLOCKS,) + BLOCK_SET
    scale = 1.0 / math.sqrt(
        lax.axis_size("gx") * lax.axis_size("gy") * OFFSETS * in_slots.shape[3] * VOXELS
    )
    field = jax.ShapeDtypeStruct(tile, jnp.bfloat16)
    grad = jax.ShapeDtypeStruct((FULL, 128), jnp.bfloat16)
    vmem, hbm = (pl.BlockSpec(memory_space=space) for space in (pltpu.VMEM, pltpu.HBM))

    def slots(values):
        return values.reshape(values.shape[2:]).T

    def in_hbm(*values):
        return [pltpu.with_memory_space_constraint(value, pltpu.HBM) for value in values]

    outputs = pl.pallas_call(
        functools.partial(block_kernel, scale),
        out_shape=(field, field, grad, grad),
        in_specs=[hbm] * 7,
        out_specs=[vmem] * 4,
        scratch_shapes=SCRATCH + Reduce.scratch * 2,
        compiler_params=pltpu.CompilerParams(
            collective_id=0, has_side_effects=True, vmem_limit_bytes=48 * 1024 * 1024
        ),
        cost_estimate=pl.CostEstimate(
            flops=6 * 54 * VOXELS * 128 * 128 * 2,
            bytes_accessed=4 * FULL * 256,
            transcendentals=4 * BLOCKS * VOXELS * 128,
        ),
        name="block",
    )(
        *in_hbm(
            voxels.reshape(tile),
            first_weight,
            second_weight,
            slots(in_slots),
            slots(out_slots),
            slots(live_slots),
            out_grad.reshape(tile),
        )
    )
    whole = jax.ShapeDtypeStruct((ROWS, 128), jnp.bfloat16)
    result, input_grad, first_grad, second_grad = pl.pallas_call(
        lambda *refs: place_kernel(
            refs[0], refs[1], refs[2].at[pl.ds(0, ROWS)], refs[3].at[pl.ds(0, ROWS)], *refs[4:]
        ),
        out_shape=(field, field, whole, whole),
        in_specs=[vmem] * 4,
        out_specs=[hbm] * 4,
        scratch_shapes=[pltpu.SemaphoreType.DMA((4,))],
        compiler_params=pltpu.CompilerParams(vmem_limit_bytes=1024 * 1024),
        name="place",
    )(*outputs)
    return (
        result.reshape(voxels.shape),
        input_grad.reshape(voxels.shape),
        first_grad.reshape(first_weight.shape),
        second_grad.reshape(first_weight.shape),
    )


def solution(mesh):
    return jax.shard_map(
        shards,
        mesh=mesh,
        in_specs=(
            P("gx", "gy", None, None, None),
            P(),
            P(),
            P("gx", "gy", None, None),
            P("gx", "gy", None, None),
            P("gx", "gy", None, None),
            P("gx", "gy", None, None, None),
        ),
        out_specs=(P("gx", "gy", None, None, None), P("gx", "gy", None, None, None), P(), P()),
        check_vma=False,
    )
```

```python
import functools
import math

import jax
import jax.numpy as jnp
from jax import lax
from jax.experimental import pallas as pl
from jax.experimental.pallas import tpu as pltpu
from jax.sharding import PartitionSpec as P

RIM = 2
MESH = pl.DeviceIdType.MESH

ROWS = 27 * 128
HALF = 1792
FULL = 2 * HALF
HALF_OFFSETS = HALF // 128
PIECE = HALF // 16


def rows(start, size):
    return pl.ds(pl.multiple_of(start, 16), size)


def place():
    gx, gy = lax.axis_index("gx"), lax.axis_index("gy")
    core = lax.rem(gx, 2)
    x = lax.rem(gx // 2, 2) * 2 + gy // 4
    return gx // 4, x, lax.rem(gy, 4), core


def device(z, x, y, core):
    return ((z * 2 + x // 2) * 2 + core, lax.rem(x, 2) * 4 + y)


def partner():
    z, x, y, core = place()
    return device(z, x, y, 1 - core)


def hops(d):
    return min(d // 4, 4 - d // 4) + min(d % 4, 4 - d % 4)


PLANE = sorted(range(1, 16), key=lambda d: -hops(d))


def ring_of(d):
    return hops(d) - 1


def in_plane(d):
    z, x, y, core = place()
    return device(z, lax.rem(x + d // 4, 4), lax.rem(y + d % 4, 4), core)


def plane_index(d):
    _, x, y, _ = place()
    return lax.rem(x + d // 4, 4) * 4 + lax.rem(y + d % 4, 4)


def opposite(d):
    return (4 - d // 4) % 4 * 4 + (4 - d % 4) % 4


def ring(d):
    z, x, y, core = place()
    return device(lax.rem(z + d + 16, 16), x, y, core)


SPREAD = [1, 2, 3, 4, 15, 5, 14, 6, 13, 7, 12, 8, 11, 10, 9]


def wait_bytes(ref, sem):
    pltpu.make_async_copy(ref, ref, sem).wait()


class Reduce:
    scratch = [
        pltpu.VMEM((HALF, 128), jnp.bfloat16),
        pltpu.VMEM((15, PIECE, 128), jnp.bfloat16),
        pltpu.VMEM((PIECE, 128), jnp.bfloat16),
        pltpu.VMEM((15, PIECE, 128), jnp.bfloat16),
        pltpu.SemaphoreType.DMA((5,)),
        pltpu.SemaphoreType.DMA((8,)),
    ]

    def __init__(self, out, scale, *scratch):
        self.out, self.scale = out, scale
        (
            self.part,
            self.got_plane,
            self.plane_sum,
            self.got_root,
            self.send_sems,
            self.recv_sems,
        ) = scratch

    def send(self, src, dst, send_index, recv_index, device_id):
        pltpu.make_async_remote_copy(
            src_ref=src,
            dst_ref=dst,
            send_sem=self.send_sems.at[send_index],
            recv_sem=self.recv_sems.at[recv_index],
            device_id=device_id,
            device_id_type=MESH,
        ).start()

    def sent(self, index, count, size):
        wait_bytes(self.part.at[pl.ds(0, count * size)], self.send_sems.at[index])

    def start_plane(self):
        for d in PLANE:
            self.send(
                self.part.at[rows(plane_index(d) * PIECE, PIECE)],
                self.got_plane.at[d - 1],
                0,
                0,
                in_plane(d),
            )

    def start_root(self):
        wait_bytes(self.got_plane, self.recv_sems.at[0])
        total = self.part[rows(plane_index(0) * PIECE, PIECE)].astype(jnp.float32)
        for d in range(15):
            total = total + self.got_plane[d].astype(jnp.float32)
        self.plane_sum[...] = total.astype(jnp.bfloat16)
        z, x, y, core = place()

        @pl.when(z > 0)
        def _():
            self.send(self.plane_sum, self.got_root.at[z - 1], 1, 1, device(0, x, y, core))

        self.sent(0, 15, PIECE)

    def spot(self, d, core):
        return self.out.at[rows(core * HALF + plane_index(d) * PIECE, PIECE)]

    def start_spread(self):
        z, x, y, core = place()
        own = self.spot(0, core)

        def spread(planes):
            for plane in planes:
                self.send(own, own, 2, 2, device(plane, x, y, core))

        @pl.when(z == 0)
        def _():
            wait_bytes(self.got_root, self.recv_sems.at[1])
            total = self.plane_sum[...].astype(jnp.float32)
            for plane in range(15):
                total = total + self.got_root[plane].astype(jnp.float32)
            own[...] = (total * self.scale).astype(jnp.bfloat16)
            spread(SPREAD[:4])

        @pl.when(z > 0)
        def _():
            self.sent(1, 1, PIECE)
            wait_bytes(own, self.recv_sems.at[2])

        for d in PLANE:
            self.send(own, own, 3, 3 + ring_of(d), in_plane(d))
        self.send(own, own, 4, 7, partner())

        @pl.when(z == 0)
        def _():
            spread(SPREAD[4:])

    def start_core(self):
        core = place()[3]
        for index in range(4):
            group = [d for d in PLANE if ring_of(d) == index]
            wait_bytes(self.part.at[pl.ds(0, len(group) * PIECE)], self.recv_sems.at[3 + index])
            for d in group:
                piece = self.spot(opposite(d), core)
                self.send(piece, piece, 4, 7, partner())

        @pl.when(place()[0] == 0)
        def _():
            self.sent(2, 15, PIECE)

        self.sent(3, 15, PIECE)

    def finish(self):
        wait_bytes(self.part, self.recv_sems.at[7])
        self.sent(4, 16, PIECE)


def enter(peers):
    barrier = pltpu.get_barrier_semaphore()
    for peer in peers:
        pl.semaphore_signal(barrier, inc=1, device_id=peer, device_id_type=MESH)
    pl.semaphore_wait(barrier, len(peers))


BLOCKS, VOXELS, OFFSETS, SLOTS, TABLE = 8, 64, 27, 54, 24
DIRECTIONS = [(a, b) for a in (-1, 0, 1) for b in (-1, 0, 1) if (a, b) != (0, 0)]


def neighbour(direction):
    a, b = direction
    gx, gy = lax.axis_index("gx"), lax.axis_index("gy")
    return lax.rem(gx + a + 64, 64), lax.rem(gy + b + 8, 8)


def present(direction):
    a, b = direction
    gx, gy = lax.axis_index("gx") + a, lax.axis_index("gy") + b
    return (gx >= 0) & (gx < 64) & (gy >= 0) & (gy < 8)


def sigmoid(values):
    return 1.0 / (1.0 + jnp.exp(-values))


def slope(values):
    s = sigmoid(values)
    return s * (1.0 + values * (1.0 - s))


IN, DELTA, OUT_CHAIN, OUT_LAST, IN_CHAIN, IN_LAST = 0, 2, 4, 6, 8, 10


def write_plan(in_ref, out_ref, live_ref, plan):
    shape = (OFFSETS, OFFSETS)
    lane = lax.broadcasted_iota(jnp.int32, shape, 1)
    offset = lax.broadcasted_iota(jnp.int32, shape, 0)

    def across(values, s):
        return jnp.broadcast_to(values[s : s + 1], shape)

    def down(values, s):
        picked = jnp.where(lane == offset, across(values, s), -1)
        return jnp.broadcast_to(jnp.max(picked, axis=1, keepdims=True), shape)

    def chain(values, row, last_row):
        columns = [down(values, s) for s in (0, 1)]
        last = jnp.zeros(shape, jnp.int32)
        for s in (0, 1):
            target = across(values, s)
            found = jnp.zeros(shape, jnp.int32)
            for t in (0, 1):
                earlier = 2 * offset + t < 2 * lane + s
                same = (columns[t] == target) & earlier & (target >= 0)
                found = jnp.maximum(found, jnp.where(same, 2 * offset + t + 1, 0))
            last = jnp.maximum(last, jnp.where(columns[s] == lane, 2 * offset + s + 1, 0))
            plan[row + s : row + s + 1, :OFFSETS] = jnp.max(found, axis=0, keepdims=True)
        plan[last_row : last_row + 1, :OFFSETS] = jnp.max(last, axis=0, keepdims=True)

    plan[...] = jnp.zeros_like(plan)
    source, target, live = in_ref[...], out_ref[...], live_ref[...]
    plan[IN : IN + 2, :OFFSETS] = source
    plan[DELTA : DELTA + 2, :OFFSETS] = jnp.where(live > 0, target, BLOCKS)
    chain(jnp.where(live > 0, target, -1), OUT_CHAIN, OUT_LAST)
    chain(jnp.where(live > 0, source, -1), IN_CHAIN, IN_LAST)


UNROLL = 27


def step_loop(count, body, unroll=None):
    unroll = unroll or UNROLL
    unroll = max(u for u in range(1, unroll + 1) if count % u == 0)

    @pl.loop(0, count // unroll)
    def _(step):
        for u in range(unroll):
            body(step * unroll + u)


def pair_of(table, plan, row, k):
    return [table[plan[row, k]], table[plan[row + 1, k]]]


def convolve(table, plan, row, chain, weight, sums, flipped):
    def body(k):
        product = lax.dot_general(
            jnp.concatenate(pair_of(table, plan, row, k), axis=0),
            weight[k],
            (((1,), (1 if flipped else 0,)), ((), ())),
            preferred_element_type=jnp.float32,
        )
        sums[2 * k + 1] = sums[plan[chain, k]] + product[:VOXELS]
        sums[2 * k + 2] = sums[plan[chain + 1, k]] + product[VOXELS:]

    step_loop(OFFSETS, body)


def weight_terms(tables, deltas, plans, part):
    core = place()[3]

    def body(j):
        k = jnp.minimum(core * HALF_OFFSETS + j, OFFSETS - 1)
        left, right = [], []
        for table, delta, plan in zip(tables, deltas, plans):
            left += pair_of(table, plan, IN, k)
            right += pair_of(delta, plan, DELTA, k)
        product = lax.dot_general(
            jnp.concatenate(left, axis=0),
            jnp.concatenate(right, axis=0),
            (((0,), (0,)), ((), ())),
            preferred_element_type=jnp.float32,
        )
        part[rows(j * 128, 128)] = product.astype(jnp.bfloat16)

    step_loop(HALF_OFFSETS, body, 14)


class Swap:
    def __init__(self, index, sems, sources, targets, blocks):
        self.sems, self.blocks = [sems.at[side, index] for side in (0, 1)], blocks
        for g, direction in enumerate(DIRECTIONS):
            pltpu.make_async_remote_copy(
                src_ref=sources[g],
                dst_ref=targets[7 - g],
                send_sem=self.sems[0],
                recv_sem=self.sems[1],
                device_id=neighbour(direction),
                device_id_type=MESH,
            ).start()

    def arrive(self):
        wait_bytes(self.blocks, self.sems[1])

    def finish(self):
        wait_bytes(self.blocks, self.sems[0])


def beyond(table):
    return table.at[pl.ds(BLOCKS, 8 * RIM)]


def rim_slots(table):
    return [table.at[pl.ds(BLOCKS + RIM * g, RIM)] for g in range(8)]


def clear_outside(table):
    for g, direction in enumerate(DIRECTIONS):

        @pl.when(jnp.logical_not(present(direction)))
        def _():
            table[BLOCKS + RIM * g : BLOCKS + RIM * (g + 1)] = jnp.zeros(
                (RIM, VOXELS, 128), jnp.bfloat16
            )


def routed(own, arrived, r):
    total = own
    for g, direction in enumerate(DIRECTIONS):
        total = total + jnp.where(present(direction), arrived[g, r].astype(jnp.float32), 0.0)
    return total


BLOCK_SET = (VOXELS, 128)
SCRATCH = [
    pltpu.VMEM((3, 2, OFFSETS), jnp.int32),
    pltpu.VMEM((OFFSETS, 128, 128), jnp.bfloat16),
    pltpu.VMEM((OFFSETS, 128, 128), jnp.bfloat16),
    pltpu.VMEM((BLOCKS,) + BLOCK_SET, jnp.bfloat16),
    pltpu.VMEM((16, 128), jnp.int32),
    pltpu.VMEM((16, 128), jnp.int32),
    pltpu.SMEM((16, 128), jnp.int32),
    pltpu.SMEM((16, 128), jnp.int32),
    pltpu.VMEM((TABLE,) + BLOCK_SET, jnp.bfloat16),
    pltpu.VMEM((TABLE,) + BLOCK_SET, jnp.bfloat16),
    pltpu.VMEM((TABLE,) + BLOCK_SET, jnp.bfloat16),
    pltpu.VMEM((TABLE,) + BLOCK_SET, jnp.bfloat16),
    pltpu.VMEM((2 * OFFSETS + 2,) + BLOCK_SET, jnp.float32),
    pltpu.VMEM((BLOCKS,) + BLOCK_SET, jnp.float32),
    pltpu.VMEM((BLOCKS + 1,) + BLOCK_SET, jnp.bfloat16),
    pltpu.VMEM((BLOCKS + 1,) + BLOCK_SET, jnp.bfloat16),
    pltpu.VMEM((BLOCKS + 1,) + BLOCK_SET, jnp.bfloat16),
    pltpu.VMEM((BLOCKS + 1,) + BLOCK_SET, jnp.bfloat16),
    pltpu.VMEM((8, RIM) + BLOCK_SET, jnp.bfloat16),
    pltpu.VMEM((8, RIM) + BLOCK_SET, jnp.bfloat16),
    pltpu.VMEM((8, RIM) + BLOCK_SET, jnp.bfloat16),
    pltpu.VMEM((8, RIM) + BLOCK_SET, jnp.bfloat16),
    pltpu.SemaphoreType.DMA((5,)),
    pltpu.SemaphoreType.DMA((7,)),
    pltpu.SemaphoreType.DMA((2, 4)),
    pltpu.SemaphoreType.REGULAR((3,)),
]


def block_kernel(
    scale,
    voxels_in,
    first_weight_in,
    second_weight_in,
    in_slots,
    out_slots,
    live_slots,
    out_grad_in,
    result,
    input_grad,
    first_grad,
    second_grad,
    *scratch,
):
    (
        slot_rows,
        first_weight,
        second_weight,
        out_grad,
        plan_rows,
        other_rows,
        plan,
        other_plan,
        table_x,
        table_h,
        other_x,
        other_h,
        sums,
        first_sum,
        first_delta,
        second_delta,
        other_first,
        other_second,
        give_h,
        got_h,
        give_x,
        got_x,
        load_sems,
        core_sems,
        swap_sems,
        reach,
    ) = scratch[: len(SCRATCH)]
    count = len(Reduce.scratch)
    reduces = scratch[len(SCRATCH) :]
    first = Reduce(first_grad, scale, *reduces[:count])
    second = Reduce(second_grad, scale, *reduces[count:])

    def load(index, src, dst):
        copy = pltpu.make_async_copy(src, dst, load_sems.at[index])
        copy.start()
        return copy

    def share(index, src, dst):
        copy = pltpu.make_async_remote_copy(
            src_ref=src,
            dst_ref=dst,
            send_sem=core_sems.at[6],
            recv_sem=core_sems.at[index],
            device_id=partner(),
            device_id_type=MESH,
        )
        copy.start()
        return copy

    own = table_x.at[pl.ds(0, BLOCKS)]
    load_x = load(0, voxels_in, own)
    for index, slots in enumerate((in_slots, out_slots, live_slots)):
        load(1, slots, slot_rows.at[index])
    load_first = load(2, first_weight_in, first_weight)
    load_second = load(3, second_weight_in, second_weight)
    load_grad = load(4, out_grad_in, out_grad)

    def signal_reach(step):
        for d in (1 << step, -(1 << step)):
            pl.semaphore_signal(reach.at[step], inc=1, device_id=ring(d), device_id_type=MESH)

    enter(
        [neighbour(direction) for direction in DIRECTIONS]
        + [in_plane(d) for d in PLANE]
        + [ring(1), ring(-1), partner()]
    )
    load_x.wait()
    rim_x = table_x.at[pl.ds(0, RIM)]
    swap_x = Swap(0, swap_sems, [rim_x] * 8, rim_slots(table_x), beyond(table_x))
    signal_reach(0)

    wait_bytes(slot_rows, load_sems.at[1])
    write_plan(slot_rows.at[0], slot_rows.at[1], slot_rows.at[2], plan_rows)
    load_plan = load(0, plan_rows, plan)
    share_plan = share(0, plan_rows, other_rows)
    zeros = jnp.zeros(BLOCK_SET, jnp.bfloat16)
    for delta in (first_delta, second_delta, other_first, other_second):
        delta[BLOCKS] = zeros
    sums[0] = jnp.zeros(BLOCK_SET, jnp.float32)
    load_plan.wait()
    share_plan.wait_recv()
    load_other = load(1, other_rows, other_plan)
    load_first.wait()

    swap_x.arrive()
    pl.semaphore_wait(reach.at[0], 2)
    signal_reach(1)
    clear_outside(table_x)
    share_plan.wait_send()
    share_x = share(1, table_x, other_x)
    convolve(table_x, plan, IN, OUT_CHAIN, first_weight, sums, False)

    def hide(block):
        total = sums[plan[OUT_LAST, block]]
        first_sum[block] = total
        table_h[block] = (total * sigmoid(total)).astype(jnp.bfloat16)

    for block in range(RIM):
        hide(block)
    rim_h = table_h.at[pl.ds(0, RIM)]
    swap_h = Swap(1, swap_sems, [rim_h] * 8, rim_slots(table_h), beyond(table_h))
    for block in range(RIM, BLOCKS):
        hide(block)
    swap_x.finish()

    load_other.wait()
    load_second.wait()
    load_grad.wait()
    swap_h.arrive()
    pl.semaphore_wait(reach.at[1], 2)
    signal_reach(2)
    clear_outside(table_h)
    share_x.wait_send()
    share_h = share(2, table_h, other_h)
    convolve(table_h, plan, IN, OUT_CHAIN, second_weight, sums, False)

    for block in range(BLOCKS):
        joined = sums[plan[OUT_LAST, block]] + table_x[block].astype(jnp.float32)
        gate = sigmoid(joined)
        result[block] = (joined * gate).astype(jnp.bfloat16)
        second_delta[block] = (
            out_grad[block].astype(jnp.float32) * (gate * (1.0 + joined * (1.0 - gate)))
        ).astype(jnp.bfloat16)

    def all_of(delta, first_block, last_block):
        return delta.at[pl.ds(first_block, last_block - first_block)]

    share_h.wait_send()
    share_second = share(
        3, all_of(second_delta, 0, BLOCKS), all_of(other_second, 0, BLOCKS)
    )

    def give(buffer):
        for g in range(8):
            for r in range(RIM):
                buffer[g, r] = sums[plan[IN_LAST, BLOCKS + RIM * g + r]].astype(jnp.bfloat16)

    def eight(buffer):
        return [buffer.at[g] for g in range(8)]

    convolve(second_delta, plan, DELTA, IN_CHAIN, second_weight, sums, True)
    give(give_h)
    back_h = Swap(2, swap_sems, eight(give_h), eight(got_h), got_h)

    def descend(block, total):
        first_delta[block] = (total * slope(first_sum[block])).astype(jnp.bfloat16)

    swap_h.finish()
    for block in range(RIM, BLOCKS):
        descend(block, sums[plan[IN_LAST, block]])

    share_second.wait_send()
    share_inner = share(
        4, all_of(first_delta, RIM, BLOCKS), all_of(other_first, RIM, BLOCKS)
    )
    share_h.wait_recv()
    share_second.wait_recv()
    weight_terms(
        (table_h, other_h), (second_delta, other_second), (plan, other_plan), second.part
    )
    second.start_plane()

    pl.semaphore_wait(reach.at[2], 2)
    back_h.arrive()
    for r in range(RIM):
        descend(r, routed(sums[plan[IN_LAST, r]], got_h, r))
    share_inner.wait_send()
    share_rim = share(5, all_of(first_delta, 0, RIM), all_of(other_first, 0, RIM))
    share_x.wait_recv()
    share_inner.wait_recv()
    share_rim.wait_recv()
    weight_terms((table_x, other_x), (first_delta, other_first), (plan, other_plan), first.part)
    first.start_plane()

    second.start_root()
    convolve(first_delta, plan, DELTA, IN_CHAIN, first_weight, sums, True)
    give(give_x)
    back_x = Swap(3, swap_sems, eight(give_x), eight(got_x), got_x)
    back_h.finish()

    def land(block, total):
        input_grad[block] = (total + second_delta[block].astype(jnp.float32)).astype(jnp.bfloat16)

    for block in range(RIM, BLOCKS):
        land(block, sums[plan[IN_LAST, block]])
    first.start_root()
    back_x.arrive()
    for r in range(RIM):
        land(r, routed(sums[plan[IN_LAST, r]], got_x, r))
    share_rim.wait_send()
    back_x.finish()
    second.start_spread()
    second.start_core()
    first.start_spread()
    second.finish()
    first.start_core()
    first.finish()


def place_kernel(*refs):
    sems = refs[-1]
    copies = []
    for index in range(4):
        copy = pltpu.make_async_copy(refs[index], refs[4 + index], sems.at[index])
        copy.start()
        copies.append(copy)
    for copy in copies:
        copy.wait()


def shards(voxels, first_weight, second_weight, in_slots, out_slots, live_slots, out_grad):
    tile = (BLOCKS,) + BLOCK_SET
    scale = 1.0 / math.sqrt(
        lax.axis_size("gx") * lax.axis_size("gy") * OFFSETS * in_slots.shape[3] * VOXELS
    )
    field = jax.ShapeDtypeStruct(tile, jnp.bfloat16)
    grad = jax.ShapeDtypeStruct((FULL, 128), jnp.bfloat16)
    vmem, hbm = (pl.BlockSpec(memory_space=space) for space in (pltpu.VMEM, pltpu.HBM))

    def slots(values):
        return values.reshape(values.shape[2:]).T

    def in_hbm(*values):
        return [pltpu.with_memory_space_constraint(value, pltpu.HBM) for value in values]

    outputs = pl.pallas_call(
        functools.partial(block_kernel, scale),
        out_shape=(field, field, grad, grad),
        in_specs=[hbm] * 7,
        out_specs=[vmem] * 4,
        scratch_shapes=SCRATCH + Reduce.scratch * 2,
        compiler_params=pltpu.CompilerParams(
            collective_id=0, has_side_effects=True, vmem_limit_bytes=48 * 1024 * 1024
        ),
        cost_estimate=pl.CostEstimate(
            flops=6 * 54 * VOXELS * 128 * 128 * 2,
            bytes_accessed=4 * FULL * 256,
            transcendentals=4 * BLOCKS * VOXELS * 128,
        ),
        name="block",
    )(
        *in_hbm(
            voxels.reshape(tile),
            first_weight,
            second_weight,
            slots(in_slots),
            slots(out_slots),
            slots(live_slots),
            out_grad.reshape(tile),
        )
    )
    whole = jax.ShapeDtypeStruct((ROWS, 128), jnp.bfloat16)
    result, input_grad, first_grad, second_grad = pl.pallas_call(
        lambda *refs: place_kernel(
            refs[0], refs[1], refs[2].at[pl.ds(0, ROWS)], refs[3].at[pl.ds(0, ROWS)], *refs[4:]
        ),
        out_shape=(field, field, whole, whole),
        in_specs=[vmem] * 4,
        out_specs=[hbm] * 4,
        scratch_shapes=[pltpu.SemaphoreType.DMA((4,))],
        compiler_params=pltpu.CompilerParams(vmem_limit_bytes=1024 * 1024),
        name="place",
    )(*outputs)
    return (
        result.reshape(voxels.shape),
        input_grad.reshape(voxels.shape),
        first_grad.reshape(first_weight.shape),
        second_grad.reshape(first_weight.shape),
    )


def solution(mesh):
    return jax.shard_map(
        shards,
        mesh=mesh,
        in_specs=(
            P("gx", "gy", None, None, None),
            P(),
            P(),
            P("gx", "gy", None, None),
            P("gx", "gy", None, None),
            P("gx", "gy", None, None),
            P("gx", "gy", None, None, None),
        ),
        out_specs=(P("gx", "gy", None, None, None), P("gx", "gy", None, None, None), P(), P()),
        check_vma=False,
    )
```

```python
import functools
import math

import jax
import jax.numpy as jnp
from jax import lax
from jax.experimental import pallas as pl
from jax.experimental.pallas import tpu as pltpu
from jax.sharding import PartitionSpec as P

RIM = 2
MESH = pl.DeviceIdType.MESH

ROWS = 27 * 128
HALF = 1792
FULL = 2 * HALF
HALF_OFFSETS = HALF // 128
PIECE = HALF // 16


def rows(start, size):
    return pl.ds(pl.multiple_of(start, 16), size)


def place():
    gx, gy = lax.axis_index("gx"), lax.axis_index("gy")
    core = lax.rem(gx, 2)
    x = lax.rem(gx // 2, 2) * 2 + gy // 4
    return gx // 4, x, lax.rem(gy, 4), core


def device(z, x, y, core):
    return ((z * 2 + x // 2) * 2 + core, lax.rem(x, 2) * 4 + y)


def partner():
    z, x, y, core = place()
    return device(z, x, y, 1 - core)


def hops(d):
    return min(d // 4, 4 - d // 4) + min(d % 4, 4 - d % 4)


PLANE = sorted(range(1, 16), key=lambda d: -hops(d))


def ring_of(d):
    return hops(d) - 1


def in_plane(d):
    z, x, y, core = place()
    return device(z, lax.rem(x + d // 4, 4), lax.rem(y + d % 4, 4), core)


def plane_index(d):
    _, x, y, _ = place()
    return lax.rem(x + d // 4, 4) * 4 + lax.rem(y + d % 4, 4)


def opposite(d):
    return (4 - d // 4) % 4 * 4 + (4 - d % 4) % 4


def ring(d):
    z, x, y, core = place()
    return device(lax.rem(z + d + 16, 16), x, y, core)


SPREAD = [1, 2, 3, 4, 15, 5, 14, 6, 13, 7, 12, 8, 11, 10, 9]


def wait_bytes(ref, sem):
    pltpu.make_async_copy(ref, ref, sem).wait()


class Reduce:
    scratch = [
        pltpu.VMEM((HALF, 128), jnp.bfloat16),
        pltpu.VMEM((15, PIECE, 128), jnp.bfloat16),
        pltpu.VMEM((PIECE, 128), jnp.bfloat16),
        pltpu.VMEM((15, PIECE, 128), jnp.bfloat16),
        pltpu.SemaphoreType.DMA((5,)),
        pltpu.SemaphoreType.DMA((8,)),
    ]

    def __init__(self, out, scale, *scratch):
        self.out, self.scale = out, scale
        (
            self.part,
            self.got_plane,
            self.plane_sum,
            self.got_root,
            self.send_sems,
            self.recv_sems,
        ) = scratch

    def send(self, src, dst, send_index, recv_index, device_id):
        pltpu.make_async_remote_copy(
            src_ref=src,
            dst_ref=dst,
            send_sem=self.send_sems.at[send_index],
            recv_sem=self.recv_sems.at[recv_index],
            device_id=device_id,
            device_id_type=MESH,
        ).start()

    def sent(self, index, count, size):
        wait_bytes(self.part.at[pl.ds(0, count * size)], self.send_sems.at[index])

    def start_plane(self):
        for d in PLANE:
            self.send(
                self.part.at[rows(plane_index(d) * PIECE, PIECE)],
                self.got_plane.at[d - 1],
                0,
                0,
                in_plane(d),
            )

    def start_root(self):
        wait_bytes(self.got_plane, self.recv_sems.at[0])
        total = self.part[rows(plane_index(0) * PIECE, PIECE)].astype(jnp.float32)
        for d in range(15):
            total = total + self.got_plane[d].astype(jnp.float32)
        self.plane_sum[...] = total.astype(jnp.bfloat16)
        z, x, y, core = place()

        @pl.when(z > 0)
        def _():
            self.send(self.plane_sum, self.got_root.at[z - 1], 1, 1, device(0, x, y, core))

        self.sent(0, 15, PIECE)

    def spot(self, d, core):
        return self.out.at[rows(core * HALF + plane_index(d) * PIECE, PIECE)]

    def start_spread(self):
        z, x, y, core = place()
        own = self.spot(0, core)

        def spread(planes):
            for plane in planes:
                self.send(own, own, 2, 2, device(plane, x, y, core))

        @pl.when(z == 0)
        def _():
            wait_bytes(self.got_root, self.recv_sems.at[1])
            total = self.plane_sum[...].astype(jnp.float32)
            for plane in range(15):
                total = total + self.got_root[plane].astype(jnp.float32)
            own[...] = (total * self.scale).astype(jnp.bfloat16)
            spread(SPREAD[:4])

        @pl.when(z > 0)
        def _():
            self.sent(1, 1, PIECE)
            wait_bytes(own, self.recv_sems.at[2])

        for d in PLANE:
            self.send(own, own, 3, 3 + ring_of(d), in_plane(d))
        self.send(own, own, 4, 7, partner())

        @pl.when(z == 0)
        def _():
            spread(SPREAD[4:])

    def start_core(self):
        core = place()[3]
        for index in range(4):
            group = [d for d in PLANE if ring_of(d) == index]
            wait_bytes(self.part.at[pl.ds(0, len(group) * PIECE)], self.recv_sems.at[3 + index])
            for d in group:
                piece = self.spot(opposite(d), core)
                self.send(piece, piece, 4, 7, partner())

        @pl.when(place()[0] == 0)
        def _():
            self.sent(2, 15, PIECE)

        self.sent(3, 15, PIECE)

    def finish(self):
        wait_bytes(self.part, self.recv_sems.at[7])
        self.sent(4, 16, PIECE)


def enter(peers):
    barrier = pltpu.get_barrier_semaphore()
    for peer in peers:
        pl.semaphore_signal(barrier, inc=1, device_id=peer, device_id_type=MESH)
    pl.semaphore_wait(barrier, len(peers))


BLOCKS, VOXELS, OFFSETS, SLOTS, TABLE = 8, 64, 27, 54, 24
DIRECTIONS = [(a, b) for a in (-1, 0, 1) for b in (-1, 0, 1) if (a, b) != (0, 0)]


def neighbour(direction):
    a, b = direction
    gx, gy = lax.axis_index("gx"), lax.axis_index("gy")
    return lax.rem(gx + a + 64, 64), lax.rem(gy + b + 8, 8)


def present(direction):
    a, b = direction
    gx, gy = lax.axis_index("gx") + a, lax.axis_index("gy") + b
    return (gx >= 0) & (gx < 64) & (gy >= 0) & (gy < 8)


def sigmoid(values):
    return 1.0 / (1.0 + jnp.exp(-values))


def slope(values):
    s = sigmoid(values)
    return s * (1.0 + values * (1.0 - s))


IN, DELTA, OUT_CHAIN, OUT_LAST, IN_CHAIN, IN_LAST = 0, 2, 4, 6, 8, 10


def write_plan(in_ref, out_ref, live_ref, plan):
    shape = (OFFSETS, OFFSETS)
    lane = lax.broadcasted_iota(jnp.int32, shape, 1)
    offset = lax.broadcasted_iota(jnp.int32, shape, 0)

    def across(values, s):
        return jnp.broadcast_to(values[s : s + 1], shape)

    def down(values, s):
        picked = jnp.where(lane == offset, across(values, s), -1)
        return jnp.broadcast_to(jnp.max(picked, axis=1, keepdims=True), shape)

    def chain(values, row, last_row):
        columns = [down(values, s) for s in (0, 1)]
        last = jnp.zeros(shape, jnp.int32)
        for s in (0, 1):
            target = across(values, s)
            found = jnp.zeros(shape, jnp.int32)
            for t in (0, 1):
                earlier = 2 * offset + t < 2 * lane + s
                same = (columns[t] == target) & earlier & (target >= 0)
                found = jnp.maximum(found, jnp.where(same, 2 * offset + t + 1, 0))
            last = jnp.maximum(last, jnp.where(columns[s] == lane, 2 * offset + s + 1, 0))
            plan[row + s : row + s + 1, :OFFSETS] = jnp.max(found, axis=0, keepdims=True)
        plan[last_row : last_row + 1, :OFFSETS] = jnp.max(last, axis=0, keepdims=True)

    plan[...] = jnp.zeros_like(plan)
    source, target, live = in_ref[...], out_ref[...], live_ref[...]
    plan[IN : IN + 2, :OFFSETS] = source
    plan[DELTA : DELTA + 2, :OFFSETS] = jnp.where(live > 0, target, BLOCKS)
    chain(jnp.where(live > 0, target, -1), OUT_CHAIN, OUT_LAST)
    chain(jnp.where(live > 0, source, -1), IN_CHAIN, IN_LAST)


UNROLL = 27


def step_loop(count, body, unroll=None):
    unroll = unroll or UNROLL
    unroll = max(u for u in range(1, unroll + 1) if count % u == 0)

    @pl.loop(0, count // unroll)
    def _(step):
        for u in range(unroll):
            body(step * unroll + u)


def pair_of(table, plan, row, k):
    return [table[plan[row, k]], table[plan[row + 1, k]]]


def convolve(table, plan, row, chain, weight, sums, flipped):
    def body(k):
        product = lax.dot_general(
            jnp.concatenate(pair_of(table, plan, row, k), axis=0),
            weight[k],
            (((1,), (1 if flipped else 0,)), ((), ())),
            preferred_element_type=jnp.float32,
        )
        sums[2 * k + 1] = sums[plan[chain, k]] + product[:VOXELS]
        sums[2 * k + 2] = sums[plan[chain + 1, k]] + product[VOXELS:]

    step_loop(OFFSETS, body)


def weight_terms(tables, deltas, plans, part):
    core = place()[3]

    def body(j):
        k = jnp.minimum(core * HALF_OFFSETS + j, OFFSETS - 1)
        left, right = [], []
        for table, delta, plan in zip(tables, deltas, plans):
            left += pair_of(table, plan, IN, k)
            right += pair_of(delta, plan, DELTA, k)
        product = lax.dot_general(
            jnp.concatenate(left, axis=0),
            jnp.concatenate(right, axis=0),
            (((0,), (0,)), ((), ())),
            preferred_element_type=jnp.float32,
        )
        part[rows(j * 128, 128)] = product.astype(jnp.bfloat16)

    step_loop(HALF_OFFSETS, body, 14)


class Swap:
    def __init__(self, index, sems, sources, targets, blocks):
        self.sems, self.blocks = [sems.at[side, index] for side in (0, 1)], blocks
        for g, direction in enumerate(DIRECTIONS):
            pltpu.make_async_remote_copy(
                src_ref=sources[g],
                dst_ref=targets[7 - g],
                send_sem=self.sems[0],
                recv_sem=self.sems[1],
                device_id=neighbour(direction),
                device_id_type=MESH,
            ).start()

    def arrive(self):
        wait_bytes(self.blocks, self.sems[1])

    def finish(self):
        wait_bytes(self.blocks, self.sems[0])


def beyond(table):
    return table.at[pl.ds(BLOCKS, 8 * RIM)]


def rim_slots(table):
    return [table.at[pl.ds(BLOCKS + RIM * g, RIM)] for g in range(8)]


def clear_outside(table):
    for g, direction in enumerate(DIRECTIONS):

        @pl.when(jnp.logical_not(present(direction)))
        def _():
            table[BLOCKS + RIM * g : BLOCKS + RIM * (g + 1)] = jnp.zeros(
                (RIM, VOXELS, 128), jnp.bfloat16
            )


def routed(own, arrived, r):
    total = own
    for g, direction in enumerate(DIRECTIONS):
        total = total + jnp.where(present(direction), arrived[g, r].astype(jnp.float32), 0.0)
    return total


BLOCK_SET = (VOXELS, 128)
SCRATCH = [
    pltpu.VMEM((3, 2, OFFSETS), jnp.int32),
    pltpu.VMEM((OFFSETS, 128, 128), jnp.bfloat16),
    pltpu.VMEM((OFFSETS, 128, 128), jnp.bfloat16),
    pltpu.VMEM((BLOCKS,) + BLOCK_SET, jnp.bfloat16),
    pltpu.VMEM((16, 128), jnp.int32),
    pltpu.VMEM((16, 128), jnp.int32),
    pltpu.SMEM((16, 128), jnp.int32),
    pltpu.SMEM((16, 128), jnp.int32),
    pltpu.VMEM((TABLE,) + BLOCK_SET, jnp.bfloat16),
    pltpu.VMEM((TABLE,) + BLOCK_SET, jnp.bfloat16),
    pltpu.VMEM((TABLE,) + BLOCK_SET, jnp.bfloat16),
    pltpu.VMEM((TABLE,) + BLOCK_SET, jnp.bfloat16),
    pltpu.VMEM((2 * OFFSETS + 2,) + BLOCK_SET, jnp.float32),
    pltpu.VMEM((BLOCKS,) + BLOCK_SET, jnp.float32),
    pltpu.VMEM((BLOCKS + 1,) + BLOCK_SET, jnp.bfloat16),
    pltpu.VMEM((BLOCKS + 1,) + BLOCK_SET, jnp.bfloat16),
    pltpu.VMEM((BLOCKS + 1,) + BLOCK_SET, jnp.bfloat16),
    pltpu.VMEM((BLOCKS + 1,) + BLOCK_SET, jnp.bfloat16),
    pltpu.VMEM((8, RIM) + BLOCK_SET, jnp.bfloat16),
    pltpu.VMEM((8, RIM) + BLOCK_SET, jnp.bfloat16),
    pltpu.VMEM((8, RIM) + BLOCK_SET, jnp.bfloat16),
    pltpu.VMEM((8, RIM) + BLOCK_SET, jnp.bfloat16),
    pltpu.SemaphoreType.DMA((5,)),
    pltpu.SemaphoreType.DMA((7,)),
    pltpu.SemaphoreType.DMA((2, 4)),
    pltpu.SemaphoreType.REGULAR((3,)),
]


def block_kernel(
    scale,
    voxels_in,
    first_weight_in,
    second_weight_in,
    in_slots,
    out_slots,
    live_slots,
    out_grad_in,
    result,
    input_grad,
    first_grad,
    second_grad,
    *scratch,
):
    (
        slot_rows,
        first_weight,
        second_weight,
        out_grad,
        plan_rows,
        other_rows,
        plan,
        other_plan,
        table_x,
        table_h,
        other_x,
        other_h,
        sums,
        first_sum,
        first_delta,
        second_delta,
        other_first,
        other_second,
        give_h,
        got_h,
        give_x,
        got_x,
        load_sems,
        core_sems,
        swap_sems,
        reach,
    ) = scratch[: len(SCRATCH)]
    count = len(Reduce.scratch)
    reduces = scratch[len(SCRATCH) :]
    first = Reduce(first_grad, scale, *reduces[:count])
    second = Reduce(second_grad, scale, *reduces[count:])

    def load(index, src, dst):
        copy = pltpu.make_async_copy(src, dst, load_sems.at[index])
        copy.start()
        return copy

    def share(index, src, dst):
        copy = pltpu.make_async_remote_copy(
            src_ref=src,
            dst_ref=dst,
            send_sem=core_sems.at[6],
            recv_sem=core_sems.at[index],
            device_id=partner(),
            device_id_type=MESH,
        )
        copy.start()
        return copy

    own = table_x.at[pl.ds(0, BLOCKS)]
    load_x = load(0, voxels_in, own)
    for index, slots in enumerate((in_slots, out_slots, live_slots)):
        load(1, slots, slot_rows.at[index])
    load_first = load(2, first_weight_in, first_weight)
    load_second = load(3, second_weight_in, second_weight)
    load_grad = load(4, out_grad_in, out_grad)

    def signal_reach(step):
        for d in (1 << step, -(1 << step)):
            pl.semaphore_signal(reach.at[step], inc=1, device_id=ring(d), device_id_type=MESH)

    enter(
        [neighbour(direction) for direction in DIRECTIONS]
        + [in_plane(d) for d in PLANE]
        + [ring(1), ring(-1), partner()]
    )
    load_x.wait()
    rim_x = table_x.at[pl.ds(0, RIM)]
    swap_x = Swap(0, swap_sems, [rim_x] * 8, rim_slots(table_x), beyond(table_x))
    signal_reach(0)

    wait_bytes(slot_rows, load_sems.at[1])
    write_plan(slot_rows.at[0], slot_rows.at[1], slot_rows.at[2], plan_rows)
    load_plan = load(0, plan_rows, plan)
    share_plan = share(0, plan_rows, other_rows)
    zeros = jnp.zeros(BLOCK_SET, jnp.bfloat16)
    for delta in (first_delta, second_delta, other_first, other_second):
        delta[BLOCKS] = zeros
    sums[0] = jnp.zeros(BLOCK_SET, jnp.float32)
    load_plan.wait()
    share_plan.wait_recv()
    load_other = load(1, other_rows, other_plan)
    load_first.wait()

    swap_x.arrive()
    pl.semaphore_wait(reach.at[0], 2)
    signal_reach(1)
    clear_outside(table_x)
    convolve(table_x, plan, IN, OUT_CHAIN, first_weight, sums, False)

    def hide(block):
        total = sums[plan[OUT_LAST, block]]
        first_sum[block] = total
        table_h[block] = (total * sigmoid(total)).astype(jnp.bfloat16)

    for block in range(RIM):
        hide(block)
    rim_h = table_h.at[pl.ds(0, RIM)]
    swap_h = Swap(1, swap_sems, [rim_h] * 8, rim_slots(table_h), beyond(table_h))
    for block in range(RIM, BLOCKS):
        hide(block)
    share_plan.wait_send()
    share_x = share(1, table_x, other_x)
    swap_x.finish()

    load_other.wait()
    load_second.wait()
    load_grad.wait()
    swap_h.arrive()
    pl.semaphore_wait(reach.at[1], 2)
    signal_reach(2)
    clear_outside(table_h)
    share_x.wait_send()
    share_h = share(2, table_h, other_h)
    convolve(table_h, plan, IN, OUT_CHAIN, second_weight, sums, False)

    for block in range(BLOCKS):
        joined = sums[plan[OUT_LAST, block]] + table_x[block].astype(jnp.float32)
        gate = sigmoid(joined)
        result[block] = (joined * gate).astype(jnp.bfloat16)
        second_delta[block] = (
            out_grad[block].astype(jnp.float32) * (gate * (1.0 + joined * (1.0 - gate)))
        ).astype(jnp.bfloat16)

    def all_of(delta, first_block, last_block):
        return delta.at[pl.ds(first_block, last_block - first_block)]

    share_h.wait_send()
    share_second = share(
        3, all_of(second_delta, 0, BLOCKS), all_of(other_second, 0, BLOCKS)
    )

    def give(buffer):
        for g in range(8):
            for r in range(RIM):
                buffer[g, r] = sums[plan[IN_LAST, BLOCKS + RIM * g + r]].astype(jnp.bfloat16)

    def eight(buffer):
        return [buffer.at[g] for g in range(8)]

    convolve(second_delta, plan, DELTA, IN_CHAIN, second_weight, sums, True)
    give(give_h)
    back_h = Swap(2, swap_sems, eight(give_h), eight(got_h), got_h)

    def descend(block, total):
        first_delta[block] = (total * slope(first_sum[block])).astype(jnp.bfloat16)

    swap_h.finish()
    for block in range(RIM, BLOCKS):
        descend(block, sums[plan[IN_LAST, block]])

    share_second.wait_send()
    share_inner = share(
        4, all_of(first_delta, RIM, BLOCKS), all_of(other_first, RIM, BLOCKS)
    )
    share_h.wait_recv()
    share_second.wait_recv()
    weight_terms(
        (table_h, other_h), (second_delta, other_second), (plan, other_plan), second.part
    )
    second.start_plane()

    pl.semaphore_wait(reach.at[2], 2)
    back_h.arrive()
    for r in range(RIM):
        descend(r, routed(sums[plan[IN_LAST, r]], got_h, r))
    share_inner.wait_send()
    share_rim = share(5, all_of(first_delta, 0, RIM), all_of(other_first, 0, RIM))
    share_x.wait_recv()
    share_inner.wait_recv()
    share_rim.wait_recv()
    weight_terms((table_x, other_x), (first_delta, other_first), (plan, other_plan), first.part)
    first.start_plane()

    second.start_root()
    back_h.finish()

    def land(block, total):
        input_grad[block] = (total + second_delta[block].astype(jnp.float32)).astype(jnp.bfloat16)

    first.start_root()
    convolve(first_delta, plan, DELTA, IN_CHAIN, first_weight, sums, True)
    give(give_x)
    back_x = Swap(3, swap_sems, eight(give_x), eight(got_x), got_x)
    for block in range(RIM, BLOCKS):
        land(block, sums[plan[IN_LAST, block]])
    second.start_spread()
    back_x.arrive()
    for r in range(RIM):
        land(r, routed(sums[plan[IN_LAST, r]], got_x, r))
    share_rim.wait_send()
    back_x.finish()
    first.start_spread()
    second.start_core()
    second.finish()
    first.start_core()
    first.finish()


def place_kernel(*refs):
    sems = refs[-1]
    copies = []
    for index in range(4):
        copy = pltpu.make_async_copy(refs[index], refs[4 + index], sems.at[index])
        copy.start()
        copies.append(copy)
    for copy in copies:
        copy.wait()


def shards(voxels, first_weight, second_weight, in_slots, out_slots, live_slots, out_grad):
    tile = (BLOCKS,) + BLOCK_SET
    scale = 1.0 / math.sqrt(
        lax.axis_size("gx") * lax.axis_size("gy") * OFFSETS * in_slots.shape[3] * VOXELS
    )
    field = jax.ShapeDtypeStruct(tile, jnp.bfloat16)
    grad = jax.ShapeDtypeStruct((FULL, 128), jnp.bfloat16)
    vmem, hbm = (pl.BlockSpec(memory_space=space) for space in (pltpu.VMEM, pltpu.HBM))

    def slots(values):
        return values.reshape(values.shape[2:]).T

    def in_hbm(*values):
        return [pltpu.with_memory_space_constraint(value, pltpu.HBM) for value in values]

    outputs = pl.pallas_call(
        functools.partial(block_kernel, scale),
        out_shape=(field, field, grad, grad),
        in_specs=[hbm] * 7,
        out_specs=[vmem] * 4,
        scratch_shapes=SCRATCH + Reduce.scratch * 2,
        compiler_params=pltpu.CompilerParams(
            collective_id=0, has_side_effects=True, vmem_limit_bytes=48 * 1024 * 1024
        ),
        cost_estimate=pl.CostEstimate(
            flops=6 * 54 * VOXELS * 128 * 128 * 2,
            bytes_accessed=4 * FULL * 256,
            transcendentals=4 * BLOCKS * VOXELS * 128,
        ),
        name="block",
    )(
        *in_hbm(
            voxels.reshape(tile),
            first_weight,
            second_weight,
            slots(in_slots),
            slots(out_slots),
            slots(live_slots),
            out_grad.reshape(tile),
        )
    )
    whole = jax.ShapeDtypeStruct((ROWS, 128), jnp.bfloat16)
    result, input_grad, first_grad, second_grad = pl.pallas_call(
        lambda *refs: place_kernel(
            refs[0], refs[1], refs[2].at[pl.ds(0, ROWS)], refs[3].at[pl.ds(0, ROWS)], *refs[4:]
        ),
        out_shape=(field, field, whole, whole),
        in_specs=[vmem] * 4,
        out_specs=[hbm] * 4,
        scratch_shapes=[pltpu.SemaphoreType.DMA((4,))],
        compiler_params=pltpu.CompilerParams(vmem_limit_bytes=1024 * 1024),
        name="place",
    )(*outputs)
    return (
        result.reshape(voxels.shape),
        input_grad.reshape(voxels.shape),
        first_grad.reshape(first_weight.shape),
        second_grad.reshape(first_weight.shape),
    )


def solution(mesh):
    return jax.shard_map(
        shards,
        mesh=mesh,
        in_specs=(
            P("gx", "gy", None, None, None),
            P(),
            P(),
            P("gx", "gy", None, None),
            P("gx", "gy", None, None),
            P("gx", "gy", None, None),
            P("gx", "gy", None, None, None),
        ),
        out_specs=(P("gx", "gy", None, None, None), P("gx", "gy", None, None, None), P(), P()),
        check_vma=False,
    )
```

```python
import functools
import math

import jax
import jax.numpy as jnp
from jax import lax
from jax.experimental import pallas as pl
from jax.experimental.pallas import tpu as pltpu
from jax.sharding import PartitionSpec as P

RIM = 2
MESH = pl.DeviceIdType.MESH

ROWS = 27 * 128
HALF = 1792
FULL = 2 * HALF
HALF_OFFSETS = HALF // 128
PIECE = HALF // 16


def rows(start, size):
    return pl.ds(pl.multiple_of(start, 16), size)


def place():
    gx, gy = lax.axis_index("gx"), lax.axis_index("gy")
    core = lax.rem(gx, 2)
    x = lax.rem(gx // 2, 2) * 2 + gy // 4
    return gx // 4, x, lax.rem(gy, 4), core


def device(z, x, y, core):
    return ((z * 2 + x // 2) * 2 + core, lax.rem(x, 2) * 4 + y)


def partner():
    z, x, y, core = place()
    return device(z, x, y, 1 - core)


def hops(d):
    return min(d // 4, 4 - d // 4) + min(d % 4, 4 - d % 4)


PLANE = sorted(range(1, 16), key=lambda d: -hops(d))


def ring_of(d):
    return hops(d) - 1


def in_plane(d):
    z, x, y, core = place()
    return device(z, lax.rem(x + d // 4, 4), lax.rem(y + d % 4, 4), core)


def plane_index(d):
    _, x, y, _ = place()
    return lax.rem(x + d // 4, 4) * 4 + lax.rem(y + d % 4, 4)


def opposite(d):
    return (4 - d // 4) % 4 * 4 + (4 - d % 4) % 4


def ring(d):
    z, x, y, core = place()
    return device(lax.rem(z + d + 16, 16), x, y, core)


SPREAD = [1, 2, 3, 4, 15, 5, 14, 6, 13, 7, 12, 8, 11, 10, 9]


def wait_bytes(ref, sem):
    pltpu.make_async_copy(ref, ref, sem).wait()


class Reduce:
    scratch = [
        pltpu.VMEM((HALF, 128), jnp.bfloat16),
        pltpu.VMEM((15, PIECE, 128), jnp.bfloat16),
        pltpu.VMEM((PIECE, 128), jnp.bfloat16),
        pltpu.VMEM((15, PIECE, 128), jnp.bfloat16),
        pltpu.SemaphoreType.DMA((5,)),
        pltpu.SemaphoreType.DMA((8,)),
    ]

    def __init__(self, out, scale, *scratch):
        self.out, self.scale = out, scale
        (
            self.part,
            self.got_plane,
            self.plane_sum,
            self.got_root,
            self.send_sems,
            self.recv_sems,
        ) = scratch

    def send(self, src, dst, send_index, recv_index, device_id):
        pltpu.make_async_remote_copy(
            src_ref=src,
            dst_ref=dst,
            send_sem=self.send_sems.at[send_index],
            recv_sem=self.recv_sems.at[recv_index],
            device_id=device_id,
            device_id_type=MESH,
        ).start()

    def sent(self, index, count, size):
        wait_bytes(self.part.at[pl.ds(0, count * size)], self.send_sems.at[index])

    def start_plane(self):
        for d in PLANE:
            self.send(
                self.part.at[rows(plane_index(d) * PIECE, PIECE)],
                self.got_plane.at[d - 1],
                0,
                0,
                in_plane(d),
            )

    def start_root(self):
        wait_bytes(self.got_plane, self.recv_sems.at[0])
        total = self.part[rows(plane_index(0) * PIECE, PIECE)].astype(jnp.float32)
        for d in range(15):
            total = total + self.got_plane[d].astype(jnp.float32)
        self.plane_sum[...] = total.astype(jnp.bfloat16)
        z, x, y, core = place()

        @pl.when(z > 0)
        def _():
            self.send(self.plane_sum, self.got_root.at[z - 1], 1, 1, device(0, x, y, core))

        self.sent(0, 15, PIECE)

    def spot(self, d, core):
        return self.out.at[rows(core * HALF + plane_index(d) * PIECE, PIECE)]

    def start_spread(self):
        z, x, y, core = place()
        own = self.spot(0, core)

        def spread(planes):
            for plane in planes:
                self.send(own, own, 2, 2, device(plane, x, y, core))

        @pl.when(z == 0)
        def _():
            wait_bytes(self.got_root, self.recv_sems.at[1])
            total = self.plane_sum[...].astype(jnp.float32)
            for plane in range(15):
                total = total + self.got_root[plane].astype(jnp.float32)
            own[...] = (total * self.scale).astype(jnp.bfloat16)
            spread(SPREAD[:4])

        @pl.when(z > 0)
        def _():
            self.sent(1, 1, PIECE)
            wait_bytes(own, self.recv_sems.at[2])

        for d in PLANE:
            self.send(own, own, 3, 3 + ring_of(d), in_plane(d))
        self.send(own, own, 4, 7, partner())

        @pl.when(z == 0)
        def _():
            spread(SPREAD[4:])

    def start_core(self):
        core = place()[3]
        for index in range(4):
            group = [d for d in PLANE if ring_of(d) == index]
            wait_bytes(self.part.at[pl.ds(0, len(group) * PIECE)], self.recv_sems.at[3 + index])
            for d in group:
                piece = self.spot(opposite(d), core)
                self.send(piece, piece, 4, 7, partner())

        @pl.when(place()[0] == 0)
        def _():
            self.sent(2, 15, PIECE)

        self.sent(3, 15, PIECE)

    def finish(self):
        wait_bytes(self.part, self.recv_sems.at[7])
        self.sent(4, 16, PIECE)


def greet(peers):
    barrier = pltpu.get_barrier_semaphore()
    for peer in peers:
        pl.semaphore_signal(barrier, inc=1, device_id=peer, device_id_type=MESH)
    return lambda: pl.semaphore_wait(barrier, len(peers))


BLOCKS, VOXELS, OFFSETS, SLOTS, TABLE = 8, 64, 27, 54, 24
DIRECTIONS = [(a, b) for a in (-1, 0, 1) for b in (-1, 0, 1) if (a, b) != (0, 0)]


def neighbour(direction):
    a, b = direction
    gx, gy = lax.axis_index("gx"), lax.axis_index("gy")
    return lax.rem(gx + a + 64, 64), lax.rem(gy + b + 8, 8)


def present(direction):
    a, b = direction
    gx, gy = lax.axis_index("gx") + a, lax.axis_index("gy") + b
    return (gx >= 0) & (gx < 64) & (gy >= 0) & (gy < 8)


def sigmoid(values):
    return 1.0 / (1.0 + jnp.exp(-values))


def slope(values):
    s = sigmoid(values)
    return s * (1.0 + values * (1.0 - s))


IN, DELTA, OUT_CHAIN, OUT_LAST, IN_CHAIN, IN_LAST = 0, 2, 4, 6, 8, 10


def write_plan(in_ref, out_ref, live_ref, plan):
    shape = (OFFSETS, OFFSETS)
    lane = lax.broadcasted_iota(jnp.int32, shape, 1)
    offset = lax.broadcasted_iota(jnp.int32, shape, 0)

    def across(values, s):
        return jnp.broadcast_to(values[s : s + 1], shape)

    def down(values, s):
        picked = jnp.where(lane == offset, across(values, s), -1)
        return jnp.broadcast_to(jnp.max(picked, axis=1, keepdims=True), shape)

    def chain(values, row, last_row):
        columns = [down(values, s) for s in (0, 1)]
        last = jnp.zeros(shape, jnp.int32)
        for s in (0, 1):
            target = across(values, s)
            found = jnp.zeros(shape, jnp.int32)
            for t in (0, 1):
                earlier = 2 * offset + t < 2 * lane + s
                same = (columns[t] == target) & earlier & (target >= 0)
                found = jnp.maximum(found, jnp.where(same, 2 * offset + t + 1, 0))
            last = jnp.maximum(last, jnp.where(columns[s] == lane, 2 * offset + s + 1, 0))
            plan[row + s : row + s + 1, :OFFSETS] = jnp.max(found, axis=0, keepdims=True)
        plan[last_row : last_row + 1, :OFFSETS] = jnp.max(last, axis=0, keepdims=True)

    plan[...] = jnp.zeros_like(plan)
    source, target, live = in_ref[...], out_ref[...], live_ref[...]
    plan[IN : IN + 2, :OFFSETS] = source
    plan[DELTA : DELTA + 2, :OFFSETS] = jnp.where(live > 0, target, BLOCKS)
    chain(jnp.where(live > 0, target, -1), OUT_CHAIN, OUT_LAST)
    chain(jnp.where(live > 0, source, -1), IN_CHAIN, IN_LAST)


UNROLL = 27


def step_loop(count, body, unroll=None):
    unroll = unroll or UNROLL
    unroll = max(u for u in range(1, unroll + 1) if count % u == 0)

    @pl.loop(0, count // unroll)
    def _(step):
        for u in range(unroll):
            body(step * unroll + u)


def pair_of(table, plan, row, k):
    return [table[plan[row, k]], table[plan[row + 1, k]]]


def convolve(table, plan, row, chain, weight, sums, flipped):
    def body(k):
        product = lax.dot_general(
            jnp.concatenate(pair_of(table, plan, row, k), axis=0),
            weight[k],
            (((1,), (1 if flipped else 0,)), ((), ())),
            preferred_element_type=jnp.float32,
        )
        sums[2 * k + 1] = sums[plan[chain, k]] + product[:VOXELS]
        sums[2 * k + 2] = sums[plan[chain + 1, k]] + product[VOXELS:]

    step_loop(OFFSETS, body)


def weight_terms(tables, deltas, plans, part):
    core = place()[3]

    def body(j):
        k = jnp.minimum(core * HALF_OFFSETS + j, OFFSETS - 1)
        left, right = [], []
        for table, delta, plan in zip(tables, deltas, plans):
            left += pair_of(table, plan, IN, k)
            right += pair_of(delta, plan, DELTA, k)
        product = lax.dot_general(
            jnp.concatenate(left, axis=0),
            jnp.concatenate(right, axis=0),
            (((0,), (0,)), ((), ())),
            preferred_element_type=jnp.float32,
        )
        part[rows(j * 128, 128)] = product.astype(jnp.bfloat16)

    step_loop(HALF_OFFSETS, body, 14)


class Swap:
    def __init__(self, index, sems, sources, targets, blocks):
        self.sems, self.blocks = [sems.at[side, index] for side in (0, 1)], blocks
        outer = 2 * place()[3] - 1
        for side in (1, 0, -1):
            for b in (-1, 1, 0):
                if (side, b) == (0, 0):
                    continue
                a = side * outer
                cell = 3 * (a + 1) + b + 1
                g = cell - jnp.where(cell > 4, 1, 0)
                pltpu.make_async_remote_copy(
                    src_ref=sources(g),
                    dst_ref=targets(7 - g),
                    send_sem=self.sems[0],
                    recv_sem=self.sems[1],
                    device_id=neighbour((a, b)),
                    device_id_type=MESH,
                ).start()

    def arrive(self):
        wait_bytes(self.blocks, self.sems[1])

    def finish(self):
        wait_bytes(self.blocks, self.sems[0])


def beyond(table):
    return table.at[pl.ds(BLOCKS, 8 * RIM)]


def rim_slots(table):
    return lambda g: table.at[pl.ds(BLOCKS + RIM * g, RIM)]


def clear_outside(table):
    for g, direction in enumerate(DIRECTIONS):

        @pl.when(jnp.logical_not(present(direction)))
        def _():
            table[BLOCKS + RIM * g : BLOCKS + RIM * (g + 1)] = jnp.zeros(
                (RIM, VOXELS, 128), jnp.bfloat16
            )


def routed(own, arrived, r):
    total = own
    for g, direction in enumerate(DIRECTIONS):
        total = total + jnp.where(present(direction), arrived[g, r].astype(jnp.float32), 0.0)
    return total


BLOCK_SET = (VOXELS, 128)
SCRATCH = [
    pltpu.VMEM((3, 2, OFFSETS), jnp.int32),
    pltpu.VMEM((OFFSETS, 128, 128), jnp.bfloat16),
    pltpu.VMEM((OFFSETS, 128, 128), jnp.bfloat16),
    pltpu.VMEM((BLOCKS,) + BLOCK_SET, jnp.bfloat16),
    pltpu.VMEM((16, 128), jnp.int32),
    pltpu.VMEM((16, 128), jnp.int32),
    pltpu.SMEM((16, 128), jnp.int32),
    pltpu.SMEM((16, 128), jnp.int32),
    pltpu.VMEM((TABLE,) + BLOCK_SET, jnp.bfloat16),
    pltpu.VMEM((TABLE,) + BLOCK_SET, jnp.bfloat16),
    pltpu.VMEM((TABLE,) + BLOCK_SET, jnp.bfloat16),
    pltpu.VMEM((TABLE,) + BLOCK_SET, jnp.bfloat16),
    pltpu.VMEM((2 * OFFSETS + 2,) + BLOCK_SET, jnp.float32),
    pltpu.VMEM((BLOCKS,) + BLOCK_SET, jnp.float32),
    pltpu.VMEM((BLOCKS + 1,) + BLOCK_SET, jnp.bfloat16),
    pltpu.VMEM((BLOCKS + 1,) + BLOCK_SET, jnp.bfloat16),
    pltpu.VMEM((BLOCKS + 1,) + BLOCK_SET, jnp.bfloat16),
    pltpu.VMEM((BLOCKS + 1,) + BLOCK_SET, jnp.bfloat16),
    pltpu.VMEM((8, RIM) + BLOCK_SET, jnp.bfloat16),
    pltpu.VMEM((8, RIM) + BLOCK_SET, jnp.bfloat16),
    pltpu.VMEM((8, RIM) + BLOCK_SET, jnp.bfloat16),
    pltpu.VMEM((8, RIM) + BLOCK_SET, jnp.bfloat16),
    pltpu.SemaphoreType.DMA((5,)),
    pltpu.SemaphoreType.DMA((7,)),
    pltpu.SemaphoreType.DMA((2, 4)),
    pltpu.SemaphoreType.REGULAR((3,)),
]


def block_kernel(
    scale,
    voxels_in,
    first_weight_in,
    second_weight_in,
    in_slots,
    out_slots,
    live_slots,
    out_grad_in,
    result,
    input_grad,
    first_grad,
    second_grad,
    *scratch,
):
    (
        slot_rows,
        first_weight,
        second_weight,
        out_grad,
        plan_rows,
        other_rows,
        plan,
        other_plan,
        table_x,
        table_h,
        other_x,
        other_h,
        sums,
        first_sum,
        first_delta,
        second_delta,
        other_first,
        other_second,
        give_h,
        got_h,
        give_x,
        got_x,
        load_sems,
        core_sems,
        swap_sems,
        reach,
    ) = scratch[: len(SCRATCH)]
    count = len(Reduce.scratch)
    reduces = scratch[len(SCRATCH) :]
    first = Reduce(first_grad, scale, *reduces[:count])
    second = Reduce(second_grad, scale, *reduces[count:])

    def load(index, src, dst):
        copy = pltpu.make_async_copy(src, dst, load_sems.at[index])
        copy.start()
        return copy

    def share(index, src, dst):
        copy = pltpu.make_async_remote_copy(
            src_ref=src,
            dst_ref=dst,
            send_sem=core_sems.at[6],
            recv_sem=core_sems.at[index],
            device_id=partner(),
            device_id_type=MESH,
        )
        copy.start()
        return copy

    enter = greet(
        [neighbour(direction) for direction in DIRECTIONS]
        + [in_plane(d) for d in PLANE]
        + [ring(1), ring(-1), partner()]
    )
    own = table_x.at[pl.ds(0, BLOCKS)]
    load_x = load(0, voxels_in, own)
    for index, slots in enumerate((in_slots, out_slots, live_slots)):
        load(1, slots, slot_rows.at[index])
    load_first = load(2, first_weight_in, first_weight)
    load_second = load(3, second_weight_in, second_weight)
    load_grad = load(4, out_grad_in, out_grad)

    def signal_reach(step):
        for d in (1 << step, -(1 << step)):
            pl.semaphore_signal(reach.at[step], inc=1, device_id=ring(d), device_id_type=MESH)

    enter()
    load_x.wait()
    rim_x = table_x.at[pl.ds(0, RIM)]
    swap_x = Swap(0, swap_sems, lambda g: rim_x, rim_slots(table_x), beyond(table_x))
    signal_reach(0)

    wait_bytes(slot_rows, load_sems.at[1])
    write_plan(slot_rows.at[0], slot_rows.at[1], slot_rows.at[2], plan_rows)
    load_plan = load(0, plan_rows, plan)
    share_plan = share(0, plan_rows, other_rows)
    zeros = jnp.zeros(BLOCK_SET, jnp.bfloat16)
    for delta in (first_delta, second_delta, other_first, other_second):
        delta[BLOCKS] = zeros
    sums[0] = jnp.zeros(BLOCK_SET, jnp.float32)
    load_plan.wait()
    share_plan.wait_recv()
    load_other = load(1, other_rows, other_plan)
    load_first.wait()

    swap_x.arrive()
    pl.semaphore_wait(reach.at[0], 2)
    signal_reach(1)
    clear_outside(table_x)
    convolve(table_x, plan, IN, OUT_CHAIN, first_weight, sums, False)

    def hide(block):
        total = sums[plan[OUT_LAST, block]]
        first_sum[block] = total
        table_h[block] = (total * sigmoid(total)).astype(jnp.bfloat16)

    for block in range(RIM):
        hide(block)
    rim_h = table_h.at[pl.ds(0, RIM)]
    swap_h = Swap(1, swap_sems, lambda g: rim_h, rim_slots(table_h), beyond(table_h))
    for block in range(RIM, BLOCKS):
        hide(block)
    share_plan.wait_send()
    share_x = share(1, table_x, other_x)
    swap_x.finish()

    load_other.wait()
    load_second.wait()
    load_grad.wait()
    swap_h.arrive()
    pl.semaphore_wait(reach.at[1], 2)
    signal_reach(2)
    clear_outside(table_h)
    share_x.wait_send()
    share_h = share(2, table_h, other_h)
    convolve(table_h, plan, IN, OUT_CHAIN, second_weight, sums, False)

    for block in range(BLOCKS):
        joined = sums[plan[OUT_LAST, block]] + table_x[block].astype(jnp.float32)
        gate = sigmoid(joined)
        result[block] = (joined * gate).astype(jnp.bfloat16)
        second_delta[block] = (
            out_grad[block].astype(jnp.float32) * (gate * (1.0 + joined * (1.0 - gate)))
        ).astype(jnp.bfloat16)

    def all_of(delta, first_block, last_block):
        return delta.at[pl.ds(first_block, last_block - first_block)]

    share_h.wait_send()
    share_second = share(
        3, all_of(second_delta, 0, BLOCKS), all_of(other_second, 0, BLOCKS)
    )

    def give(buffer):
        for g in range(8):
            for r in range(RIM):
                buffer[g, r] = sums[plan[IN_LAST, BLOCKS + RIM * g + r]].astype(jnp.bfloat16)

    def eight(buffer):
        return lambda g: buffer.at[g]

    convolve(second_delta, plan, DELTA, IN_CHAIN, second_weight, sums, True)
    give(give_h)
    back_h = Swap(2, swap_sems, eight(give_h), eight(got_h), got_h)

    def descend(block, total):
        first_delta[block] = (total * slope(first_sum[block])).astype(jnp.bfloat16)

    share_h.wait_recv()
    share_second.wait_recv()
    weight_terms(
        (table_h, other_h), (second_delta, other_second), (plan, other_plan), second.part
    )
    second.start_plane()
    swap_h.finish()
    for block in range(RIM, BLOCKS):
        descend(block, sums[plan[IN_LAST, block]])

    share_second.wait_send()
    share_inner = share(
        4, all_of(first_delta, RIM, BLOCKS), all_of(other_first, RIM, BLOCKS)
    )

    pl.semaphore_wait(reach.at[2], 2)
    back_h.arrive()
    for r in range(RIM):
        descend(r, routed(sums[plan[IN_LAST, r]], got_h, r))
    share_inner.wait_send()
    share_rim = share(5, all_of(first_delta, 0, RIM), all_of(other_first, 0, RIM))
    share_x.wait_recv()
    share_inner.wait_recv()
    share_rim.wait_recv()
    weight_terms((table_x, other_x), (first_delta, other_first), (plan, other_plan), first.part)
    first.start_plane()

    second.start_root()
    back_h.finish()

    def land(block, total):
        input_grad[block] = (total + second_delta[block].astype(jnp.float32)).astype(jnp.bfloat16)

    first.start_root()
    convolve(first_delta, plan, DELTA, IN_CHAIN, first_weight, sums, True)
    give(give_x)
    back_x = Swap(3, swap_sems, eight(give_x), eight(got_x), got_x)
    for block in range(RIM, BLOCKS):
        land(block, sums[plan[IN_LAST, block]])
    second.start_spread()
    back_x.arrive()
    for r in range(RIM):
        land(r, routed(sums[plan[IN_LAST, r]], got_x, r))
    share_rim.wait_send()
    back_x.finish()
    first.start_spread()
    second.start_core()
    second.finish()
    first.start_core()
    first.finish()


def place_kernel(*refs):
    sems = refs[-1]
    copies = []
    for index in range(4):
        copy = pltpu.make_async_copy(refs[index], refs[4 + index], sems.at[index])
        copy.start()
        copies.append(copy)
    for copy in copies:
        copy.wait()


def shards(voxels, first_weight, second_weight, in_slots, out_slots, live_slots, out_grad):
    tile = (BLOCKS,) + BLOCK_SET
    scale = 1.0 / math.sqrt(
        lax.axis_size("gx") * lax.axis_size("gy") * OFFSETS * in_slots.shape[3] * VOXELS
    )
    field = jax.ShapeDtypeStruct(tile, jnp.bfloat16)
    grad = jax.ShapeDtypeStruct((FULL, 128), jnp.bfloat16)
    vmem, hbm = (pl.BlockSpec(memory_space=space) for space in (pltpu.VMEM, pltpu.HBM))

    def slots(values):
        return values.reshape(values.shape[2:]).T

    def in_hbm(*values):
        return [pltpu.with_memory_space_constraint(value, pltpu.HBM) for value in values]

    outputs = pl.pallas_call(
        functools.partial(block_kernel, scale),
        out_shape=(field, field, grad, grad),
        in_specs=[hbm] * 7,
        out_specs=[vmem] * 4,
        scratch_shapes=SCRATCH + Reduce.scratch * 2,
        compiler_params=pltpu.CompilerParams(
            collective_id=0, has_side_effects=True, vmem_limit_bytes=48 * 1024 * 1024
        ),
        cost_estimate=pl.CostEstimate(
            flops=6 * 54 * VOXELS * 128 * 128 * 2,
            bytes_accessed=4 * FULL * 256,
            transcendentals=4 * BLOCKS * VOXELS * 128,
        ),
        name="block",
    )(
        *in_hbm(
            voxels.reshape(tile),
            first_weight,
            second_weight,
            slots(in_slots),
            slots(out_slots),
            slots(live_slots),
            out_grad.reshape(tile),
        )
    )
    whole = jax.ShapeDtypeStruct((ROWS, 128), jnp.bfloat16)
    result, input_grad, first_grad, second_grad = pl.pallas_call(
        lambda *refs: place_kernel(
            refs[0], refs[1], refs[2].at[pl.ds(0, ROWS)], refs[3].at[pl.ds(0, ROWS)], *refs[4:]
        ),
        out_shape=(field, field, whole, whole),
        in_specs=[vmem] * 4,
        out_specs=[hbm] * 4,
        scratch_shapes=[pltpu.SemaphoreType.DMA((4,))],
        compiler_params=pltpu.CompilerParams(vmem_limit_bytes=1024 * 1024),
        name="place",
    )(*outputs)
    return (
        result.reshape(voxels.shape),
        input_grad.reshape(voxels.shape),
        first_grad.reshape(first_weight.shape),
        second_grad.reshape(first_weight.shape),
    )


def solution(mesh):
    return jax.shard_map(
        shards,
        mesh=mesh,
        in_specs=(
            P("gx", "gy", None, None, None),
            P(),
            P(),
            P("gx", "gy", None, None),
            P("gx", "gy", None, None),
            P("gx", "gy", None, None),
            P("gx", "gy", None, None, None),
        ),
        out_specs=(P("gx", "gy", None, None, None), P("gx", "gy", None, None, None), P(), P()),
        check_vma=False,
    )
```

```python
import functools
import math

import jax
import jax.numpy as jnp
from jax import lax
from jax.experimental import pallas as pl
from jax.experimental.pallas import tpu as pltpu
from jax.sharding import PartitionSpec as P

RIM = 2
MESH = pl.DeviceIdType.MESH

ROWS = 27 * 128
HALF = 1792
FULL = 2 * HALF
HALF_OFFSETS = HALF // 128
PIECE = HALF // 16
CHUNKS = ((0, 64), (64, 48))


def rows(start, size):
    return pl.ds(pl.multiple_of(start, 16), size)


def place():
    gx, gy = lax.axis_index("gx"), lax.axis_index("gy")
    core = lax.rem(gx, 2)
    x = lax.rem(gx // 2, 2) * 2 + gy // 4
    return gx // 4, x, lax.rem(gy, 4), core


def device(z, x, y, core):
    return ((z * 2 + x // 2) * 2 + core, lax.rem(x, 2) * 4 + y)


def partner():
    z, x, y, core = place()
    return device(z, x, y, 1 - core)


def hops(d):
    return min(d // 4, 4 - d // 4) + min(d % 4, 4 - d % 4)


PLANE = sorted(range(1, 16), key=lambda d: -hops(d))


def ring_of(d):
    return hops(d) - 1


def in_plane(d):
    z, x, y, core = place()
    return device(z, lax.rem(x + d // 4, 4), lax.rem(y + d % 4, 4), core)


def plane_index(d):
    _, x, y, _ = place()
    return lax.rem(x + d // 4, 4) * 4 + lax.rem(y + d % 4, 4)


def opposite(d):
    return (4 - d // 4) % 4 * 4 + (4 - d % 4) % 4


def ring(d):
    z, x, y, core = place()
    return device(lax.rem(z + d + 16, 16), x, y, core)


SPREAD = [1, 2, 3, 4, 15, 5, 14, 6, 13, 7, 12, 8, 11, 10, 9]


def wait_bytes(ref, sem):
    pltpu.make_async_copy(ref, ref, sem).wait()


class Reduce:
    @staticmethod
    def scratch(size):
        return [
            pltpu.VMEM((15, size, 128), jnp.bfloat16),
            pltpu.VMEM((size, 128), jnp.bfloat16),
            pltpu.VMEM((15, size, 128), jnp.bfloat16),
            pltpu.SemaphoreType.DMA((5,)),
            pltpu.SemaphoreType.DMA((8,)),
        ]

    def __init__(self, part, out, scale, offset, size, scratch):
        self.part, self.out, self.scale, self.offset, self.size = part, out, scale, offset, size
        self.got_plane, self.plane_sum, self.got_root, self.send_sems, self.recv_sems = scratch

    def piece(self, d):
        return rows(plane_index(d) * PIECE + self.offset, self.size)

    def send(self, src, dst, send_index, recv_index, device_id):
        pltpu.make_async_remote_copy(
            src_ref=src,
            dst_ref=dst,
            send_sem=self.send_sems.at[send_index],
            recv_sem=self.recv_sems.at[recv_index],
            device_id=device_id,
            device_id_type=MESH,
        ).start()

    def sent(self, index, count):
        wait_bytes(self.part.at[pl.ds(0, count * self.size)], self.send_sems.at[index])

    def start_plane(self):
        for d in PLANE:
            self.send(
                self.part.at[self.piece(d)],
                self.got_plane.at[d - 1],
                0,
                0,
                in_plane(d),
            )

    def start_root(self):
        wait_bytes(self.got_plane, self.recv_sems.at[0])
        total = self.part[self.piece(0)].astype(jnp.float32)
        for d in range(15):
            total = total + self.got_plane[d].astype(jnp.float32)
        self.plane_sum[...] = total.astype(jnp.bfloat16)
        z, x, y, core = place()

        @pl.when(z > 0)
        def _():
            self.send(self.plane_sum, self.got_root.at[z - 1], 1, 1, device(0, x, y, core))

        self.sent(0, 15)

    def spot(self, d, core):
        return self.out.at[
            rows(core * HALF + plane_index(d) * PIECE + self.offset, self.size)
        ]

    def start_spread(self):
        z, x, y, core = place()
        own = self.spot(0, core)

        def spread(planes):
            for plane in planes:
                self.send(own, own, 2, 2, device(plane, x, y, core))

        @pl.when(z == 0)
        def _():
            wait_bytes(self.got_root, self.recv_sems.at[1])
            total = self.plane_sum[...].astype(jnp.float32)
            for plane in range(15):
                total = total + self.got_root[plane].astype(jnp.float32)
            own[...] = (total * self.scale).astype(jnp.bfloat16)
            spread(SPREAD[:4])

        @pl.when(z > 0)
        def _():
            self.sent(1, 1)
            wait_bytes(own, self.recv_sems.at[2])

        for d in PLANE:
            self.send(own, own, 3, 3 + ring_of(d), in_plane(d))
        self.send(own, own, 4, 7, partner())

        @pl.when(z == 0)
        def _():
            spread(SPREAD[4:])

    def start_core(self):
        core = place()[3]
        for index in (3, 2, 1, 0):
            group = [d for d in PLANE if ring_of(d) == index]
            wait_bytes(self.part.at[pl.ds(0, len(group) * self.size)], self.recv_sems.at[3 + index])
            for d in group:
                piece = self.spot(opposite(d), core)
                self.send(piece, piece, 4, 7, partner())

        @pl.when(place()[0] == 0)
        def _():
            self.sent(2, 15)

        self.sent(3, 15)

    def finish(self):
        wait_bytes(self.part.at[pl.ds(0, 16 * self.size)], self.recv_sems.at[7])
        self.sent(4, 16)


def greet(peers):
    barrier = pltpu.get_barrier_semaphore()
    for peer in peers:
        pl.semaphore_signal(barrier, inc=1, device_id=peer, device_id_type=MESH)
    return lambda: pl.semaphore_wait(barrier, len(peers))


BLOCKS, VOXELS, OFFSETS, SLOTS, TABLE = 8, 64, 27, 54, 24
DIRECTIONS = [(a, b) for a in (-1, 0, 1) for b in (-1, 0, 1) if (a, b) != (0, 0)]


def neighbour(direction):
    a, b = direction
    gx, gy = lax.axis_index("gx"), lax.axis_index("gy")
    return lax.rem(gx + a + 64, 64), lax.rem(gy + b + 8, 8)


def present(direction):
    a, b = direction
    gx, gy = lax.axis_index("gx") + a, lax.axis_index("gy") + b
    return (gx >= 0) & (gx < 64) & (gy >= 0) & (gy < 8)


def sigmoid(values):
    return 1.0 / (1.0 + jnp.exp(-values))


def slope(values):
    s = sigmoid(values)
    return s * (1.0 + values * (1.0 - s))


IN, DELTA, OUT_CHAIN, OUT_LAST, IN_CHAIN, IN_LAST = 0, 2, 4, 6, 8, 10


def write_plan(in_ref, out_ref, live_ref, plan):
    shape = (OFFSETS, OFFSETS)
    lane = lax.broadcasted_iota(jnp.int32, shape, 1)
    offset = lax.broadcasted_iota(jnp.int32, shape, 0)

    def across(values, s):
        return jnp.broadcast_to(values[s : s + 1], shape)

    def down(values, s):
        picked = jnp.where(lane == offset, across(values, s), -1)
        return jnp.broadcast_to(jnp.max(picked, axis=1, keepdims=True), shape)

    def chain(values, row, last_row):
        columns = [down(values, s) for s in (0, 1)]
        last = jnp.zeros(shape, jnp.int32)
        for s in (0, 1):
            target = across(values, s)
            found = jnp.zeros(shape, jnp.int32)
            for t in (0, 1):
                earlier = 2 * offset + t < 2 * lane + s
                same = (columns[t] == target) & earlier & (target >= 0)
                found = jnp.maximum(found, jnp.where(same, 2 * offset + t + 1, 0))
            last = jnp.maximum(last, jnp.where(columns[s] == lane, 2 * offset + s + 1, 0))
            plan[row + s : row + s + 1, :OFFSETS] = jnp.max(found, axis=0, keepdims=True)
        plan[last_row : last_row + 1, :OFFSETS] = jnp.max(last, axis=0, keepdims=True)

    plan[...] = jnp.zeros_like(plan)
    source, target, live = in_ref[...], out_ref[...], live_ref[...]
    plan[IN : IN + 2, :OFFSETS] = source
    plan[DELTA : DELTA + 2, :OFFSETS] = jnp.where(live > 0, target, BLOCKS)
    chain(jnp.where(live > 0, target, -1), OUT_CHAIN, OUT_LAST)
    chain(jnp.where(live > 0, source, -1), IN_CHAIN, IN_LAST)


UNROLL = 27


def step_loop(count, body, unroll=None):
    unroll = unroll or UNROLL
    unroll = max(u for u in range(1, unroll + 1) if count % u == 0)

    @pl.loop(0, count // unroll)
    def _(step):
        for u in range(unroll):
            body(step * unroll + u)


def pair_of(table, plan, row, k):
    return [table[plan[row, k]], table[plan[row + 1, k]]]


def convolve(table, plan, row, chain, weight, sums, flipped):
    def body(k):
        product = lax.dot_general(
            jnp.concatenate(pair_of(table, plan, row, k), axis=0),
            weight[k],
            (((1,), (1 if flipped else 0,)), ((), ())),
            preferred_element_type=jnp.float32,
        )
        sums[2 * k + 1] = sums[plan[chain, k]] + product[:VOXELS]
        sums[2 * k + 2] = sums[plan[chain + 1, k]] + product[VOXELS:]

    step_loop(OFFSETS, body)


def weight_terms(tables, deltas, plans, part):
    core = place()[3]

    def body(j):
        k = jnp.minimum(core * HALF_OFFSETS + j, OFFSETS - 1)
        left, right = [], []
        for table, delta, plan in zip(tables, deltas, plans):
            left += pair_of(table, plan, IN, k)
            right += pair_of(delta, plan, DELTA, k)
        product = lax.dot_general(
            jnp.concatenate(left, axis=0),
            jnp.concatenate(right, axis=0),
            (((0,), (0,)), ((), ())),
            preferred_element_type=jnp.float32,
        )
        part[rows(j * 128, 128)] = product.astype(jnp.bfloat16)

    step_loop(HALF_OFFSETS, body, 14)


class Swap:
    def __init__(self, index, sems, sources, targets, blocks):
        self.sems, self.blocks = [sems.at[side, index] for side in (0, 1)], blocks
        outer = 2 * place()[3] - 1
        for side in (1, 0, -1):
            for b in (-1, 1, 0):
                if (side, b) == (0, 0):
                    continue
                a = side * outer
                cell = 3 * (a + 1) + b + 1
                g = cell - jnp.where(cell > 4, 1, 0)
                pltpu.make_async_remote_copy(
                    src_ref=sources(g),
                    dst_ref=targets(7 - g),
                    send_sem=self.sems[0],
                    recv_sem=self.sems[1],
                    device_id=neighbour((a, b)),
                    device_id_type=MESH,
                ).start()

    def arrive(self):
        wait_bytes(self.blocks, self.sems[1])

    def finish(self):
        wait_bytes(self.blocks, self.sems[0])


def beyond(table):
    return table.at[pl.ds(BLOCKS, 8 * RIM)]


def rim_slots(table):
    return lambda g: table.at[pl.ds(BLOCKS + RIM * g, RIM)]


def clear_outside(table):
    for g, direction in enumerate(DIRECTIONS):

        @pl.when(jnp.logical_not(present(direction)))
        def _():
            table[BLOCKS + RIM * g : BLOCKS + RIM * (g + 1)] = jnp.zeros(
                (RIM, VOXELS, 128), jnp.bfloat16
            )


def routed(own, arrived, r):
    total = own
    for g, direction in enumerate(DIRECTIONS):
        total = total + jnp.where(present(direction), arrived[g, r].astype(jnp.float32), 0.0)
    return total


BLOCK_SET = (VOXELS, 128)
SCRATCH = [
    pltpu.VMEM((3, 2, OFFSETS), jnp.int32),
    pltpu.VMEM((OFFSETS, 128, 128), jnp.bfloat16),
    pltpu.VMEM((OFFSETS, 128, 128), jnp.bfloat16),
    pltpu.VMEM((BLOCKS,) + BLOCK_SET, jnp.bfloat16),
    pltpu.VMEM((16, 128), jnp.int32),
    pltpu.VMEM((16, 128), jnp.int32),
    pltpu.SMEM((16, 128), jnp.int32),
    pltpu.SMEM((16, 128), jnp.int32),
    pltpu.VMEM((TABLE,) + BLOCK_SET, jnp.bfloat16),
    pltpu.VMEM((TABLE,) + BLOCK_SET, jnp.bfloat16),
    pltpu.VMEM((TABLE,) + BLOCK_SET, jnp.bfloat16),
    pltpu.VMEM((TABLE,) + BLOCK_SET, jnp.bfloat16),
    pltpu.VMEM((2 * OFFSETS + 2,) + BLOCK_SET, jnp.float32),
    pltpu.VMEM((BLOCKS,) + BLOCK_SET, jnp.float32),
    pltpu.VMEM((BLOCKS + 1,) + BLOCK_SET, jnp.bfloat16),
    pltpu.VMEM((BLOCKS + 1,) + BLOCK_SET, jnp.bfloat16),
    pltpu.VMEM((BLOCKS + 1,) + BLOCK_SET, jnp.bfloat16),
    pltpu.VMEM((BLOCKS + 1,) + BLOCK_SET, jnp.bfloat16),
    pltpu.VMEM((8, RIM) + BLOCK_SET, jnp.bfloat16),
    pltpu.VMEM((8, RIM) + BLOCK_SET, jnp.bfloat16),
    pltpu.VMEM((8, RIM) + BLOCK_SET, jnp.bfloat16),
    pltpu.VMEM((8, RIM) + BLOCK_SET, jnp.bfloat16),
    pltpu.SemaphoreType.DMA((5,)),
    pltpu.SemaphoreType.DMA((7,)),
    pltpu.SemaphoreType.DMA((2, 4)),
    pltpu.SemaphoreType.REGULAR((3,)),
    pltpu.VMEM((HALF, 128), jnp.bfloat16),
    pltpu.VMEM((HALF, 128), jnp.bfloat16),
]


def block_kernel(
    scale,
    voxels_in,
    first_weight_in,
    second_weight_in,
    in_slots,
    out_slots,
    live_slots,
    out_grad_in,
    result,
    input_grad,
    first_grad,
    second_grad,
    *scratch,
):
    (
        slot_rows,
        first_weight,
        second_weight,
        out_grad,
        plan_rows,
        other_rows,
        plan,
        other_plan,
        table_x,
        table_h,
        other_x,
        other_h,
        sums,
        first_sum,
        first_delta,
        second_delta,
        other_first,
        other_second,
        give_h,
        got_h,
        give_x,
        got_x,
        load_sems,
        core_sems,
        swap_sems,
        reach,
        first_part,
        second_part,
    ) = scratch[: len(SCRATCH)]
    reduces = scratch[len(SCRATCH) :]
    first = [
        Reduce(first_part, first_grad, scale, *chunk, reduces[5 * n : 5 * n + 5])
        for n, chunk in enumerate(CHUNKS)
    ]
    second = Reduce(second_part, second_grad, scale, 0, PIECE, reduces[5 * len(CHUNKS) :])


    def load(index, src, dst):
        copy = pltpu.make_async_copy(src, dst, load_sems.at[index])
        copy.start()
        return copy

    def share(index, src, dst):
        copy = pltpu.make_async_remote_copy(
            src_ref=src,
            dst_ref=dst,
            send_sem=core_sems.at[6],
            recv_sem=core_sems.at[index],
            device_id=partner(),
            device_id_type=MESH,
        )
        copy.start()
        return copy

    enter = greet(
        [neighbour(direction) for direction in DIRECTIONS]
        + [in_plane(d) for d in PLANE]
        + [ring(1), ring(-1), partner()]
    )
    own = table_x.at[pl.ds(0, BLOCKS)]
    load_x = load(0, voxels_in, own)
    for index, slots in enumerate((in_slots, out_slots, live_slots)):
        load(1, slots, slot_rows.at[index])
    load_first = load(2, first_weight_in, first_weight)
    load_second = load(3, second_weight_in, second_weight)
    load_grad = load(4, out_grad_in, out_grad)

    def signal_reach(step):
        for d in (1 << step, -(1 << step)):
            pl.semaphore_signal(reach.at[step], inc=1, device_id=ring(d), device_id_type=MESH)

    enter()
    load_x.wait()
    rim_x = table_x.at[pl.ds(0, RIM)]
    swap_x = Swap(0, swap_sems, lambda g: rim_x, rim_slots(table_x), beyond(table_x))
    signal_reach(0)

    wait_bytes(slot_rows, load_sems.at[1])
    write_plan(slot_rows.at[0], slot_rows.at[1], slot_rows.at[2], plan_rows)
    load_plan = load(0, plan_rows, plan)
    share_plan = share(0, plan_rows, other_rows)
    zeros = jnp.zeros(BLOCK_SET, jnp.bfloat16)
    for delta in (first_delta, second_delta, other_first, other_second):
        delta[BLOCKS] = zeros
    sums[0] = jnp.zeros(BLOCK_SET, jnp.float32)
    load_plan.wait()
    share_plan.wait_recv()
    load_other = load(1, other_rows, other_plan)
    load_first.wait()

    swap_x.arrive()
    pl.semaphore_wait(reach.at[0], 2)
    signal_reach(1)
    clear_outside(table_x)
    convolve(table_x, plan, IN, OUT_CHAIN, first_weight, sums, False)

    def hide(block):
        total = sums[plan[OUT_LAST, block]]
        first_sum[block] = total
        table_h[block] = (total * sigmoid(total)).astype(jnp.bfloat16)

    for block in range(RIM):
        hide(block)
    rim_h = table_h.at[pl.ds(0, RIM)]
    swap_h = Swap(1, swap_sems, lambda g: rim_h, rim_slots(table_h), beyond(table_h))
    for block in range(RIM, BLOCKS):
        hide(block)
    share_plan.wait_send()
    share_x = share(1, table_x, other_x)
    swap_x.finish()

    load_other.wait()
    load_second.wait()
    load_grad.wait()
    swap_h.arrive()
    pl.semaphore_wait(reach.at[1], 2)
    signal_reach(2)
    clear_outside(table_h)
    share_x.wait_send()
    share_h = share(2, table_h, other_h)
    convolve(table_h, plan, IN, OUT_CHAIN, second_weight, sums, False)

    for block in range(BLOCKS):
        joined = sums[plan[OUT_LAST, block]] + table_x[block].astype(jnp.float32)
        gate = sigmoid(joined)
        result[block] = (joined * gate).astype(jnp.bfloat16)
        second_delta[block] = (
            out_grad[block].astype(jnp.float32) * (gate * (1.0 + joined * (1.0 - gate)))
        ).astype(jnp.bfloat16)

    def all_of(delta, first_block, last_block):
        return delta.at[pl.ds(first_block, last_block - first_block)]

    share_h.wait_send()
    share_second = share(
        3, all_of(second_delta, 0, BLOCKS), all_of(other_second, 0, BLOCKS)
    )

    def give(buffer):
        for g in range(8):
            for r in range(RIM):
                buffer[g, r] = sums[plan[IN_LAST, BLOCKS + RIM * g + r]].astype(jnp.bfloat16)

    def eight(buffer):
        return lambda g: buffer.at[g]

    convolve(second_delta, plan, DELTA, IN_CHAIN, second_weight, sums, True)
    give(give_h)
    back_h = Swap(2, swap_sems, eight(give_h), eight(got_h), got_h)

    def descend(block, total):
        first_delta[block] = (total * slope(first_sum[block])).astype(jnp.bfloat16)

    share_h.wait_recv()
    share_second.wait_recv()
    weight_terms(
        (table_h, other_h), (second_delta, other_second), (plan, other_plan), second_part
    )
    second.start_plane()
    swap_h.finish()
    for block in range(RIM, BLOCKS):
        descend(block, sums[plan[IN_LAST, block]])

    share_second.wait_send()
    share_inner = share(
        4, all_of(first_delta, RIM, BLOCKS), all_of(other_first, RIM, BLOCKS)
    )

    pl.semaphore_wait(reach.at[2], 2)
    back_h.arrive()
    for r in range(RIM):
        descend(r, routed(sums[plan[IN_LAST, r]], got_h, r))
    share_inner.wait_send()
    share_rim = share(5, all_of(first_delta, 0, RIM), all_of(other_first, 0, RIM))
    share_x.wait_recv()
    share_inner.wait_recv()
    share_rim.wait_recv()
    weight_terms((table_x, other_x), (first_delta, other_first), (plan, other_plan), first_part)
    for chunk in first:
        chunk.start_plane()

    second.start_root()
    back_h.finish()

    def land(block, total):
        input_grad[block] = (total + second_delta[block].astype(jnp.float32)).astype(jnp.bfloat16)

    for chunk in first:
        chunk.start_root()
    convolve(first_delta, plan, DELTA, IN_CHAIN, first_weight, sums, True)
    give(give_x)
    back_x = Swap(3, swap_sems, eight(give_x), eight(got_x), got_x)
    for block in range(RIM, BLOCKS):
        land(block, sums[plan[IN_LAST, block]])
    second.start_spread()
    back_x.arrive()
    for r in range(RIM):
        land(r, routed(sums[plan[IN_LAST, r]], got_x, r))
    share_rim.wait_send()
    back_x.finish()
    for chunk in first:
        chunk.start_spread()
    second.start_core()
    for chunk in first:
        chunk.start_core()
    second.finish()
    for chunk in first:
        chunk.finish()


def place_kernel(*refs):
    sems = refs[-1]
    copies = []
    for index in range(4):
        copy = pltpu.make_async_copy(refs[index], refs[4 + index], sems.at[index])
        copy.start()
        copies.append(copy)
    for copy in copies:
        copy.wait()


def shards(voxels, first_weight, second_weight, in_slots, out_slots, live_slots, out_grad):
    tile = (BLOCKS,) + BLOCK_SET
    scale = 1.0 / math.sqrt(
        lax.axis_size("gx") * lax.axis_size("gy") * OFFSETS * in_slots.shape[3] * VOXELS
    )
    field = jax.ShapeDtypeStruct(tile, jnp.bfloat16)
    grad = jax.ShapeDtypeStruct((FULL, 128), jnp.bfloat16)
    vmem, hbm = (pl.BlockSpec(memory_space=space) for space in (pltpu.VMEM, pltpu.HBM))

    def slots(values):
        return values.reshape(values.shape[2:]).T

    def in_hbm(*values):
        return [pltpu.with_memory_space_constraint(value, pltpu.HBM) for value in values]

    outputs = pl.pallas_call(
        functools.partial(block_kernel, scale),
        out_shape=(field, field, grad, grad),
        in_specs=[hbm] * 7,
        out_specs=[vmem] * 4,
        scratch_shapes=SCRATCH
        + [shape for _, size in CHUNKS for shape in Reduce.scratch(size)]
        + Reduce.scratch(PIECE),
        compiler_params=pltpu.CompilerParams(
            collective_id=0, has_side_effects=True, vmem_limit_bytes=48 * 1024 * 1024
        ),
        cost_estimate=pl.CostEstimate(
            flops=6 * 54 * VOXELS * 128 * 128 * 2,
            bytes_accessed=4 * FULL * 256,
            transcendentals=4 * BLOCKS * VOXELS * 128,
        ),
        name="block",
    )(
        *in_hbm(
            voxels.reshape(tile),
            first_weight,
            second_weight,
            slots(in_slots),
            slots(out_slots),
            slots(live_slots),
            out_grad.reshape(tile),
        )
    )
    whole = jax.ShapeDtypeStruct((ROWS, 128), jnp.bfloat16)
    result, input_grad, first_grad, second_grad = pl.pallas_call(
        lambda *refs: place_kernel(
            refs[0], refs[1], refs[2].at[pl.ds(0, ROWS)], refs[3].at[pl.ds(0, ROWS)], *refs[4:]
        ),
        out_shape=(field, field, whole, whole),
        in_specs=[vmem] * 4,
        out_specs=[hbm] * 4,
        scratch_shapes=[pltpu.SemaphoreType.DMA((4,))],
        compiler_params=pltpu.CompilerParams(vmem_limit_bytes=1024 * 1024),
        name="place",
    )(*outputs)
    return (
        result.reshape(voxels.shape),
        input_grad.reshape(voxels.shape),
        first_grad.reshape(first_weight.shape),
        second_grad.reshape(first_weight.shape),
    )


def solution(mesh):
    return jax.shard_map(
        shards,
        mesh=mesh,
        in_specs=(
            P("gx", "gy", None, None, None),
            P(),
            P(),
            P("gx", "gy", None, None),
            P("gx", "gy", None, None),
            P("gx", "gy", None, None),
            P("gx", "gy", None, None, None),
        ),
        out_specs=(P("gx", "gy", None, None, None), P("gx", "gy", None, None, None), P(), P()),
        check_vma=False,
    )
```

```python
import functools
import math

import jax
import jax.numpy as jnp
from jax import lax
from jax.experimental import pallas as pl
from jax.experimental.pallas import tpu as pltpu
from jax.sharding import PartitionSpec as P

RIM = 2
MESH = pl.DeviceIdType.MESH

ROWS = 27 * 128
HALF = 1792
FULL = 2 * HALF
HALF_OFFSETS = HALF // 128
PIECE = HALF // 16


def rows(start, size):
    return pl.ds(pl.multiple_of(start, 16), size)


def place():
    gx, gy = lax.axis_index("gx"), lax.axis_index("gy")
    core = lax.rem(gx, 2)
    x = lax.rem(gx // 2, 2) * 2 + gy // 4
    return gx // 4, x, lax.rem(gy, 4), core


def device(z, x, y, core):
    return ((z * 2 + x // 2) * 2 + core, lax.rem(x, 2) * 4 + y)


def partner():
    z, x, y, core = place()
    return device(z, x, y, 1 - core)


def hops(d):
    return min(d // 4, 4 - d // 4) + min(d % 4, 4 - d % 4)


PLANE = sorted(range(1, 16), key=lambda d: -hops(d))


def ring_of(d):
    return hops(d) - 1


def in_plane(d):
    z, x, y, core = place()
    return device(z, lax.rem(x + d // 4, 4), lax.rem(y + d % 4, 4), core)


def plane_index(d):
    _, x, y, _ = place()
    return lax.rem(x + d // 4, 4) * 4 + lax.rem(y + d % 4, 4)


def opposite(d):
    return (4 - d // 4) % 4 * 4 + (4 - d % 4) % 4


def ring(d):
    z, x, y, core = place()
    return device(lax.rem(z + d + 16, 16), x, y, core)


SPREAD = [1, 2, 3, 4, 15, 5, 14, 6, 13, 7, 12, 8, 11, 10, 9]


def wait_bytes(ref, sem):
    pltpu.make_async_copy(ref, ref, sem).wait()


class Reduce:
    scratch = [
        pltpu.VMEM((HALF, 128), jnp.bfloat16),
        pltpu.VMEM((15, PIECE, 128), jnp.bfloat16),
        pltpu.VMEM((PIECE, 128), jnp.bfloat16),
        pltpu.VMEM((15, PIECE, 128), jnp.bfloat16),
        pltpu.SemaphoreType.DMA((5,)),
        pltpu.SemaphoreType.DMA((8,)),
    ]

    def __init__(self, out, scale, *scratch):
        self.out, self.scale = out, scale
        (
            self.part,
            self.got_plane,
            self.plane_sum,
            self.got_root,
            self.send_sems,
            self.recv_sems,
        ) = scratch

    def send(self, src, dst, send_index, recv_index, device_id):
        pltpu.make_async_remote_copy(
            src_ref=src,
            dst_ref=dst,
            send_sem=self.send_sems.at[send_index],
            recv_sem=self.recv_sems.at[recv_index],
            device_id=device_id,
            device_id_type=MESH,
        ).start()

    def sent(self, index, count, size):
        wait_bytes(self.part.at[pl.ds(0, count * size)], self.send_sems.at[index])

    def start_plane(self):
        for d in PLANE:
            self.send(
                self.part.at[rows(plane_index(d) * PIECE, PIECE)],
                self.got_plane.at[d - 1],
                0,
                0,
                in_plane(d),
            )

    def start_root(self):
        wait_bytes(self.got_plane, self.recv_sems.at[0])
        total = self.part[rows(plane_index(0) * PIECE, PIECE)].astype(jnp.float32)
        for d in range(15):
            total = total + self.got_plane[d].astype(jnp.float32)
        self.plane_sum[...] = total.astype(jnp.bfloat16)
        z, x, y, core = place()

        @pl.when(z > 0)
        def _():
            self.send(self.plane_sum, self.got_root.at[z - 1], 1, 1, device(0, x, y, core))

        self.sent(0, 15, PIECE)

    def spot(self, d, core):
        return self.out.at[rows(core * HALF + plane_index(d) * PIECE, PIECE)]

    def start_spread(self):
        z, x, y, core = place()
        own = self.spot(0, core)

        def spread(planes):
            for plane in planes:
                self.send(own, own, 2, 2, device(plane, x, y, core))

        @pl.when(z == 0)
        def _():
            wait_bytes(self.got_root, self.recv_sems.at[1])
            total = self.plane_sum[...].astype(jnp.float32)
            for plane in range(15):
                total = total + self.got_root[plane].astype(jnp.float32)
            own[...] = (total * self.scale).astype(jnp.bfloat16)
            spread(SPREAD[:4])

        @pl.when(z > 0)
        def _():
            self.sent(1, 1, PIECE)
            wait_bytes(own, self.recv_sems.at[2])

        for d in PLANE:
            self.send(own, own, 3, 3 + ring_of(d), in_plane(d))
        self.send(own, own, 4, 7, partner())

        @pl.when(z == 0)
        def _():
            spread(SPREAD[4:])

    def start_core(self):
        core = place()[3]
        for index in (3, 2, 1, 0):
            group = [d for d in PLANE if ring_of(d) == index]
            wait_bytes(self.part.at[pl.ds(0, len(group) * PIECE)], self.recv_sems.at[3 + index])
            for d in group:
                piece = self.spot(opposite(d), core)
                self.send(piece, piece, 4, 7, partner())

        @pl.when(place()[0] == 0)
        def _():
            self.sent(2, 15, PIECE)

        self.sent(3, 15, PIECE)

    def finish(self):
        wait_bytes(self.part, self.recv_sems.at[7])
        self.sent(4, 16, PIECE)


def greet(peers):
    barrier = pltpu.get_barrier_semaphore()
    for peer in peers:
        pl.semaphore_signal(barrier, inc=1, device_id=peer, device_id_type=MESH)
    return lambda: pl.semaphore_wait(barrier, len(peers))


BLOCKS, VOXELS, OFFSETS, SLOTS, TABLE = 8, 64, 27, 54, 24
DIRECTIONS = [(a, b) for a in (-1, 0, 1) for b in (-1, 0, 1) if (a, b) != (0, 0)]


def neighbour(direction):
    a, b = direction
    gx, gy = lax.axis_index("gx"), lax.axis_index("gy")
    return lax.rem(gx + a + 64, 64), lax.rem(gy + b + 8, 8)


def present(direction):
    a, b = direction
    gx, gy = lax.axis_index("gx") + a, lax.axis_index("gy") + b
    return (gx >= 0) & (gx < 64) & (gy >= 0) & (gy < 8)


def sigmoid(values):
    return 1.0 / (1.0 + jnp.exp(-values))


def slope(values):
    s = sigmoid(values)
    return s * (1.0 + values * (1.0 - s))


IN, DELTA, OUT_CHAIN, OUT_LAST, IN_CHAIN, IN_LAST = 0, 2, 4, 6, 8, 10


def write_plan(in_ref, out_ref, live_ref, plan):
    shape = (OFFSETS, OFFSETS)
    lane = lax.broadcasted_iota(jnp.int32, shape, 1)
    offset = lax.broadcasted_iota(jnp.int32, shape, 0)

    def across(values, s):
        return jnp.broadcast_to(values[s : s + 1], shape)

    def down(values, s):
        picked = jnp.where(lane == offset, across(values, s), -1)
        return jnp.broadcast_to(jnp.max(picked, axis=1, keepdims=True), shape)

    def chain(values, row, last_row):
        columns = [down(values, s) for s in (0, 1)]
        last = jnp.zeros(shape, jnp.int32)
        for s in (0, 1):
            target = across(values, s)
            found = jnp.zeros(shape, jnp.int32)
            for t in (0, 1):
                earlier = 2 * offset + t < 2 * lane + s
                same = (columns[t] == target) & earlier & (target >= 0)
                found = jnp.maximum(found, jnp.where(same, 2 * offset + t + 1, 0))
            last = jnp.maximum(last, jnp.where(columns[s] == lane, 2 * offset + s + 1, 0))
            plan[row + s : row + s + 1, :OFFSETS] = jnp.max(found, axis=0, keepdims=True)
        plan[last_row : last_row + 1, :OFFSETS] = jnp.max(last, axis=0, keepdims=True)

    plan[...] = jnp.zeros_like(plan)
    source, target, live = in_ref[...], out_ref[...], live_ref[...]
    plan[IN : IN + 2, :OFFSETS] = source
    plan[DELTA : DELTA + 2, :OFFSETS] = jnp.where(live > 0, target, BLOCKS)
    chain(jnp.where(live > 0, target, -1), OUT_CHAIN, OUT_LAST)
    chain(jnp.where(live > 0, source, -1), IN_CHAIN, IN_LAST)


UNROLL = 27


def step_loop(count, body, unroll=None):
    unroll = unroll or UNROLL
    unroll = max(u for u in range(1, unroll + 1) if count % u == 0)

    @pl.loop(0, count // unroll)
    def _(step):
        for u in range(unroll):
            body(step * unroll + u)


def pair_of(table, plan, row, k):
    return [table[plan[row, k]], table[plan[row + 1, k]]]


def convolve(table, plan, row, chain, weight, sums, flipped):
    def body(k):
        product = lax.dot_general(
            jnp.concatenate(pair_of(table, plan, row, k), axis=0),
            weight[k],
            (((1,), (1 if flipped else 0,)), ((), ())),
            preferred_element_type=jnp.float32,
        )
        sums[2 * k + 1] = sums[plan[chain, k]] + product[:VOXELS]
        sums[2 * k + 2] = sums[plan[chain + 1, k]] + product[VOXELS:]

    step_loop(OFFSETS, body)


def weight_terms(tables, deltas, plans, part):
    core = place()[3]

    def body(j):
        k = jnp.minimum(core * HALF_OFFSETS + j, OFFSETS - 1)
        left, right = [], []
        for table, delta, plan in zip(tables, deltas, plans):
            left += pair_of(table, plan, IN, k)
            right += pair_of(delta, plan, DELTA, k)
        product = lax.dot_general(
            jnp.concatenate(left, axis=0),
            jnp.concatenate(right, axis=0),
            (((0,), (0,)), ((), ())),
            preferred_element_type=jnp.float32,
        )
        part[rows(j * 128, 128)] = product.astype(jnp.bfloat16)

    step_loop(HALF_OFFSETS, body, 14)


class Swap:
    def __init__(self, index, sems, sources, targets, blocks):
        self.sems, self.blocks = [sems.at[side, index] for side in (0, 1)], blocks
        outer = 2 * place()[3] - 1
        for side in (1, 0, -1):
            for b in (-1, 1, 0):
                if (side, b) == (0, 0):
                    continue
                a = side * outer
                cell = 3 * (a + 1) + b + 1
                g = cell - jnp.where(cell > 4, 1, 0)
                pltpu.make_async_remote_copy(
                    src_ref=sources(g),
                    dst_ref=targets(7 - g),
                    send_sem=self.sems[0],
                    recv_sem=self.sems[1],
                    device_id=neighbour((a, b)),
                    device_id_type=MESH,
                ).start()

    def arrive(self):
        wait_bytes(self.blocks, self.sems[1])

    def finish(self):
        wait_bytes(self.blocks, self.sems[0])


def beyond(table):
    return table.at[pl.ds(BLOCKS, 8 * RIM)]


def rim_slots(table):
    return lambda g: table.at[pl.ds(BLOCKS + RIM * g, RIM)]


def clear_outside(table):
    for g, direction in enumerate(DIRECTIONS):

        @pl.when(jnp.logical_not(present(direction)))
        def _():
            table[BLOCKS + RIM * g : BLOCKS + RIM * (g + 1)] = jnp.zeros(
                (RIM, VOXELS, 128), jnp.bfloat16
            )


def routed(own, arrived, r):
    total = own
    for g, direction in enumerate(DIRECTIONS):
        total = total + jnp.where(present(direction), arrived[g, r].astype(jnp.float32), 0.0)
    return total


BLOCK_SET = (VOXELS, 128)
SCRATCH = [
    pltpu.VMEM((3, 2, OFFSETS), jnp.int32),
    pltpu.VMEM((OFFSETS, 128, 128), jnp.bfloat16),
    pltpu.VMEM((OFFSETS, 128, 128), jnp.bfloat16),
    pltpu.VMEM((BLOCKS,) + BLOCK_SET, jnp.bfloat16),
    pltpu.VMEM((16, 128), jnp.int32),
    pltpu.VMEM((16, 128), jnp.int32),
    pltpu.SMEM((16, 128), jnp.int32),
    pltpu.SMEM((16, 128), jnp.int32),
    pltpu.VMEM((TABLE,) + BLOCK_SET, jnp.bfloat16),
    pltpu.VMEM((TABLE,) + BLOCK_SET, jnp.bfloat16),
    pltpu.VMEM((TABLE,) + BLOCK_SET, jnp.bfloat16),
    pltpu.VMEM((TABLE,) + BLOCK_SET, jnp.bfloat16),
    pltpu.VMEM((2 * OFFSETS + 2,) + BLOCK_SET, jnp.float32),
    pltpu.VMEM((BLOCKS,) + BLOCK_SET, jnp.float32),
    pltpu.VMEM((BLOCKS + 1,) + BLOCK_SET, jnp.bfloat16),
    pltpu.VMEM((BLOCKS + 1,) + BLOCK_SET, jnp.bfloat16),
    pltpu.VMEM((BLOCKS + 1,) + BLOCK_SET, jnp.bfloat16),
    pltpu.VMEM((BLOCKS + 1,) + BLOCK_SET, jnp.bfloat16),
    pltpu.VMEM((8, RIM) + BLOCK_SET, jnp.bfloat16),
    pltpu.VMEM((8, RIM) + BLOCK_SET, jnp.bfloat16),
    pltpu.VMEM((8, RIM) + BLOCK_SET, jnp.bfloat16),
    pltpu.VMEM((8, RIM) + BLOCK_SET, jnp.bfloat16),
    pltpu.SemaphoreType.DMA((5,)),
    pltpu.SemaphoreType.DMA((7,)),
    pltpu.SemaphoreType.DMA((2, 4)),
    pltpu.SemaphoreType.REGULAR((3,)),
]


def block_kernel(
    scale,
    voxels_in,
    first_weight_in,
    second_weight_in,
    in_slots,
    out_slots,
    live_slots,
    out_grad_in,
    result,
    input_grad,
    first_grad,
    second_grad,
    *scratch,
):
    (
        slot_rows,
        first_weight,
        second_weight,
        out_grad,
        plan_rows,
        other_rows,
        plan,
        other_plan,
        table_x,
        table_h,
        other_x,
        other_h,
        sums,
        first_sum,
        first_delta,
        second_delta,
        other_first,
        other_second,
        give_h,
        got_h,
        give_x,
        got_x,
        load_sems,
        core_sems,
        swap_sems,
        reach,
    ) = scratch[: len(SCRATCH)]
    count = len(Reduce.scratch)
    reduces = scratch[len(SCRATCH) :]
    first = Reduce(first_grad, scale, *reduces[:count])
    second = Reduce(second_grad, scale, *reduces[count:])

    def load(index, src, dst):
        copy = pltpu.make_async_copy(src, dst, load_sems.at[index])
        copy.start()
        return copy

    def share(index, src, dst):
        copy = pltpu.make_async_remote_copy(
            src_ref=src,
            dst_ref=dst,
            send_sem=core_sems.at[6],
            recv_sem=core_sems.at[index],
            device_id=partner(),
            device_id_type=MESH,
        )
        copy.start()
        return copy

    enter = greet(
        [neighbour(direction) for direction in DIRECTIONS]
        + [in_plane(d) for d in PLANE]
        + [ring(1), ring(-1), partner()]
    )
    own = table_x.at[pl.ds(0, BLOCKS)]
    load_x = load(0, voxels_in, own)
    for index, slots in enumerate((in_slots, out_slots, live_slots)):
        load(1, slots, slot_rows.at[index])
    load_first = load(2, first_weight_in, first_weight)
    load_second = load(3, second_weight_in, second_weight)
    load_grad = load(4, out_grad_in, out_grad)

    def signal_reach(step):
        for d in (1 << step, -(1 << step)):
            pl.semaphore_signal(reach.at[step], inc=1, device_id=ring(d), device_id_type=MESH)

    enter()
    load_x.wait()
    rim_x = table_x.at[pl.ds(0, RIM)]
    swap_x = Swap(0, swap_sems, lambda g: rim_x, rim_slots(table_x), beyond(table_x))
    signal_reach(0)

    wait_bytes(slot_rows, load_sems.at[1])
    write_plan(slot_rows.at[0], slot_rows.at[1], slot_rows.at[2], plan_rows)
    load_plan = load(0, plan_rows, plan)
    share_plan = share(0, plan_rows, other_rows)
    zeros = jnp.zeros(BLOCK_SET, jnp.bfloat16)
    for delta in (first_delta, second_delta, other_first, other_second):
        delta[BLOCKS] = zeros
    sums[0] = jnp.zeros(BLOCK_SET, jnp.float32)
    load_plan.wait()
    share_plan.wait_recv()
    load_other = load(1, other_rows, other_plan)
    load_first.wait()

    swap_x.arrive()
    pl.semaphore_wait(reach.at[0], 2)
    signal_reach(1)
    clear_outside(table_x)
    convolve(table_x, plan, IN, OUT_CHAIN, first_weight, sums, False)

    def hide(block):
        total = sums[plan[OUT_LAST, block]]
        first_sum[block] = total
        table_h[block] = (total * sigmoid(total)).astype(jnp.bfloat16)

    for block in range(RIM):
        hide(block)
    rim_h = table_h.at[pl.ds(0, RIM)]
    swap_h = Swap(1, swap_sems, lambda g: rim_h, rim_slots(table_h), beyond(table_h))
    for block in range(RIM, BLOCKS):
        hide(block)
    share_plan.wait_send()
    share_x = share(1, table_x, other_x)
    swap_x.finish()

    load_other.wait()
    load_second.wait()
    load_grad.wait()
    swap_h.arrive()
    pl.semaphore_wait(reach.at[1], 2)
    signal_reach(2)
    clear_outside(table_h)
    share_x.wait_send()
    share_h = share(2, table_h, other_h)
    convolve(table_h, plan, IN, OUT_CHAIN, second_weight, sums, False)

    for block in range(BLOCKS):
        joined = sums[plan[OUT_LAST, block]] + table_x[block].astype(jnp.float32)
        gate = sigmoid(joined)
        result[block] = (joined * gate).astype(jnp.bfloat16)
        second_delta[block] = (
            out_grad[block].astype(jnp.float32) * (gate * (1.0 + joined * (1.0 - gate)))
        ).astype(jnp.bfloat16)

    def all_of(delta, first_block, last_block):
        return delta.at[pl.ds(first_block, last_block - first_block)]

    share_h.wait_send()
    share_second = share(
        3, all_of(second_delta, 0, BLOCKS), all_of(other_second, 0, BLOCKS)
    )

    def give(buffer):
        for g in range(8):
            for r in range(RIM):
                buffer[g, r] = sums[plan[IN_LAST, BLOCKS + RIM * g + r]].astype(jnp.bfloat16)

    def eight(buffer):
        return lambda g: buffer.at[g]

    convolve(second_delta, plan, DELTA, IN_CHAIN, second_weight, sums, True)
    give(give_h)
    back_h = Swap(2, swap_sems, eight(give_h), eight(got_h), got_h)

    def descend(block, total):
        first_delta[block] = (total * slope(first_sum[block])).astype(jnp.bfloat16)

    share_h.wait_recv()
    share_second.wait_recv()
    weight_terms(
        (table_h, other_h), (second_delta, other_second), (plan, other_plan), second.part
    )
    second.start_plane()
    swap_h.finish()
    for block in range(RIM, BLOCKS):
        descend(block, sums[plan[IN_LAST, block]])

    share_second.wait_send()
    share_inner = share(
        4, all_of(first_delta, RIM, BLOCKS), all_of(other_first, RIM, BLOCKS)
    )

    pl.semaphore_wait(reach.at[2], 2)
    back_h.arrive()
    for r in range(RIM):
        descend(r, routed(sums[plan[IN_LAST, r]], got_h, r))
    share_inner.wait_send()
    share_rim = share(5, all_of(first_delta, 0, RIM), all_of(other_first, 0, RIM))
    share_x.wait_recv()
    share_inner.wait_recv()
    share_rim.wait_recv()
    weight_terms((table_x, other_x), (first_delta, other_first), (plan, other_plan), first.part)
    first.start_plane()

    second.start_root()
    back_h.finish()

    def land(block, total):
        input_grad[block] = (total + second_delta[block].astype(jnp.float32)).astype(jnp.bfloat16)

    first.start_root()
    convolve(first_delta, plan, DELTA, IN_CHAIN, first_weight, sums, True)
    give(give_x)
    back_x = Swap(3, swap_sems, eight(give_x), eight(got_x), got_x)
    for block in range(RIM, BLOCKS):
        land(block, sums[plan[IN_LAST, block]])
    second.start_spread()
    back_x.arrive()
    for r in range(RIM):
        land(r, routed(sums[plan[IN_LAST, r]], got_x, r))
    share_rim.wait_send()
    back_x.finish()
    first.start_spread()
    second.start_core()
    first.start_core()
    second.finish()
    first.finish()


def place_kernel(*refs):
    sems = refs[-1]
    copies = []
    for index in range(4):
        copy = pltpu.make_async_copy(refs[index], refs[4 + index], sems.at[index])
        copy.start()
        copies.append(copy)
    for copy in copies:
        copy.wait()


def shards(voxels, first_weight, second_weight, in_slots, out_slots, live_slots, out_grad):
    tile = (BLOCKS,) + BLOCK_SET
    scale = 1.0 / math.sqrt(
        lax.axis_size("gx") * lax.axis_size("gy") * OFFSETS * in_slots.shape[3] * VOXELS
    )
    field = jax.ShapeDtypeStruct(tile, jnp.bfloat16)
    grad = jax.ShapeDtypeStruct((FULL, 128), jnp.bfloat16)
    vmem, hbm = (pl.BlockSpec(memory_space=space) for space in (pltpu.VMEM, pltpu.HBM))

    def slots(values):
        return values.reshape(values.shape[2:]).T

    def in_hbm(*values):
        return [pltpu.with_memory_space_constraint(value, pltpu.HBM) for value in values]

    outputs = pl.pallas_call(
        functools.partial(block_kernel, scale),
        out_shape=(field, field, grad, grad),
        in_specs=[hbm] * 7,
        out_specs=[vmem] * 4,
        scratch_shapes=SCRATCH + Reduce.scratch * 2,
        compiler_params=pltpu.CompilerParams(
            collective_id=0, has_side_effects=True, vmem_limit_bytes=48 * 1024 * 1024
        ),
        cost_estimate=pl.CostEstimate(
            flops=6 * 54 * VOXELS * 128 * 128 * 2,
            bytes_accessed=4 * FULL * 256,
            transcendentals=4 * BLOCKS * VOXELS * 128,
        ),
        name="block",
    )(
        *in_hbm(
            voxels.reshape(tile),
            first_weight,
            second_weight,
            slots(in_slots),
            slots(out_slots),
            slots(live_slots),
            out_grad.reshape(tile),
        )
    )
    whole = jax.ShapeDtypeStruct((ROWS, 128), jnp.bfloat16)
    result, input_grad, first_grad, second_grad = pl.pallas_call(
        lambda *refs: place_kernel(
            refs[0], refs[1], refs[2].at[pl.ds(0, ROWS)], refs[3].at[pl.ds(0, ROWS)], *refs[4:]
        ),
        out_shape=(field, field, whole, whole),
        in_specs=[vmem] * 4,
        out_specs=[hbm] * 4,
        scratch_shapes=[pltpu.SemaphoreType.DMA((4,))],
        compiler_params=pltpu.CompilerParams(vmem_limit_bytes=1024 * 1024),
        name="place",
    )(*outputs)
    return (
        result.reshape(voxels.shape),
        input_grad.reshape(voxels.shape),
        first_grad.reshape(first_weight.shape),
        second_grad.reshape(first_weight.shape),
    )


def solution(mesh):
    return jax.shard_map(
        shards,
        mesh=mesh,
        in_specs=(
            P("gx", "gy", None, None, None),
            P(),
            P(),
            P("gx", "gy", None, None),
            P("gx", "gy", None, None),
            P("gx", "gy", None, None),
            P("gx", "gy", None, None, None),
        ),
        out_specs=(P("gx", "gy", None, None, None), P("gx", "gy", None, None, None), P(), P()),
        check_vma=False,
    )
```
